32 devices in a mesh: dp: 8 (over y, x, core), tensor: 4 (over z).
Axes of the slice: x: 2, y: 2, z: 4, core: 2. Of those that a mesh axis runs over, the one named last changes fastest.
Arguments:
- x_long: bfloat16 [2048, 64, 128], P('dp', None, 'tensor'), may hold values from -6 to 6
- dv_long: bfloat16 [2048, 1024], P('dp'), may hold values from -0.059814453 to 0.059814453
- x_short: bfloat16 [2048, 64, 128], P('tensor', 'dp'), may hold values from -6 to 6
- dv_short: bfloat16 [2048, 1024], P('tensor'), may hold values from -0.059814453 to 0.059814453
- long_len: int32 [8], P('dp'), may hold values from 64 to 256, as said below
- short_len: int32 [4], P('tensor'), may hold values from 128 to 512, as said below
- master: float32 [64, 128, 1024], P('dp', 'tensor'), may hold values from -0.3 to 0.3
- moment1: float32 [64, 128, 1024], P('dp', 'tensor'), may hold values from -2 to 2
- moment2: float32 [64, 128, 1024], P('dp', 'tensor'), may hold values from 0.1 to 2
Outputs:
- v_long: bfloat16 [2048, 1024], P(('dp', 'tensor'))
- new_master: float32 [64, 128, 1024], P('dp', 'tensor')
- new_moment1: float32 [64, 128, 1024], P('dp', 'tensor')
- new_moment2: float32 [64, 128, 1024], P('dp', 'tensor')
- next_weight: bfloat16 [64, 128, 1024], P(None, 'tensor')
The draws below stay inside these ranges and needn't reach their ends.
Inputs may be any that keep to these rules, and one draw needn't show every extreme that they name: `long_len`: some group has all 256 rows live; every group has at least 64 and at least one. `short_len`: some group has all 512 rows live; every group has at least 128 and at least one.
All inputs are finite; a program needn't handle non-finite values.
Results may differ from the reference program's by a relative error of at most 0.005.
Values may be sent and summed in bfloat16 or wider, within the bound.
No kernel may reach another device: no remote copies, remote signals or barrier semaphores. Data moves between devices by JAX's collectives and lax.ppermute only.
A program may use at most 64 MiB of HBM per device.

```python
import math
import jax
import jax.numpy as jnp

D = 8192
KV = 1024
D_OUTER = 64
D_INNER = 128
ROWS_L = 256
ROWS_S = 512
LONG_GROUPS = 8
SHORT_GROUPS = 4


def draw_lengths(key, count, most):
    lowest = max(most // 4, 1)
    lengths = jax.random.randint(key, (count,), lowest, most + 1, dtype=jnp.int32)
    place = jax.random.randint(jax.random.fold_in(key, 7), (), 0, count, dtype=jnp.int32)
    return jnp.where(jnp.arange(count, dtype=jnp.int32) == place, jnp.int32(most), lengths).astype(jnp.int32)


def draw_long_len(key, part):
    return draw_lengths(jax.random.fold_in(key, 11), LONG_GROUPS, ROWS_L)


def draw_short_len(key, part):
    return draw_lengths(jax.random.fold_in(key, 13), SHORT_GROUPS, ROWS_S)


def strengthened(result, key, source, target, parts, factor):
    owner, partner = [(jnp.arange(result.shape[axis_at]) // (result.shape[axis_at] // parts)).reshape([-1 if axis == axis_at else 1 for axis in range(result.ndim)]) for axis_at in (source, target)]
    chosen = jax.random.permutation(key, parts)[partner]
    strong = (owner == chosen) | (owner == (partner + parts // 2) % parts)
    return jnp.where(strong, factor * result, result)


def block_levels(rng, extent, shards, least, largest):
    factor_of = 1.0
    for axis_at, blocks in shards:
        draws = jax.random.uniform(jax.random.fold_in(jax.random.fold_in(rng, 6), axis_at), (blocks,), jnp.float32, least / len(shards), largest / len(shards))
        factor_of = factor_of * jnp.repeat(jnp.exp(draws), extent[axis_at] // blocks).reshape((-1,) + (1,) * (len(extent) - 1 - axis_at))
    return factor_of


def centred(rng, dims, spread, most, cuts=(), kind=jnp.bfloat16):
    entries = spread * jax.random.normal(rng, dims, jnp.float32)
    if cuts:
        entries = entries * block_levels(rng, dims, cuts, -0.22, 0.18)
    return jnp.clip(entries, -most, most).astype(kind)


def bell_draw_with(own_key, dims, scale, most, cuts, heavy, kind=jnp.bfloat16):
    values = scale * jax.random.normal(own_key, dims, jnp.float32)
    if cuts:
        values = values * block_levels(own_key, dims, cuts, -0.22, 0.18)
    return jnp.clip(strengthened(values, jax.random.fold_in(own_key, 3), *heavy), -most, most).astype(kind)


def setup_inputs(seed: int = 0) -> dict:
    key_of = jax.random.split(jax.random.key(seed), 10)
    x_long = bell_draw_with(key_of[0], (ROWS_L * LONG_GROUPS, D_OUTER, D_INNER), 1.0, 6.0, ((0, 8), (2, 4)), (0, 1, 8, 2.0))
    dv_long = centred(key_of[1], (ROWS_L * LONG_GROUPS, KV), 0.01, 0.059814453, ((0, 8),))
    x_short = bell_draw_with(key_of[2], (ROWS_S * SHORT_GROUPS, D_OUTER, D_INNER), 1.0, 6.0, ((0, 4), (1, 8)), (0, 2, 4, 2.0))
    dv_short = centred(key_of[3], (ROWS_S * SHORT_GROUPS, KV), 0.01, 0.059814453, ((0, 4),))
    long_len = draw_long_len(jax.random.fold_in(key_of[9], 71), 0)
    short_len = draw_short_len(jax.random.fold_in(key_of[9], 71), 0)
    master = centred(key_of[6], (D_OUTER, D_INNER, KV), 0.05, 0.3, ((0, 8), (1, 4)), jnp.float32)
    moment1 = centred(key_of[7], (D_OUTER, D_INNER, KV), 0.3, 2.0, ((0, 8), (1, 4)), jnp.float32)
    moment2 = jnp.clip(jnp.exp(math.log(2.0) - 2.9957323 * jax.random.uniform(key_of[8], (D_OUTER, D_INNER, KV), jnp.float32) ** block_levels(key_of[8], (D_OUTER, D_INNER, KV), ((0, 8), (1, 4)), -0.2, 0.2)), 0.1, 2.0)
    return dict(x_long=x_long, dv_long=dv_long, x_short=x_short, dv_short=dv_short, long_len=long_len, short_len=short_len, master=master, moment1=moment1, moment2=moment2)


def reference(x_long, dv_long, x_short, dv_short, long_len, short_len, master, moment1, moment2):
    weight = master.astype(jnp.bfloat16)
    flat_weight = weight.reshape(D, KV)
    flat_long = x_long.reshape(ROWS_L * LONG_GROUPS, D)
    flat_short = x_short.reshape(ROWS_S * SHORT_GROUPS, D)
    rows_long = jnp.arange(ROWS_L * LONG_GROUPS, dtype=jnp.int32)
    long_live = rows_long % ROWS_L < long_len[rows_long // ROWS_L]
    rows_short = jnp.arange(ROWS_S * SHORT_GROUPS, dtype=jnp.int32)
    short_live = rows_short % ROWS_S < short_len[rows_short // ROWS_S]
    values = jnp.dot(flat_long, flat_weight, preferred_element_type=jnp.float32)
    v_long = jnp.where(long_live[:, None], values, jnp.float32(0.0)).astype(jnp.bfloat16)
    live_dv_long = jnp.where(long_live[:, None], dv_long, jnp.zeros_like(dv_long))
    live_dv_short = jnp.where(short_live[:, None], dv_short, jnp.zeros_like(dv_short))
    grad_long = jnp.dot(flat_long.T, live_dv_long, preferred_element_type=jnp.float32)
    grad_short = jnp.dot(flat_short.T, live_dv_short, preferred_element_type=jnp.float32)
    grad = (grad_long + grad_short).reshape(D_OUTER, D_INNER, KV)
    new_moment1 = 0.9 * moment1 + 0.1 * grad
    new_moment2 = 0.999 * moment2 + 0.001 * grad * grad
    first_corr = 1.0 - 0.9 ** 10
    second_corr = 1.0 - 0.999 ** 10
    update = new_moment1 / first_corr / (jnp.sqrt(new_moment2 / second_corr) + 1e-08)
    new_master = master - 0.01 * (update + 0.1 * master)
    next_weight = new_master.astype(jnp.bfloat16)
    return (v_long, new_master, new_moment1, new_moment2, next_weight)
```

```python
import functools

import jax
import jax.numpy as jnp
from jax import lax
from jax.experimental import pallas as pl
from jax.experimental.pallas import tpu as pltpu
from jax.sharding import PartitionSpec as P

BF16 = jnp.bfloat16
F32 = jnp.float32
MIB = 1 << 20
VMEM = pl.BlockSpec(memory_space=pltpu.VMEM)
SMEM = pl.BlockSpec(memory_space=pltpu.SMEM)
ANY = pl.BlockSpec(memory_space=pl.ANY)


def contract_rows(left, right):
    return lax.dot_general(
        left, right, (((0,), (0,)), ((), ())), preferred_element_type=jnp.float32
    )


def adam(master, moment1, moment2, grad):
    new_moment1 = 0.9 * moment1 + 0.1 * grad
    new_moment2 = 0.999 * moment2 + 0.001 * grad * grad
    first_corr = 1.0 - 0.9**10
    second_corr = 1.0 - 0.999**10
    update = new_moment1 / first_corr / (jnp.sqrt(new_moment2 / second_corr) + 1e-08)
    new_master = master - 0.01 * (update + 0.1 * master)
    return new_master, new_moment1, new_moment2


def plain_body(x_long, dv_long, x_short, dv_short, long_len, short_len, master, moment1, moment2):
    weight_shard = master.astype(BF16)
    long_rows, _, inner_part = x_long.shape
    kv_width = master.shape[2]
    short_rows, outer_part, inner_whole = x_short.shape
    piece = lax.all_gather(weight_shard, "dp", axis=0, tiled=True)
    flat_inputs = x_long.reshape(long_rows, piece.shape[0] * inner_part)
    flat_piece = piece.reshape(piece.shape[0] * inner_part, kv_width)
    partial_values = jnp.dot(flat_inputs, flat_piece, preferred_element_type=F32)
    values = lax.psum_scatter(partial_values, "tensor", scatter_dimension=0, tiled=True)
    own_rows = values.shape[0]
    row_start = lax.axis_index("tensor") * own_rows
    own_live = row_start + jnp.arange(own_rows, dtype=jnp.int32) < long_len[0]
    v_long = jnp.where(own_live[:, None], values, 0.0).astype(BF16)
    long_live = jnp.arange(long_rows, dtype=jnp.int32) < long_len[0]
    short_live = jnp.arange(short_rows, dtype=jnp.int32) < short_len[0]
    live_dv_long = jnp.where(long_live[:, None], dv_long, jnp.zeros_like(dv_long))
    live_dv_short = jnp.where(short_live[:, None], dv_short, jnp.zeros_like(dv_short))
    count = lax.axis_size("dp") * master.shape[0]
    grad_long = lax.psum_scatter(
        contract_rows(flat_inputs, live_dv_long).reshape(count, inner_part, kv_width),
        "dp",
        scatter_dimension=0,
        tiled=True,
    )
    flat_inputs = x_short.reshape(short_rows, outer_part * inner_whole)
    product = contract_rows(flat_inputs, live_dv_short).reshape(outer_part, inner_whole, kv_width)
    grad_short = lax.psum_scatter(product, "tensor", scatter_dimension=1, tiled=True)
    new_master, new_moment1, new_moment2 = adam(master, moment1, moment2, grad_long + grad_short)
    next_weight = lax.all_gather(new_master.astype(BF16), "dp", axis=0, tiled=True)
    return (v_long, new_master, new_moment1, new_moment2, next_weight)


def short_kernel(len_ref, x_ref, dv_ref, *refs):
    outs, wide, live = refs[:-2], refs[-2], refs[-1]
    rows, outer, inner = x_ref.shape
    parts = len(outs)
    part = inner // parts
    z = lax.axis_index("tensor")
    wide[...] = x_ref[...].reshape(rows * outer, inner).astype(F32)
    row = lax.broadcasted_iota(jnp.int32, dv_ref.shape, 0)
    dv = dv_ref[...]
    live[...] = jnp.where(row < len_ref[0], dv, jnp.zeros_like(dv))
    shift = lax.rem(inner - z * part, inner)
    for a in range(outer):
        xa = wide[pl.ds(a, rows, outer), :]
        xa = pltpu.roll(xa, shift, 1).astype(BF16)
        prod = contract_rows(xa, live[...])
        for k in range(parts):
            outs[k][a] = prod[k * part : (k + 1) * part].astype(BF16)


def long_kernel(orders, len_ref, x_ref, dv_ref, xs_ref, dvs_ref, *refs):
    outs, live = refs[:-1], refs[-1]
    chips, outer, inner, rows = xs_ref.shape
    me = lax.axis_index("dp")
    chip, core = me // 2, lax.rem(me, 2)
    row = lax.broadcasted_iota(jnp.int32, dv_ref.shape, 0)
    dv = dv_ref[...]
    live[...] = jnp.where(row < len_ref[0], dv, jnp.zeros_like(dv))
    half = outer // 2
    for rel in range(chips):
        j = lax.bitwise_xor(chip, jnp.int32(rel))
        mine = x_ref[pl.ds((2 * j + core) * outer, outer)].reshape(outer * inner, rows)
        other = xs_ref[j].reshape(outer * inner, rows)
        prod = jnp.dot(mine, live[...], preferred_element_type=F32)
        prod = prod + jnp.dot(other, dvs_ref[...], preferred_element_type=F32)
        prod = prod.reshape(outer, inner, prod.shape[-1]).astype(BF16)
        for p, (send, keep) in enumerate(orders):
            piece = prod[p * half : (p + 1) * half]
            if rel in send:
                outs[2 * p][send.index(rel)] = piece
            else:
                outs[2 * p + 1][keep.index(rel)] = piece


def values_kernel(chips, x_ref, xs_ref, *refs):
    weights, mine_ref, other_ref, acc = refs[: 2 * chips], refs[-3], refs[-2], refs[-1]
    _, outer, inner, rows = xs_ref.shape
    parts, part, width = mine_ref.shape
    half = outer // 2
    me = lax.axis_index("dp")
    z = lax.axis_index("tensor")
    chip, core = me // 2, lax.rem(me, 2)
    for which, out in ((0, mine_ref), (1, other_ref)):
        total = None
        for rel in range(chips):
            j = lax.bitwise_xor(chip, jnp.int32(rel))
            for p in range(2):
                if which == 0:
                    x = x_ref[pl.ds((2 * j + core) * outer + p * half, half)]
                else:
                    x = xs_ref[j, pl.ds(p * half, half)]
                w = weights[2 * rel + p][...].reshape(half * inner, width)
                term = contract_rows(x.reshape(half * inner, rows), w)
                total = term if total is None else total + term
        acc[...] = total
        for k in range(parts):
            j = lax.rem(z + k, parts)
            out[k] = acc[pl.ds(pl.multiple_of(j * part, part), part), :].astype(out.dtype)


def adam_kernel(n_short, n_path, steps, *refs):
    i = pl.program_id(0)
    short, refs = refs[:n_short], refs[n_short:]
    first, refs = refs[:n_path], refs[n_path:]
    second, refs = refs[:n_path], refs[n_path:]
    master, moment1, moment2, new_master, new_moment1, new_moment2, w0, w1 = refs

    def total(terms):
        out = None
        for t in terms:
            value = t[...].reshape(master.shape).astype(F32)
            out = value if out is None else out + value
        return out

    def run(terms, w_ref):
        grad = total(terms) + total(short)
        values = adam(master[...], moment1[...], moment2[...], grad)
        new_master[...], new_moment1[...], new_moment2[...] = values
        w_ref[...] = values[0].astype(BF16)

    pl.when(i < steps)(lambda: run(first, w0))
    pl.when(i >= steps)(lambda: run(second, w1))


def place_kernel(keys, half, *refs):
    n = len(keys)
    pieces, out, sems = refs[:n], refs[n], refs[n + 1]
    me = lax.axis_index("dp")
    copies = []
    for s, (rel, p) in enumerate(keys):
        owner = lax.bitwise_xor(me, jnp.int32(rel))
        start = (2 * owner + p) * half
        copies.append(pltpu.make_async_copy(pieces[s], out.at[pl.ds(start, half)], sems.at[s]))
    for copy in copies:
        copy.start()
    for copy in copies:
        copy.wait()


def params(mib):
    return pltpu.CompilerParams(vmem_limit_bytes=mib * MIB)


def cost(flops, moved):
    return pl.CostEstimate(flops=flops, bytes_accessed=moved, transcendentals=0)


def swap(x, bit):
    n = lax.axis_size("dp")
    return lax.ppermute(x, "dp", [(i, i ^ bit) for i in range(n)])


def gather_path(piece, order):
    have = {0: piece}
    for bit in order:
        have.update({rel | bit: swap(x, 2 * bit) for rel, x in list(have.items())})
    return have


def split_orders(order):
    def spread(bits):
        return [0] if not bits else [b + r for b in (0, bits[0]) for r in spread(bits[1:])]

    keep = spread(order[1:])
    return [order[0] | r for r in keep], keep


def scatter_path(send, keep, order):
    terms = [keep]
    received = swap(send, 2 * order[0])
    terms.append(received)
    for bit in order[1:]:
        half = terms[0].shape[0] // 2
        upper = sum(t[half:].astype(F32) for t in terms).astype(BF16)
        terms = [t[:half] for t in terms] + [swap(upper, 2 * bit)]
    return terms


def line_scatter(block):
    n = lax.axis_size("tensor")
    right = left = None
    for s in range(1, n):
        go_right, go_left = block(n - s), block(s)
        if right is not None:
            go_right = go_right.astype(F32) + right.astype(F32)
            go_left = go_left.astype(F32) + left.astype(F32)
        right = lax.ppermute(go_right.astype(BF16), "tensor", [(i, i + 1) for i in range(s)])
        left = lax.ppermute(
            go_left.astype(BF16), "tensor", [(n - 1 - i, n - 2 - i) for i in range(s)]
        )
    return [block(0)] + ([] if right is None else [right, left])


def body(x_long, dv_long, x_short, dv_short, long_len, short_len, master, moment1, moment2):
    n = lax.axis_size("dp")
    parts = lax.axis_size("tensor")
    outer, inner, width = master.shape
    rows = x_long.shape[0]
    short_rows, _, inner_whole = x_short.shape
    chips = n // 2
    own_rows = rows // parts
    half = outer // 2
    aligned = (
        n & (n - 1) == 0
        and chips > 1
        and outer % 2 == 0
        and inner % 16 == 0
        and own_rows % 16 == 0
        and rows % 128 == 0
        and short_rows % 128 == 0
        and inner_whole % 128 == 0
        and width % 128 == 0
    )
    if not aligned:
        return plain_body(
            x_long, dv_long, x_short, dv_short, long_len, short_len, master, moment1, moment2
        )
    core = lax.rem(lax.axis_index("dp"), 2)
    bits = [1 << b for b in range(chips.bit_length() - 1)]
    paths = [bits, bits[::-1]]

    x_t = jnp.transpose(x_long, (1, 2, 0))
    live = jnp.arange(rows, dtype=jnp.int32) < long_len[0]
    grouped = x_t.reshape(chips, 2, outer, inner, rows)
    theirs = lax.dynamic_index_in_dim(grouped, 1 - core, 1, keepdims=False)
    theirs = jnp.where(live, theirs, jnp.zeros_like(theirs))
    x_other = swap(theirs, 1)
    dv_other = swap(dv_long, 1)

    weight = master.astype(BF16)
    gathered = [gather_path(weight[p * half : (p + 1) * half], paths[p]) for p in range(2)]

    short_parts = pl.pallas_call(
        short_kernel,
        out_shape=[jax.ShapeDtypeStruct((outer, inner, width), BF16)] * parts,
        in_specs=[SMEM, VMEM, VMEM],
        out_specs=[VMEM] * parts,
        scratch_shapes=[
            pltpu.VMEM((short_rows * outer, inner_whole), F32),
            pltpu.VMEM((short_rows, width), BF16),
        ],
        compiler_params=params(40),
        cost_estimate=cost(2 * short_rows * outer * inner_whole * width, 4 * MIB),
        name="short_grad",
    )(short_len, x_short, dv_short)
    short_terms = line_scatter(lambda k: short_parts[k])

    orders = [split_orders(order) for order in paths]
    long_parts = pl.pallas_call(
        functools.partial(long_kernel, orders),
        out_shape=[jax.ShapeDtypeStruct((chips // 2, half, inner, width), BF16)] * 4,
        in_specs=[SMEM] + [VMEM] * 4,
        out_specs=[VMEM] * 4,
        scratch_shapes=[pltpu.VMEM((rows, width), BF16)],
        compiler_params=params(40),
        cost_estimate=cost(4 * rows * chips * outer * inner * width, 4 * MIB),
        name="long_grad",
    )(long_len, x_t, dv_long, x_other, dv_other)
    long_terms = [
        scatter_path(long_parts[2 * p], long_parts[2 * p + 1], paths[p]) for p in range(2)
    ]

    weights = [gathered[p][rel] for rel in range(chips) for p in range(2)]
    mine, other = pl.pallas_call(
        functools.partial(values_kernel, chips),
        out_shape=[jax.ShapeDtypeStruct((parts, own_rows, width), F32)] * 2,
        in_specs=[VMEM] * (2 + 2 * chips),
        out_specs=[VMEM] * 2,
        scratch_shapes=[pltpu.VMEM((rows, width), F32)],
        compiler_params=params(40),
        cost_estimate=cost(4 * rows * chips * outer * inner * width, 6 * MIB),
        name="values",
    )(x_t, x_other, *weights)
    received = swap(other, 1)
    value_terms = line_scatter(lambda k: mine[k] + received[k])
    values = sum(t.astype(F32) for t in value_terms)
    row_start = lax.axis_index("tensor") * own_rows
    own_live = row_start + jnp.arange(own_rows, dtype=jnp.int32) < long_len[0]
    v_long = jnp.where(own_live[:, None], values, 0.0).astype(BF16)

    per = 2 if half % 2 == 0 else 1
    steps = half // per
    whole = pl.BlockSpec((per, inner, width), lambda i: (i, 0, 0))
    low = pl.BlockSpec((per, inner, width), lambda i: (jnp.minimum(i, steps - 1), 0, 0))
    high = pl.BlockSpec((per, inner, width), lambda i: (jnp.maximum(i - steps, 0), 0, 0))
    low4 = pl.BlockSpec((1, per, inner, width), lambda i: (0, jnp.minimum(i, steps - 1), 0, 0))
    high4 = pl.BlockSpec((1, per, inner, width), lambda i: (0, jnp.maximum(i - steps, 0), 0, 0))
    n_path = len(long_terms[0])
    state = jax.ShapeDtypeStruct(master.shape, F32)
    half_weight = jax.ShapeDtypeStruct((half, inner, width), BF16)
    new_master, new_moment1, new_moment2, next0, next1 = pl.pallas_call(
        functools.partial(adam_kernel, len(short_terms), n_path, steps),
        grid=(2 * steps,),
        out_shape=[state, state, state, half_weight, half_weight],
        in_specs=[whole] * len(short_terms) + [low4] * n_path + [high4] * n_path + [whole] * 3,
        out_specs=[whole] * 3 + [low, high],
        compiler_params=params(40),
        cost_estimate=cost(20 * outer * inner * width, 10 * MIB),
        name="adam",
    )(*short_terms, *long_terms[0], *long_terms[1], master, moment1, moment2)

    keys, pieces = [], []
    for p, shard in enumerate((next0, next1)):
        for rel, x in gather_path(shard, paths[p]).items():
            keys += [(2 * rel, p), (2 * rel + 1, p)]
            pieces += [x, swap(x, 1)]
    next_weight = pl.pallas_call(
        functools.partial(place_kernel, keys, half),
        out_shape=jax.ShapeDtypeStruct((n * outer, inner, width), BF16),
        in_specs=[ANY] * len(pieces),
        out_specs=ANY,
        scratch_shapes=[pltpu.SemaphoreType.DMA((len(pieces),))],
        cost_estimate=cost(0, 8 * MIB),
        name="place",
    )(*pieces)
    return (v_long, new_master, new_moment1, new_moment2, next_weight)


def solution(mesh):
    placed = (
        P("dp", None, "tensor"),
        P("dp", None),
        P("tensor", "dp", None),
        P("tensor", None),
        P("dp"),
        P("tensor"),
        P("dp", "tensor", None),
        P("dp", "tensor", None),
        P("dp", "tensor", None),
    )
    return jax.shard_map(
        body,
        mesh=mesh,
        in_specs=placed,
        out_specs=(
            P(("dp", "tensor"), None),
            P("dp", "tensor", None),
            P("dp", "tensor", None),
            P("dp", "tensor", None),
            P(None, "tensor", None),
        ),
        check_vma=False,
    )
```

```python
import functools

import jax
import jax.numpy as jnp
from jax import lax
from jax.experimental import pallas as pl
from jax.experimental.pallas import tpu as pltpu
from jax.sharding import PartitionSpec as P

BF16 = jnp.bfloat16
F32 = jnp.float32
MIB = 1 << 20
VMEM = pl.BlockSpec(memory_space=pltpu.VMEM)
SMEM = pl.BlockSpec(memory_space=pltpu.SMEM)
ANY = pl.BlockSpec(memory_space=pl.ANY)
HBM = pl.BlockSpec(memory_space=pltpu.HBM)


def contract_rows(left, right):
    return lax.dot_general(
        left, right, (((0,), (0,)), ((), ())), preferred_element_type=jnp.float32
    )


def adam(master, moment1, moment2, grad):
    new_moment1 = 0.9 * moment1 + 0.1 * grad
    new_moment2 = 0.999 * moment2 + 0.001 * grad * grad
    first_corr = 1.0 - 0.9**10
    second_corr = 1.0 - 0.999**10
    update = new_moment1 / first_corr / (jnp.sqrt(new_moment2 / second_corr) + 1e-08)
    new_master = master - 0.01 * (update + 0.1 * master)
    return new_master, new_moment1, new_moment2


def plain_body(x_long, dv_long, x_short, dv_short, long_len, short_len, master, moment1, moment2):
    weight_shard = master.astype(BF16)
    long_rows, _, inner_part = x_long.shape
    kv_width = master.shape[2]
    short_rows, outer_part, inner_whole = x_short.shape
    piece = lax.all_gather(weight_shard, "dp", axis=0, tiled=True)
    flat_inputs = x_long.reshape(long_rows, piece.shape[0] * inner_part)
    flat_piece = piece.reshape(piece.shape[0] * inner_part, kv_width)
    partial_values = jnp.dot(flat_inputs, flat_piece, preferred_element_type=F32)
    values = lax.psum_scatter(partial_values, "tensor", scatter_dimension=0, tiled=True)
    own_rows = values.shape[0]
    row_start = lax.axis_index("tensor") * own_rows
    own_live = row_start + jnp.arange(own_rows, dtype=jnp.int32) < long_len[0]
    v_long = jnp.where(own_live[:, None], values, 0.0).astype(BF16)
    long_live = jnp.arange(long_rows, dtype=jnp.int32) < long_len[0]
    short_live = jnp.arange(short_rows, dtype=jnp.int32) < short_len[0]
    live_dv_long = jnp.where(long_live[:, None], dv_long, jnp.zeros_like(dv_long))
    live_dv_short = jnp.where(short_live[:, None], dv_short, jnp.zeros_like(dv_short))
    count = lax.axis_size("dp") * master.shape[0]
    grad_long = lax.psum_scatter(
        contract_rows(flat_inputs, live_dv_long).reshape(count, inner_part, kv_width),
        "dp",
        scatter_dimension=0,
        tiled=True,
    )
    flat_inputs = x_short.reshape(short_rows, outer_part * inner_whole)
    product = contract_rows(flat_inputs, live_dv_short).reshape(outer_part, inner_whole, kv_width)
    grad_short = lax.psum_scatter(product, "tensor", scatter_dimension=1, tiled=True)
    new_master, new_moment1, new_moment2 = adam(master, moment1, moment2, grad_long + grad_short)
    next_weight = lax.all_gather(new_master.astype(BF16), "dp", axis=0, tiled=True)
    return (v_long, new_master, new_moment1, new_moment2, next_weight)


def first_kernel(slen_ref, llen_ref, xs_hbm, dvs_hbm, xl_hbm, master_hbm, *refs):
    blocks, theirs, weight = refs[:4], refs[4], refs[5]
    xs_ref, dvs_ref, xl_ref, master_ref, wide, sems = refs[6:]
    rows, outer, inner = xs_ref.shape
    chips, owned, _, long_rows = theirs.shape
    chunks = 4
    chunk = rows // chunks
    part = inner // 4
    z = lax.axis_index("tensor")
    odd = lax.rem(z, 2) == 1
    other = 1 - lax.rem(lax.axis_index("dp"), 2)
    pairs = []
    for c in range(chunks):
        span = pl.ds(c * chunk, chunk)
        pairs.append((xs_hbm.at[span], xs_ref.at[span]))
        pairs.append((dvs_hbm.at[span], dvs_ref.at[span]))
    for c in range(chips):
        pairs.append((xl_hbm.at[pl.ds((2 * c + other) * owned, owned)], xl_ref.at[c]))
    pairs.append((master_hbm, master_ref))
    copies = [pltpu.make_async_copy(*pair, sems.at[i]) for i, pair in enumerate(pairs)]
    for copy in copies:
        copy.start()
    for c in range(chunks):
        copies[2 * c].wait()
        copies[2 * c + 1].wait()
        x = xs_ref[c * chunk : (c + 1) * chunk]
        wide[c * chunk * outer : (c + 1) * chunk * outer] = x.reshape(chunk * outer, inner).astype(F32)
        dv = dvs_ref[c * chunk : (c + 1) * chunk]
        row = lax.broadcasted_iota(jnp.int32, dv.shape, 0) + c * chunk
        dvs_ref[c * chunk : (c + 1) * chunk] = jnp.where(row < slen_ref[0], dv, jnp.zeros_like(dv))
    shift = lax.rem(inner - z * part, inner)
    for a in range(outer):
        xa = wide[pl.ds(a, rows, outer), :]
        xa = pltpu.roll(xa, shift, 1).astype(BF16)
        prod = contract_rows(xa, dvs_ref[...])
        after, before = prod[part : 2 * part], prod[3 * part :]
        blocks[0][a] = prod[:part].astype(BF16)
        blocks[1][a] = jnp.where(odd, before, after).astype(BF16)
        blocks[2][a] = prod[2 * part : 3 * part].astype(BF16)
        blocks[3][a] = jnp.where(odd, after, before).astype(BF16)
    for c in range(chips):
        copies[2 * chunks + c].wait()
        x = xl_ref[c]
        row = lax.broadcasted_iota(jnp.int32, x.shape, 2)
        theirs[c] = jnp.where(row < llen_ref[0], x, jnp.zeros_like(x))
    copies[-1].wait()
    weight[...] = master_ref[...].astype(BF16)


def long_kernel(orders, len_ref, x_ref, dv_ref, xs_ref, dvs_ref, *refs):
    outs, live = refs[:-1], refs[-1]
    chips, outer, inner, rows = xs_ref.shape
    me = lax.axis_index("dp")
    chip, core = me // 2, lax.rem(me, 2)
    row = lax.broadcasted_iota(jnp.int32, dv_ref.shape, 0)
    dv = dv_ref[...]
    live[...] = jnp.where(row < len_ref[0], dv, jnp.zeros_like(dv))
    half = outer // 2
    for rel in range(chips):
        j = lax.bitwise_xor(chip, jnp.int32(rel))
        mine = x_ref[pl.ds((2 * j + core) * outer, outer)].reshape(outer * inner, rows)
        other = xs_ref[j].reshape(outer * inner, rows)
        prod = jnp.dot(mine, live[...], preferred_element_type=F32)
        prod = prod + jnp.dot(other, dvs_ref[...], preferred_element_type=F32)
        prod = prod.reshape(outer, inner, prod.shape[-1]).astype(BF16)
        for p, (send, keep) in enumerate(orders):
            piece = prod[p * half : (p + 1) * half]
            if rel in send:
                outs[2 * p][send.index(rel)] = piece
            else:
                outs[2 * p + 1][keep.index(rel)] = piece


def values_kernel(chips, x_ref, xs_ref, *refs):
    weights, mine_ref, other_ref, acc = refs[: chips + 1], refs[-3], refs[-2], refs[-1]
    _, outer, inner, rows = xs_ref.shape
    parts, part, width = mine_ref.shape
    half = outer // 2
    me = lax.axis_index("dp")
    z = lax.axis_index("tensor")
    chip, core = me // 2, lax.rem(me, 2)
    for which, out in ((0, mine_ref), (1, other_ref)):
        total = None
        for rel in range(chips):
            j = lax.bitwise_xor(chip, jnp.int32(rel))
            for p in range(2):
                if which == 0:
                    x = x_ref[pl.ds((2 * j + core) * outer + p * half, half)]
                else:
                    x = xs_ref[j, pl.ds(p * half, half)]
                if rel < chips - 1:
                    w = weights[rel][p * half : (p + 1) * half]
                else:
                    w = weights[rel + p][...]
                w = w.reshape(half * inner, width)
                term = contract_rows(x.reshape(half * inner, rows), w)
                total = term if total is None else total + term
        acc[...] = total
        for k in range(parts):
            j = lax.bitwise_xor(z, jnp.int32(k))
            out[k] = acc[pl.ds(pl.multiple_of(j * part, part), part), :].astype(out.dtype)


def adam_kernel(n_short, n_path, steps, *refs):
    i = pl.program_id(0)
    short, refs = refs[:n_short], refs[n_short:]
    first, refs = refs[:n_path], refs[n_path:]
    second, refs = refs[:n_path], refs[n_path:]
    master, moment1, moment2, new_master, new_moment1, new_moment2, weight = refs

    inside = interior()

    def total(terms):
        out = None
        for t in terms:
            value = t[...].reshape(master.shape).astype(F32)
            out = value if out is None else out + value
        return out

    def total_short():
        last = short[-1][...].astype(F32)
        return total(short[:-1]) + jnp.where(inside, last, 0.0)

    def run(terms):
        grad = total(terms) + total_short()
        values = adam(master[...], moment1[...], moment2[...], grad)
        new_master[...], new_moment1[...], new_moment2[...] = values
        weight[...] = values[0].astype(BF16)

    pl.when(i < steps)(lambda: run(first))
    pl.when(i >= steps)(lambda: run(second))


def place_kernel(chips, *refs):
    pieces, out, sems = refs[:-2], refs[-2], refs[-1]
    outer = pieces[0].shape[0]
    me = lax.axis_index("dp")
    copies = []
    for s, piece in enumerate(pieces):
        rel = 2 * (s % chips) + s // chips
        owner = lax.bitwise_xor(me, jnp.int32(rel))
        copies.append(
            pltpu.make_async_copy(piece, out.at[pl.ds(owner * outer, outer)], sems.at[s])
        )
    for copy in copies:
        copy.start()
    for copy in copies:
        copy.wait()


def params(mib):
    return pltpu.CompilerParams(vmem_limit_bytes=mib * MIB)


def cost(flops, moved):
    return pl.CostEstimate(flops=flops, bytes_accessed=moved, transcendentals=0)


def swap(x, bit):
    n = lax.axis_size("dp")
    return lax.ppermute(x, "dp", [(i, i ^ bit) for i in range(n)])


def near_pieces(shard, bits):
    return [swap(shard, 2 * bit) for bit in bits]


def relays(near):
    half = near[0].shape[0] // 2
    return near[0][:half], near[1][half:]


def split_orders(order):
    def spread(bits):
        return [0] if not bits else [b + r for b in (0, bits[0]) for r in spread(bits[1:])]

    keep = spread(order[1:])
    return [order[0] | r for r in keep], keep


def interior():
    z = lax.axis_index("tensor")
    return (z > 0) & (z < lax.axis_size("tensor") - 1)


def outward(x):
    return lax.ppermute(x, "tensor", [(i, i ^ 1) for i in range(lax.axis_size("tensor"))])


def inward(x):
    n = lax.axis_size("tensor")
    return lax.ppermute(x, "tensor", [(i, i ^ 3 if 0 < i < n - 1 else i) for i in range(n)])


def after(x, *earlier):
    return lax.optimization_barrier((x, *earlier))[0]


def plus(a, b):
    return (a.astype(F32) + b.astype(F32)).astype(BF16)


def body(x_long, dv_long, x_short, dv_short, long_len, short_len, master, moment1, moment2):
    n = lax.axis_size("dp")
    parts = lax.axis_size("tensor")
    outer, inner, width = master.shape
    rows = x_long.shape[0]
    short_rows, _, inner_whole = x_short.shape
    chips = n // 2
    own_rows = rows // parts
    half = outer // 2
    aligned = (
        n & (n - 1) == 0
        and chips == 4
        and parts == 4
        and short_rows % 512 == 0
        and outer % 2 == 0
        and inner % 16 == 0
        and own_rows % 16 == 0
        and rows % 128 == 0
        and short_rows % 128 == 0
        and inner_whole % 128 == 0
        and width % 128 == 0
    )
    if not aligned:
        return plain_body(
            x_long, dv_long, x_short, dv_short, long_len, short_len, master, moment1, moment2
        )
    bits = [1 << b for b in range(chips.bit_length() - 1)]
    paths = [bits, bits[::-1]]

    x_t = jnp.transpose(x_long, (1, 2, 0))
    dv_other = swap(dv_long, 1)
    block = jax.ShapeDtypeStruct((outer, inner, width), BF16)
    *blocks, theirs, weight = pl.pallas_call(
        first_kernel,
        out_shape=[block] * 4 + [jax.ShapeDtypeStruct((chips, outer, inner, rows), BF16), block],
        in_specs=[SMEM, SMEM] + [HBM] * 4,
        out_specs=[VMEM] * 6,
        scratch_shapes=[
            pltpu.VMEM(x_short.shape, BF16),
            pltpu.VMEM(dv_short.shape, BF16),
            pltpu.VMEM((chips, outer, inner, rows), BF16),
            pltpu.VMEM(master.shape, F32),
            pltpu.VMEM((short_rows * outer, inner_whole), F32),
            pltpu.SemaphoreType.DMA((9 + chips,)),
        ],
        compiler_params=params(56),
        cost_estimate=cost(2 * short_rows * outer * inner_whole * width, 8 * MIB),
        name="first",
    )(short_len, long_len, x_short, dv_short, x_t, master)
    x_other = swap(theirs, 1)
    from_end = outward(blocks[3])
    near_weight = near_pieces(weight, bits)

    orders = [split_orders(order) for order in paths]
    long_parts = pl.pallas_call(
        functools.partial(long_kernel, orders),
        out_shape=[jax.ShapeDtypeStruct((chips // 2, half, inner, width), BF16)] * 4,
        in_specs=[SMEM] + [VMEM] * 4,
        out_specs=[VMEM] * 4,
        scratch_shapes=[pltpu.VMEM((rows, width), BF16)],
        compiler_params=params(40),
        cost_estimate=cost(4 * rows * chips * outer * inner * width, 4 * MIB),
        name="long_grad",
    )(long_len, x_t, dv_long, x_other, dv_other)
    second = after(blocks[2], *long_parts)
    across_sent = plus(second, from_end)
    across = inward(across_sent)
    middle = outward(after(second, from_end))
    received, far_weight = [], []
    for p, relay in enumerate(relays(near_weight)[::-1]):
        send = after(long_parts[2 * p], across_sent)
        message = jnp.concatenate([send.reshape(outer, inner, width), relay])
        arrived = swap(message, 2 * paths[p][0])
        received.append(arrived[:outer].reshape(send.shape))
        far_weight.append(arrived[outer:])

    near_sent = plus(blocks[1], jnp.where(interior(), across, jnp.zeros_like(across)))
    near = outward(near_sent)
    inside_sent = plus(blocks[3], middle)
    inside = inward(inside_sent)
    onward = []
    for p in range(2):
        got = after(received[p], near_sent, inside_sent)
        onward.append(swap(plus(long_parts[2 * p + 1][1], got[1]), 2 * paths[p][1]))

    weights = [after(weight, *onward), *near_weight, *far_weight[::-1]]
    mine, other = pl.pallas_call(
        functools.partial(values_kernel, chips),
        out_shape=[jax.ShapeDtypeStruct((parts, own_rows, width), F32)] * 2,
        in_specs=[VMEM] * (2 + len(weights)),
        out_specs=[VMEM] * 2,
        scratch_shapes=[pltpu.VMEM((rows, width), F32)],
        compiler_params=params(40),
        cost_estimate=cost(0, 0),
        name="values",
    )(x_t, x_other, *weights)

    short_terms = [blocks[0], near, inside]
    long_terms = [
        [long_parts[2 * p + 1][:1], received[p][:1], onward[p][None]]
        for p in range(2)
    ]

    per = 2 if half % 2 == 0 else 1
    steps = half // per
    whole = pl.BlockSpec((per, inner, width), lambda i: (i, 0, 0))
    low4 = pl.BlockSpec((1, per, inner, width), lambda i: (0, jnp.minimum(i, steps - 1), 0, 0))
    high4 = pl.BlockSpec((1, per, inner, width), lambda i: (0, jnp.maximum(i - steps, 0), 0, 0))
    n_path = len(long_terms[0])
    state = jax.ShapeDtypeStruct(master.shape, F32)
    new_master, new_moment1, new_moment2, next_shard = pl.pallas_call(
        functools.partial(adam_kernel, len(short_terms), n_path, steps),
        grid=(2 * steps,),
        out_shape=[state, state, state, jax.ShapeDtypeStruct(master.shape, BF16)],
        in_specs=[whole] * len(short_terms) + [low4] * n_path + [high4] * n_path + [whole] * 3,
        out_specs=[whole] * 4,
        compiler_params=params(40),
        cost_estimate=cost(20 * outer * inner * width, 10 * MIB),
        name="adam",
    )(*short_terms, *long_terms[0], *long_terms[1], master, moment1, moment2)

    near_next = near_pieces(next_shard, bits)
    total = mine + swap(after(other, next_shard), 1)
    shares = total.astype(BF16)
    across_sent = plus(shares[2], outward(shares[3]))
    across = inward(across_sent)
    middle = outward(after(shares[2], across_sent))
    near_sent = plus(shares[1], jnp.where(interior(), across, jnp.zeros_like(across)))
    inside_sent = plus(shares[3], middle)
    near, inside = outward(near_sent), inward(inside_sent)
    values = total[0] + near.astype(F32)
    values = values + jnp.where(interior(), inside.astype(F32), 0.0)
    row_start = lax.axis_index("tensor") * own_rows
    own_live = row_start + jnp.arange(own_rows, dtype=jnp.int32) < long_len[0]
    v_long = jnp.where(own_live[:, None], values, 0.0).astype(BF16)

    low, high = relays([after(x, near_sent, inside_sent) for x in near_next])
    far_piece = jnp.concatenate([swap(low, 2 * bits[1]), swap(high, 2 * bits[0])])
    far_piece = after(far_piece, near, inside)
    pieces = [next_shard, *near_next, far_piece]
    pieces = pieces + [swap(x, 1) for x in pieces]
    next_weight = pl.pallas_call(
        functools.partial(place_kernel, chips),
        out_shape=jax.ShapeDtypeStruct((n * outer, inner, width), BF16),
        in_specs=[VMEM] * len(pieces),
        out_specs=ANY,
        scratch_shapes=[pltpu.SemaphoreType.DMA((len(pieces),))],
        compiler_params=params(40),
        cost_estimate=cost(0, 8 * MIB),
        name="place",
    )(*pieces)
    return (v_long, new_master, new_moment1, new_moment2, next_weight)


def solution(mesh):
    placed = (
        P("dp", None, "tensor"),
        P("dp", None),
        P("tensor", "dp", None),
        P("tensor", None),
        P("dp"),
        P("tensor"),
        P("dp", "tensor", None),
        P("dp", "tensor", None),
        P("dp", "tensor", None),
    )
    return jax.shard_map(
        body,
        mesh=mesh,
        in_specs=placed,
        out_specs=(
            P(("dp", "tensor"), None),
            P("dp", "tensor", None),
            P("dp", "tensor", None),
            P("dp", "tensor", None),
            P(None, "tensor", None),
        ),
        check_vma=False,
    )
```

```python
import functools

import jax
import jax.numpy as jnp
from jax import lax
from jax.experimental import pallas as pl
from jax.experimental.pallas import tpu as pltpu
from jax.sharding import PartitionSpec as P

BF16 = jnp.bfloat16
F32 = jnp.float32
MIB = 1 << 20
VMEM = pl.BlockSpec(memory_space=pltpu.VMEM)
SMEM = pl.BlockSpec(memory_space=pltpu.SMEM)
ANY = pl.BlockSpec(memory_space=pl.ANY)
HBM = pl.BlockSpec(memory_space=pltpu.HBM)


def contract_rows(left, right):
    return lax.dot_general(
        left, right, (((0,), (0,)), ((), ())), preferred_element_type=jnp.float32
    )


def adam(master, moment1, moment2, grad):
    new_moment1 = 0.9 * moment1 + 0.1 * grad
    new_moment2 = 0.999 * moment2 + 0.001 * grad * grad
    first_corr = 1.0 - 0.9**10
    second_corr = 1.0 - 0.999**10
    update = new_moment1 / first_corr / (jnp.sqrt(new_moment2 / second_corr) + 1e-08)
    new_master = master - 0.01 * (update + 0.1 * master)
    return new_master, new_moment1, new_moment2


def plain_body(x_long, dv_long, x_short, dv_short, long_len, short_len, master, moment1, moment2):
    weight_shard = master.astype(BF16)
    long_rows, _, inner_part = x_long.shape
    kv_width = master.shape[2]
    short_rows, outer_part, inner_whole = x_short.shape
    piece = lax.all_gather(weight_shard, "dp", axis=0, tiled=True)
    flat_inputs = x_long.reshape(long_rows, piece.shape[0] * inner_part)
    flat_piece = piece.reshape(piece.shape[0] * inner_part, kv_width)
    partial_values = jnp.dot(flat_inputs, flat_piece, preferred_element_type=F32)
    values = lax.psum_scatter(partial_values, "tensor", scatter_dimension=0, tiled=True)
    own_rows = values.shape[0]
    row_start = lax.axis_index("tensor") * own_rows
    own_live = row_start + jnp.arange(own_rows, dtype=jnp.int32) < long_len[0]
    v_long = jnp.where(own_live[:, None], values, 0.0).astype(BF16)
    long_live = jnp.arange(long_rows, dtype=jnp.int32) < long_len[0]
    short_live = jnp.arange(short_rows, dtype=jnp.int32) < short_len[0]
    live_dv_long = jnp.where(long_live[:, None], dv_long, jnp.zeros_like(dv_long))
    live_dv_short = jnp.where(short_live[:, None], dv_short, jnp.zeros_like(dv_short))
    count = lax.axis_size("dp") * master.shape[0]
    grad_long = lax.psum_scatter(
        contract_rows(flat_inputs, live_dv_long).reshape(count, inner_part, kv_width),
        "dp",
        scatter_dimension=0,
        tiled=True,
    )
    flat_inputs = x_short.reshape(short_rows, outer_part * inner_whole)
    product = contract_rows(flat_inputs, live_dv_short).reshape(outer_part, inner_whole, kv_width)
    grad_short = lax.psum_scatter(product, "tensor", scatter_dimension=1, tiled=True)
    new_master, new_moment1, new_moment2 = adam(master, moment1, moment2, grad_long + grad_short)
    next_weight = lax.all_gather(new_master.astype(BF16), "dp", axis=0, tiled=True)
    return (v_long, new_master, new_moment1, new_moment2, next_weight)


def first_kernel(slen_ref, llen_ref, xs_hbm, dvs_hbm, xl_hbm, master_hbm, *refs):
    blocks, theirs, weight = refs[:4], refs[4], refs[5]
    xs_ref, dvs_ref, xl_ref, master_ref, wide, turned, sems = refs[6:]
    rows, outer, inner = xs_ref.shape
    chips, owned, _, long_rows = theirs.shape
    chunks = 4
    chunk = rows // chunks
    part = inner // 4
    z = lax.axis_index("tensor")
    other = 1 - lax.rem(lax.axis_index("dp"), 2)
    pairs = []
    for c in range(chunks):
        span = pl.ds(c * chunk, chunk)
        pairs.append((xs_hbm.at[span], xs_ref.at[span]))
        pairs.append((dvs_hbm.at[span], dvs_ref.at[span]))
    for c in range(chips):
        pairs.append((xl_hbm.at[pl.ds((2 * c + other) * owned, owned)], xl_ref.at[c]))
    pairs.append((master_hbm, master_ref))
    copies = [pltpu.make_async_copy(*pair, sems.at[i]) for i, pair in enumerate(pairs)]
    for copy in copies:
        copy.start()
    for c in range(chunks):
        copies[2 * c].wait()
        copies[2 * c + 1].wait()
        span = slice(c * chunk, (c + 1) * chunk)
        wide[...] = xs_ref[span].reshape(chunk * outer, inner).astype(F32)
        for a in range(outer):
            xa = wide[pl.ds(a, chunk, outer), :].astype(BF16).T
            for j in range(4):
                turned[j, a * part : (a + 1) * part, span] = xa[j * part : (j + 1) * part]
        dv = dvs_ref[span]
        row = lax.broadcasted_iota(jnp.int32, dv.shape, 0) + c * chunk
        dvs_ref[span] = jnp.where(row < slen_ref[0], dv, jnp.zeros_like(dv))
    for k in (3, 2, 1, 0):
        x = turned[lax.bitwise_xor(z, jnp.int32(k))]
        prod = jnp.dot(x, dvs_ref[...], preferred_element_type=F32)
        blocks[k][...] = prod.reshape(outer, part, prod.shape[1]).astype(BF16)
    for c in range(chips):
        copies[2 * chunks + c].wait()
        x = xl_ref[c]
        row = lax.broadcasted_iota(jnp.int32, x.shape, 2)
        theirs[c] = jnp.where(row < llen_ref[0], x, jnp.zeros_like(x))
    copies[-1].wait()
    weight[...] = master_ref[...].astype(BF16)


def long_kernel(orders, len_ref, x_ref, dv_ref, xs_ref, dvs_ref, *refs):
    outs, live = refs[:-1], refs[-1]
    chips, outer, inner, rows = xs_ref.shape
    me = lax.axis_index("dp")
    chip, core = me // 2, lax.rem(me, 2)
    row = lax.broadcasted_iota(jnp.int32, dv_ref.shape, 0)
    dv = dv_ref[...]
    live[...] = jnp.where(row < len_ref[0], dv, jnp.zeros_like(dv))
    half = outer // 2
    for rel in range(chips):
        j = lax.bitwise_xor(chip, jnp.int32(rel))
        mine = x_ref[pl.ds((2 * j + core) * outer, outer)].reshape(outer * inner, rows)
        other = xs_ref[j].reshape(outer * inner, rows)
        prod = jnp.dot(mine, live[...], preferred_element_type=F32)
        prod = prod + jnp.dot(other, dvs_ref[...], preferred_element_type=F32)
        prod = prod.reshape(outer, inner, prod.shape[-1]).astype(BF16)
        for p, (send, keep) in enumerate(orders):
            piece = prod[p * half : (p + 1) * half]
            if rel in send:
                outs[2 * p][send.index(rel)] = piece
            else:
                outs[2 * p + 1][keep.index(rel)] = piece


def values_kernel(chips, x_ref, xs_ref, *refs):
    weights, mine_ref, other_ref, acc = refs[: chips + 1], refs[-3], refs[-2], refs[-1]
    _, outer, inner, rows = xs_ref.shape
    parts, part, width = mine_ref.shape
    half = outer // 2
    me = lax.axis_index("dp")
    z = lax.axis_index("tensor")
    chip, core = me // 2, lax.rem(me, 2)
    for which, out in ((0, mine_ref), (1, other_ref)):
        total = None
        for rel in range(chips):
            j = lax.bitwise_xor(chip, jnp.int32(rel))
            for p in range(2):
                if which == 0:
                    x = x_ref[pl.ds((2 * j + core) * outer + p * half, half)]
                else:
                    x = xs_ref[j, pl.ds(p * half, half)]
                if rel < chips - 1:
                    w = weights[rel][p * half : (p + 1) * half]
                else:
                    w = weights[rel + p][...]
                w = w.reshape(half * inner, width)
                term = contract_rows(x.reshape(half * inner, rows), w)
                total = term if total is None else total + term
        acc[...] = total
        for k in range(parts):
            j = lax.bitwise_xor(z, jnp.int32(k))
            out[k] = acc[pl.ds(pl.multiple_of(j * part, part), part), :].astype(out.dtype)


def adam_kernel(n_short, n_path, steps, *refs):
    i = pl.program_id(0)
    short, refs = refs[:n_short], refs[n_short:]
    first, refs = refs[:n_path], refs[n_path:]
    second, refs = refs[:n_path], refs[n_path:]
    master, moment1, moment2, new_master, new_moment1, new_moment2, weight = refs

    inside = interior()

    def total(terms):
        out = None
        for t in terms:
            value = t[...].reshape(master.shape).astype(F32)
            out = value if out is None else out + value
        return out

    def total_short():
        last = short[-1][...].astype(F32)
        return total(short[:-1]) + jnp.where(inside, last, 0.0)

    def run(terms):
        grad = total(terms) + total_short()
        values = adam(master[...], moment1[...], moment2[...], grad)
        new_master[...], new_moment1[...], new_moment2[...] = values
        weight[...] = values[0].astype(BF16)

    pl.when(i < steps)(lambda: run(first))
    pl.when(i >= steps)(lambda: run(second))


def place_kernel(rels, *refs):
    pieces, out, sems = refs[: len(rels)], refs[-2], refs[-1]
    outer = pieces[0].shape[0]
    me = lax.axis_index("dp")
    copies = []
    for s, (rel, piece) in enumerate(zip(rels, pieces)):
        owner = lax.bitwise_xor(me, jnp.int32(rel))
        copies.append(
            pltpu.make_async_copy(piece, out.at[pl.ds(owner * outer, outer)], sems.at[s])
        )
    for copy in copies:
        copy.start()
    for copy in copies:
        copy.wait()


def place(rels, pieces, whole, name):
    new = isinstance(whole, jax.ShapeDtypeStruct)
    return pl.pallas_call(
        functools.partial(place_kernel, rels),
        out_shape=jax.ShapeDtypeStruct(whole.shape, whole.dtype),
        in_specs=[VMEM] * len(pieces) + [ANY] * (not new),
        out_specs=ANY,
        scratch_shapes=[pltpu.SemaphoreType.DMA((len(pieces),))],
        input_output_aliases={} if new else {len(pieces): 0},
        compiler_params=params(16),
        cost_estimate=cost(0, 2 * pieces[0].size * len(pieces)),
        name=name,
    )(*pieces, *([] if new else [whole]))


def params(mib):
    return pltpu.CompilerParams(vmem_limit_bytes=mib * MIB)


def cost(flops, moved):
    return pl.CostEstimate(flops=flops, bytes_accessed=moved, transcendentals=0)


def swap(x, bit):
    n = lax.axis_size("dp")
    return lax.ppermute(x, "dp", [(i, i ^ bit) for i in range(n)])


def near_pieces(shard, bits):
    return [swap(shard, 2 * bit) for bit in bits]


def relays(near):
    half = near[0].shape[0] // 2
    return near[0][:half], near[1][half:]


def split_orders(order):
    def spread(bits):
        return [0] if not bits else [b + r for b in (0, bits[0]) for r in spread(bits[1:])]

    keep = spread(order[1:])
    return [order[0] | r for r in keep], keep


def interior():
    z = lax.axis_index("tensor")
    return (z > 0) & (z < lax.axis_size("tensor") - 1)


def outward(x):
    return lax.ppermute(x, "tensor", [(i, i ^ 1) for i in range(lax.axis_size("tensor"))])


def inward(x):
    n, m = lax.axis_size("tensor"), lax.axis_size("dp")
    pairs = []
    for d in range(m):
        for i in range(n):
            to = (d, i ^ 3) if 0 < i < n - 1 else (d ^ 1, i)
            pairs.append((d * n + i, to[0] * n + to[1]))
    return lax.ppermute(x, ("dp", "tensor"), pairs)


def after(x, *earlier):
    return lax.optimization_barrier((x, *earlier))[0]


def plus(a, b):
    return (a.astype(F32) + b.astype(F32)).astype(BF16)


def body(x_long, dv_long, x_short, dv_short, long_len, short_len, master, moment1, moment2):
    n = lax.axis_size("dp")
    parts = lax.axis_size("tensor")
    outer, inner, width = master.shape
    rows = x_long.shape[0]
    short_rows, _, inner_whole = x_short.shape
    chips = n // 2
    own_rows = rows // parts
    half = outer // 2
    aligned = (
        n & (n - 1) == 0
        and chips == 4
        and parts == 4
        and short_rows % 512 == 0
        and outer % 2 == 0
        and inner % 16 == 0
        and own_rows % 16 == 0
        and rows % 128 == 0
        and short_rows % 128 == 0
        and inner_whole % 128 == 0
        and width % 128 == 0
    )
    if not aligned:
        return plain_body(
            x_long, dv_long, x_short, dv_short, long_len, short_len, master, moment1, moment2
        )
    bits = [1 << b for b in range(chips.bit_length() - 1)]
    paths = [bits, bits[::-1]]

    x_t = jnp.transpose(x_long, (1, 2, 0))
    dv_other = swap(dv_long, 1)
    block = jax.ShapeDtypeStruct((outer, inner, width), BF16)
    *blocks, theirs, weight = pl.pallas_call(
        first_kernel,
        out_shape=[block] * 4 + [jax.ShapeDtypeStruct((chips, outer, inner, rows), BF16), block],
        in_specs=[SMEM, SMEM] + [HBM] * 4,
        out_specs=[VMEM] * 6,
        scratch_shapes=[
            pltpu.VMEM(x_short.shape, BF16),
            pltpu.VMEM(dv_short.shape, BF16),
            pltpu.VMEM((chips, outer, inner, rows), BF16),
            pltpu.VMEM(master.shape, F32),
            pltpu.VMEM((short_rows // 4 * outer, inner_whole), F32),
            pltpu.VMEM((4, outer * inner, short_rows), BF16),
            pltpu.SemaphoreType.DMA((9 + chips,)),
        ],
        compiler_params=params(50),
        cost_estimate=cost(2 * short_rows * outer * inner_whole * width, 8 * MIB),
        name="first",
    )(short_len, long_len, x_short, dv_short, x_t, master)
    x_other = swap(theirs, 1)
    from_end = outward(blocks[3])
    near_weight = near_pieces(weight, bits)

    orders = [split_orders(order) for order in paths]
    long_parts = pl.pallas_call(
        functools.partial(long_kernel, orders),
        out_shape=[jax.ShapeDtypeStruct((chips // 2, half, inner, width), BF16)] * 4,
        in_specs=[SMEM] + [VMEM] * 4,
        out_specs=[VMEM] * 4,
        scratch_shapes=[pltpu.VMEM((rows, width), BF16)],
        compiler_params=params(16),
        cost_estimate=cost(4 * rows * chips * outer * inner * width, 4 * MIB),
        name="long_grad",
    )(long_len, x_t, dv_long, x_other, dv_other)
    second = after(blocks[2], *long_parts)
    across_sent = plus(second, from_end)
    across = inward(across_sent)
    middle = outward(after(second, from_end))
    received, far_weight = [], []
    for p, relay in enumerate(relays(near_weight)[::-1]):
        send = after(long_parts[2 * p], across_sent)
        message = jnp.concatenate([send.reshape(outer, inner, width), relay])
        arrived = swap(message, 2 * paths[p][0])
        received.append(arrived[:outer].reshape(send.shape))
        far_weight.append(arrived[outer:])

    near_sent = plus(blocks[1], jnp.where(interior(), across, jnp.zeros_like(across)))
    near = outward(near_sent)
    inside_sent = plus(blocks[3], middle)
    inside = inward(inside_sent)
    onward = []
    for p in range(2):
        got = after(received[p], near_sent, inside_sent)
        onward.append(swap(plus(long_parts[2 * p + 1][1], got[1]), 2 * paths[p][1]))

    weights = [after(weight, *onward), *near_weight, *far_weight[::-1]]
    mine, other = pl.pallas_call(
        functools.partial(values_kernel, chips),
        out_shape=[jax.ShapeDtypeStruct((parts, own_rows, width), F32)] * 2,
        in_specs=[VMEM] * (2 + len(weights)),
        out_specs=[VMEM] * 2,
        scratch_shapes=[pltpu.VMEM((rows, width), F32)],
        compiler_params=params(16),
        cost_estimate=cost(0, 0),
        name="values",
    )(x_t, x_other, *weights)

    short_terms = [blocks[0], near, inside]
    long_terms = [
        [long_parts[2 * p + 1][:1], received[p][:1], onward[p][None]]
        for p in range(2)
    ]

    per = 2 if half % 2 == 0 else 1
    steps = half // per
    whole = pl.BlockSpec((per, inner, width), lambda i: (i, 0, 0))
    low4 = pl.BlockSpec((1, per, inner, width), lambda i: (0, jnp.minimum(i, steps - 1), 0, 0))
    high4 = pl.BlockSpec((1, per, inner, width), lambda i: (0, jnp.maximum(i - steps, 0), 0, 0))
    n_path = len(long_terms[0])
    state = jax.ShapeDtypeStruct(master.shape, F32)
    new_master, new_moment1, new_moment2, next_shard = pl.pallas_call(
        functools.partial(adam_kernel, len(short_terms), n_path, steps),
        grid=(2 * steps,),
        out_shape=[state, state, state, jax.ShapeDtypeStruct(master.shape, BF16)],
        in_specs=[whole] * len(short_terms) + [low4] * n_path + [high4] * n_path + [whole] * 3,
        out_specs=[whole] * 4,
        compiler_params=params(16),
        cost_estimate=cost(20 * outer * inner * width, 10 * MIB),
        name="adam",
    )(*short_terms, *long_terms[0], *long_terms[1], master, moment1, moment2)

    near_next = near_pieces(next_shard, bits)
    total = mine + swap(after(other, next_shard), 1)
    shares = total.astype(BF16)
    across_sent = plus(shares[2], outward(shares[3]))
    across = inward(across_sent)
    middle = outward(after(shares[2], across_sent))
    near_sent = plus(shares[1], jnp.where(interior(), across, jnp.zeros_like(across)))
    inside_sent = plus(shares[3], middle)
    near, inside = outward(near_sent), inward(inside_sent)
    values = total[0] + near.astype(F32)
    values = values + jnp.where(interior(), inside.astype(F32), 0.0)
    row_start = lax.axis_index("tensor") * own_rows
    own_live = row_start + jnp.arange(own_rows, dtype=jnp.int32) < long_len[0]
    v_long = jnp.where(own_live[:, None], values, 0.0).astype(BF16)

    low, high = relays([after(x, near_sent, inside_sent) for x in near_next])
    early = [next_shard, *near_next]
    early = early + [swap(x, 1) for x in early]
    whole_shape = jax.ShapeDtypeStruct((n * outer, inner, width), BF16)
    placed = place([0, 2, 4, 1, 3, 5], early, whole_shape, "place_near")
    far_piece = jnp.concatenate([swap(low, 2 * bits[1]), swap(high, 2 * bits[0])])
    far_piece = after(far_piece, near, inside, placed)
    far = [far_piece, swap(far_piece, 1)]
    next_weight = place([6, 7], far, placed, "place_far")
    return (v_long, new_master, new_moment1, new_moment2, next_weight)


def solution(mesh):
    placed = (
        P("dp", None, "tensor"),
        P("dp", None),
        P("tensor", "dp", None),
        P("tensor", None),
        P("dp"),
        P("tensor"),
        P("dp", "tensor", None),
        P("dp", "tensor", None),
        P("dp", "tensor", None),
    )
    return jax.shard_map(
        body,
        mesh=mesh,
        in_specs=placed,
        out_specs=(
            P(("dp", "tensor"), None),
            P("dp", "tensor", None),
            P("dp", "tensor", None),
            P("dp", "tensor", None),
            P(None, "tensor", None),
        ),
        check_vma=False,
    )
```

```python
import functools

import jax
import jax.numpy as jnp
from jax import lax
from jax.experimental import pallas as pl
from jax.experimental.pallas import tpu as pltpu
from jax.sharding import PartitionSpec as P

BF16 = jnp.bfloat16
F32 = jnp.float32
MIB = 1 << 20
VMEM = pl.BlockSpec(memory_space=pltpu.VMEM)
SMEM = pl.BlockSpec(memory_space=pltpu.SMEM)
ANY = pl.BlockSpec(memory_space=pl.ANY)
HBM = pl.BlockSpec(memory_space=pltpu.HBM)


def contract_rows(left, right):
    return lax.dot_general(
        left, right, (((0,), (0,)), ((), ())), preferred_element_type=jnp.float32
    )


def adam(master, moment1, moment2, grad):
    new_moment1 = 0.9 * moment1 + 0.1 * grad
    new_moment2 = 0.999 * moment2 + 0.001 * grad * grad
    first_corr = 1.0 - 0.9**10
    second_corr = 1.0 - 0.999**10
    update = new_moment1 / first_corr / (jnp.sqrt(new_moment2 / second_corr) + 1e-08)
    new_master = master - 0.01 * (update + 0.1 * master)
    return new_master, new_moment1, new_moment2


def plain_body(x_long, dv_long, x_short, dv_short, long_len, short_len, master, moment1, moment2):
    weight_shard = master.astype(BF16)
    long_rows, _, inner_part = x_long.shape
    kv_width = master.shape[2]
    short_rows, outer_part, inner_whole = x_short.shape
    piece = lax.all_gather(weight_shard, "dp", axis=0, tiled=True)
    flat_inputs = x_long.reshape(long_rows, piece.shape[0] * inner_part)
    flat_piece = piece.reshape(piece.shape[0] * inner_part, kv_width)
    partial_values = jnp.dot(flat_inputs, flat_piece, preferred_element_type=F32)
    values = lax.psum_scatter(partial_values, "tensor", scatter_dimension=0, tiled=True)
    own_rows = values.shape[0]
    row_start = lax.axis_index("tensor") * own_rows
    own_live = row_start + jnp.arange(own_rows, dtype=jnp.int32) < long_len[0]
    v_long = jnp.where(own_live[:, None], values, 0.0).astype(BF16)
    long_live = jnp.arange(long_rows, dtype=jnp.int32) < long_len[0]
    short_live = jnp.arange(short_rows, dtype=jnp.int32) < short_len[0]
    live_dv_long = jnp.where(long_live[:, None], dv_long, jnp.zeros_like(dv_long))
    live_dv_short = jnp.where(short_live[:, None], dv_short, jnp.zeros_like(dv_short))
    count = lax.axis_size("dp") * master.shape[0]
    grad_long = lax.psum_scatter(
        contract_rows(flat_inputs, live_dv_long).reshape(count, inner_part, kv_width),
        "dp",
        scatter_dimension=0,
        tiled=True,
    )
    flat_inputs = x_short.reshape(short_rows, outer_part * inner_whole)
    product = contract_rows(flat_inputs, live_dv_short).reshape(outer_part, inner_whole, kv_width)
    grad_short = lax.psum_scatter(product, "tensor", scatter_dimension=1, tiled=True)
    new_master, new_moment1, new_moment2 = adam(master, moment1, moment2, grad_long + grad_short)
    next_weight = lax.all_gather(new_master.astype(BF16), "dp", axis=0, tiled=True)
    return (v_long, new_master, new_moment1, new_moment2, next_weight)


def first_kernel(slen_hbm, llen_hbm, xs_hbm, dvs_hbm, xl_hbm, dvl_hbm, master_hbm, *refs):
    blocks, theirs, live_dv, weight, inside, live_rows = refs[:4], *refs[4:9]
    slen_ref, llen_ref, xs_ref, dvs_ref, xl_ref, dvl_ref, master_ref, wide, turned, sems = refs[9:]
    rows, outer, inner = xs_ref.shape
    chips, owned, _, long_rows = theirs.shape
    chunks = 4
    chunk = rows // chunks
    part = inner // 4
    z = lax.axis_index("tensor")
    other = 1 - lax.rem(lax.axis_index("dp"), 2)
    pairs = []
    for c in range(chunks):
        span = pl.ds(c * chunk, chunk)
        pairs.append((xs_hbm.at[span], xs_ref.at[span]))
        pairs.append((dvs_hbm.at[span], dvs_ref.at[span]))
    for c in range(chips):
        pairs.append((xl_hbm.at[pl.ds((2 * c + other) * owned, owned)], xl_ref.at[c]))
    pairs.append((dvl_hbm, dvl_ref))
    pairs.append((master_hbm, master_ref))
    pairs.append((llen_hbm, llen_ref))
    pairs.append((slen_hbm, slen_ref))
    copies = [pltpu.make_async_copy(*pair, sems.at[i]) for i, pair in enumerate(pairs)]
    for copy in copies[::-1]:
        copy.start()
    copies[-1].wait()
    for c in range(chunks):
        copies[2 * c].wait()
        copies[2 * c + 1].wait()
        span = slice(c * chunk, (c + 1) * chunk)
        wide[...] = xs_ref[span].reshape(chunk * outer, inner).astype(F32)
        for a in range(outer):
            xa = wide[pl.ds(a, chunk, outer), :].astype(BF16).T
            for j in range(4):
                turned[j, a * part : (a + 1) * part, span] = xa[j * part : (j + 1) * part]
        dv = dvs_ref[span]
        row = lax.broadcasted_iota(jnp.int32, dv.shape, 0) + c * chunk
        dvs_ref[span] = jnp.where(row < slen_ref[0], dv, jnp.zeros_like(dv))
    for k in (3, 2, 1, 0):
        x = turned[lax.bitwise_xor(z, jnp.int32(k))]
        prod = jnp.dot(x, dvs_ref[...], preferred_element_type=F32)
        blocks[k][...] = prod.reshape(outer, part, prod.shape[1]).astype(BF16)
    copies[-2].wait()
    long_len = llen_ref[0]
    for c in range(chips):
        copies[2 * chunks + c].wait()
        x = xl_ref[c]
        row = lax.broadcasted_iota(jnp.int32, x.shape, 2)
        theirs[c] = jnp.where(row < long_len, x, jnp.zeros_like(x))
    copies[-4].wait()
    dv = dvl_ref[...]
    row = lax.broadcasted_iota(jnp.int32, dv.shape, 0)
    live_dv[...] = jnp.where(row < long_len, dv, jnp.zeros_like(dv))
    copies[-3].wait()
    weight[...] = master_ref[...].astype(BF16)
    within = jnp.where(interior(), 1.0, 0.0)
    inside[...] = jnp.full(inside.shape, within, F32)
    row = lax.broadcasted_iota(jnp.int32, live_rows.shape, 0) + z * live_rows.shape[0]
    live_rows[...] = jnp.where(row < long_len, 1.0, 0.0)


def long_kernel(orders, x_ref, dv_ref, xs_ref, dvs_ref, *outs):
    chips, outer, inner, rows = xs_ref.shape
    me = lax.axis_index("dp")
    chip, core = me // 2, lax.rem(me, 2)
    half = outer // 2
    for rel in range(chips):
        j = lax.bitwise_xor(chip, jnp.int32(rel))
        mine = x_ref[pl.ds((2 * j + core) * outer, outer)].reshape(outer * inner, rows)
        other = xs_ref[j].reshape(outer * inner, rows)
        prod = jnp.dot(mine, dv_ref[...], preferred_element_type=F32)
        prod = prod + jnp.dot(other, dvs_ref[...], preferred_element_type=F32)
        prod = prod.reshape(outer, inner, prod.shape[-1]).astype(BF16)
        for p, (send, keep) in enumerate(orders):
            piece = prod[p * half : (p + 1) * half]
            if rel in send:
                outs[2 * p][send.index(rel)] = piece
            else:
                outs[2 * p + 1][keep.index(rel)] = piece


def values_kernel(chips, x_ref, xs_ref, *refs):
    weights, mine_ref, other_ref, acc = refs[: chips + 1], refs[-3], refs[-2], refs[-1]
    _, outer, inner, rows = xs_ref.shape
    parts, part, width = mine_ref.shape
    half = outer // 2
    me = lax.axis_index("dp")
    z = lax.axis_index("tensor")
    chip, core = me // 2, lax.rem(me, 2)
    for which, out in ((0, mine_ref), (1, other_ref)):
        total = None
        for rel in range(chips):
            j = lax.bitwise_xor(chip, jnp.int32(rel))
            for p in range(2):
                if which == 0:
                    x = x_ref[pl.ds((2 * j + core) * outer + p * half, half)]
                else:
                    x = xs_ref[j, pl.ds(p * half, half)]
                if rel < chips - 1:
                    w = weights[rel][p * half : (p + 1) * half]
                else:
                    w = weights[rel + p][...]
                w = w.reshape(half * inner, width)
                term = contract_rows(x.reshape(half * inner, rows), w)
                total = term if total is None else total + term
        acc[...] = total
        for k in range(parts):
            j = lax.bitwise_xor(z, jnp.int32(k))
            out[k] = acc[pl.ds(pl.multiple_of(j * part, part), part), :].astype(out.dtype)


def adam_kernel(n_short, n_path, steps, *refs):
    i = pl.program_id(0)
    short, refs = refs[:n_short], refs[n_short:]
    first, refs = refs[:n_path], refs[n_path:]
    second, refs = refs[:n_path], refs[n_path:]
    master, moment1, moment2, new_master, new_moment1, new_moment2, weight = refs

    inside = interior()

    def total(terms):
        out = None
        for t in terms:
            value = t[...].reshape(master.shape).astype(F32)
            out = value if out is None else out + value
        return out

    def total_short():
        last = short[-1][...].astype(F32)
        return total(short[:-1]) + jnp.where(inside, last, 0.0)

    def run(terms):
        grad = total(terms) + total_short()
        values = adam(master[...], moment1[...], moment2[...], grad)
        new_master[...], new_moment1[...], new_moment2[...] = values
        weight[...] = values[0].astype(BF16)

    pl.when(i < steps)(lambda: run(first))
    pl.when(i >= steps)(lambda: run(second))


def place_kernel(rels, *refs):
    pieces, out, sems = refs[: len(rels)], refs[-2], refs[-1]
    outer = pieces[0].shape[0]
    me = lax.axis_index("dp")
    copies = []
    for s, (rel, piece) in enumerate(zip(rels, pieces)):
        owner = lax.bitwise_xor(me, jnp.int32(rel))
        copies.append(
            pltpu.make_async_copy(piece, out.at[pl.ds(owner * outer, outer)], sems.at[s])
        )
    for copy in copies:
        copy.start()
    for copy in copies:
        copy.wait()


def place(rels, pieces, whole, name):
    new = isinstance(whole, jax.ShapeDtypeStruct)
    return pl.pallas_call(
        functools.partial(place_kernel, rels),
        out_shape=jax.ShapeDtypeStruct(whole.shape, whole.dtype),
        in_specs=[VMEM] * len(pieces) + [ANY] * (not new),
        out_specs=ANY,
        scratch_shapes=[pltpu.SemaphoreType.DMA((len(pieces),))],
        input_output_aliases={} if new else {len(pieces): 0},
        compiler_params=params(16),
        cost_estimate=cost(0, 2 * pieces[0].size * len(pieces)),
        name=name,
    )(*pieces, *([] if new else [whole]))


def params(mib):
    return pltpu.CompilerParams(vmem_limit_bytes=mib * MIB)


def cost(flops, moved):
    return pl.CostEstimate(flops=flops, bytes_accessed=moved, transcendentals=0)


def swap(x, bit):
    n = lax.axis_size("dp")
    return lax.ppermute(x, "dp", [(i, i ^ bit) for i in range(n)])


def near_pieces(shard, bits):
    return [swap(shard, 2 * bit) for bit in bits]


def relays(near):
    half = near[0].shape[0] // 2
    return near[0][:half], near[1][half:]


def split_orders(order):
    def spread(bits):
        return [0] if not bits else [b + r for b in (0, bits[0]) for r in spread(bits[1:])]

    keep = spread(order[1:])
    return [order[0] | r for r in keep], keep


def interior():
    z = lax.axis_index("tensor")
    return (z > 0) & (z < lax.axis_size("tensor") - 1)


def outward(x):
    return lax.ppermute(x, "tensor", [(i, i ^ 1) for i in range(lax.axis_size("tensor"))])


def inward(x):
    n, m = lax.axis_size("tensor"), lax.axis_size("dp")
    pairs = []
    for d in range(m):
        for i in range(n):
            to = (d, i ^ 3) if 0 < i < n - 1 else (d ^ 1, i)
            pairs.append((d * n + i, to[0] * n + to[1]))
    return lax.ppermute(x, ("dp", "tensor"), pairs)


def after(x, *earlier):
    return lax.optimization_barrier((x, *earlier))[0]


def plus(a, b):
    return (a.astype(F32) + b.astype(F32)).astype(BF16)


def body(x_long, dv_long, x_short, dv_short, long_len, short_len, master, moment1, moment2):
    n = lax.axis_size("dp")
    parts = lax.axis_size("tensor")
    outer, inner, width = master.shape
    rows = x_long.shape[0]
    short_rows, _, inner_whole = x_short.shape
    chips = n // 2
    own_rows = rows // parts
    half = outer // 2
    aligned = (
        n & (n - 1) == 0
        and chips == 4
        and parts == 4
        and short_rows % 512 == 0
        and outer % 2 == 0
        and inner % 16 == 0
        and own_rows % 16 == 0
        and rows % 128 == 0
        and short_rows % 128 == 0
        and inner_whole % 128 == 0
        and width % 128 == 0
    )
    if not aligned:
        return plain_body(
            x_long, dv_long, x_short, dv_short, long_len, short_len, master, moment1, moment2
        )
    bits = [1 << b for b in range(chips.bit_length() - 1)]
    paths = [bits, bits[::-1]]

    x_t = jnp.transpose(x_long, (1, 2, 0))
    dv_other = swap(dv_long, 1)
    block = jax.ShapeDtypeStruct((outer, inner, width), BF16)
    *blocks, theirs, live_dv, weight, end_mask, row_mask = pl.pallas_call(
        first_kernel,
        out_shape=[
            *[block] * 4,
            jax.ShapeDtypeStruct((chips, outer, inner, rows), BF16),
            jax.ShapeDtypeStruct(dv_long.shape, BF16),
            block,
            jax.ShapeDtypeStruct((1, 1, width), F32),
            jax.ShapeDtypeStruct((own_rows, width), F32),
        ],
        in_specs=[HBM] * 7,
        out_specs=[VMEM] * 9,
        scratch_shapes=[
            pltpu.SMEM((1,), jnp.int32),
            pltpu.SMEM((1,), jnp.int32),
            pltpu.VMEM(x_short.shape, BF16),
            pltpu.VMEM(dv_short.shape, BF16),
            pltpu.VMEM((chips, outer, inner, rows), BF16),
            pltpu.VMEM(dv_long.shape, BF16),
            pltpu.VMEM(master.shape, F32),
            pltpu.VMEM((short_rows // 4 * outer, inner_whole), F32),
            pltpu.VMEM((4, outer * inner, short_rows), BF16),
            pltpu.SemaphoreType.DMA((12 + chips,)),
        ],
        compiler_params=params(50),
        cost_estimate=cost(2 * short_rows * outer * inner_whole * width, 8 * MIB),
        name="first",
    )(short_len, long_len, x_short, dv_short, x_t, dv_long, master)
    within = end_mask > 0.0
    x_other = swap(theirs, 1)
    from_end = outward(blocks[3])
    near_weight = near_pieces(weight, bits)

    orders = [split_orders(order) for order in paths]
    long_parts = pl.pallas_call(
        functools.partial(long_kernel, orders),
        out_shape=[jax.ShapeDtypeStruct((chips // 2, half, inner, width), BF16)] * 4,
        in_specs=[VMEM] * 4,
        out_specs=[VMEM] * 4,
        compiler_params=params(16),
        cost_estimate=cost(4 * rows * chips * outer * inner * width, 4 * MIB),
        name="long_grad",
    )(x_t, live_dv, x_other, dv_other)
    received = [swap(long_parts[2 * p], 2 * paths[p][0]) for p in range(2)]

    second = after(blocks[2], *long_parts)
    across_sent = plus(second, from_end)
    across = inward(across_sent)
    middle = outward(after(second, from_end))

    onward, far_weight = [], []
    for p, relay in enumerate(relays(near_weight)):
        got = after(received[p], across_sent)
        sent = plus(long_parts[2 * p + 1][1], got[1])
        arrived = swap(jnp.concatenate([sent, relay]), 2 * paths[p][1])
        onward.append(arrived[:half])
        far_weight.append(arrived[half:])

    near_sent = plus(blocks[1], jnp.where(within, across, jnp.zeros_like(across)))
    near = outward(near_sent)
    inside_sent = plus(blocks[3], middle)
    inside = inward(inside_sent)

    weights = [weight, *near_weight, *far_weight]
    mine, other = pl.pallas_call(
        functools.partial(values_kernel, chips),
        out_shape=[jax.ShapeDtypeStruct((parts, own_rows, width), F32)] * 2,
        in_specs=[VMEM] * (2 + len(weights)),
        out_specs=[VMEM] * 2,
        scratch_shapes=[pltpu.VMEM((rows, width), F32)],
        compiler_params=params(16),
        cost_estimate=cost(0, 0),
        name="values",
    )(x_t, x_other, *weights)

    short_terms = [blocks[0], near, inside]
    long_terms = [
        [long_parts[2 * p + 1][:1], received[p][:1], onward[p][None]]
        for p in range(2)
    ]

    per = 2 if half % 2 == 0 else 1
    steps = half // per
    whole = pl.BlockSpec((per, inner, width), lambda i: (i, 0, 0))
    low4 = pl.BlockSpec((1, per, inner, width), lambda i: (0, jnp.minimum(i, steps - 1), 0, 0))
    high4 = pl.BlockSpec((1, per, inner, width), lambda i: (0, jnp.maximum(i - steps, 0), 0, 0))
    n_path = len(long_terms[0])
    state = jax.ShapeDtypeStruct(master.shape, F32)
    new_master, new_moment1, new_moment2, next_shard = pl.pallas_call(
        functools.partial(adam_kernel, len(short_terms), n_path, steps),
        grid=(2 * steps,),
        out_shape=[state, state, state, jax.ShapeDtypeStruct(master.shape, BF16)],
        in_specs=[whole] * len(short_terms) + [low4] * n_path + [high4] * n_path + [whole] * 3,
        out_specs=[whole] * 4,
        compiler_params=params(16),
        cost_estimate=cost(20 * outer * inner * width, 10 * MIB),
        name="adam",
    )(*short_terms, *long_terms[0], *long_terms[1], master, moment1, moment2)

    near_next = near_pieces(next_shard, bits)
    total = mine + swap(after(other, next_shard), 1)
    shares = total.astype(BF16)
    across_sent = plus(shares[2], outward(shares[3]))
    across = inward(across_sent)
    middle = outward(after(shares[2], across_sent))
    near_sent = plus(shares[1], jnp.where(within[0], across, jnp.zeros_like(across)))
    inside_sent = plus(shares[3], middle)
    near, inside = outward(near_sent), inward(inside_sent)
    values = total[0] + near.astype(F32)
    values = values + jnp.where(within[0], inside.astype(F32), 0.0)
    v_long = jnp.where(row_mask > 0.0, values, 0.0).astype(BF16)

    low, high = relays([after(x, near_sent, inside_sent) for x in near_next])
    early = [next_shard, *near_next]
    early = early + [swap(x, 1) for x in early]
    whole_shape = jax.ShapeDtypeStruct((n * outer, inner, width), BF16)
    placed = place([0, 2, 4, 1, 3, 5], early, whole_shape, "place_near")
    far_piece = jnp.concatenate([swap(low, 2 * bits[1]), swap(high, 2 * bits[0])])
    far_piece = after(far_piece, near, inside, placed)
    far = [far_piece, swap(far_piece, 1)]
    next_weight = place([6, 7], far, placed, "place_far")
    return (v_long, new_master, new_moment1, new_moment2, next_weight)


def solution(mesh):
    placed = (
        P("dp", None, "tensor"),
        P("dp", None),
        P("tensor", "dp", None),
        P("tensor", None),
        P("dp"),
        P("tensor"),
        P("dp", "tensor", None),
        P("dp", "tensor", None),
        P("dp", "tensor", None),
    )
    return jax.shard_map(
        body,
        mesh=mesh,
        in_specs=placed,
        out_specs=(
            P(("dp", "tensor"), None),
            P("dp", "tensor", None),
            P("dp", "tensor", None),
            P("dp", "tensor", None),
            P(None, "tensor", None),
        ),
        check_vma=False,
    )
```

```python
import functools

import jax
import jax.numpy as jnp
from jax import lax
from jax.experimental import pallas as pl
from jax.experimental.pallas import tpu as pltpu
from jax.sharding import PartitionSpec as P

BF16 = jnp.bfloat16
F32 = jnp.float32
MIB = 1 << 20
VMEM = pl.BlockSpec(memory_space=pltpu.VMEM)
SMEM = pl.BlockSpec(memory_space=pltpu.SMEM)
ANY = pl.BlockSpec(memory_space=pl.ANY)
HBM = pl.BlockSpec(memory_space=pltpu.HBM)


def contract_rows(left, right):
    return lax.dot_general(
        left, right, (((0,), (0,)), ((), ())), preferred_element_type=jnp.float32
    )


def adam(master, moment1, moment2, grad):
    new_moment1 = 0.9 * moment1 + 0.1 * grad
    new_moment2 = 0.999 * moment2 + 0.001 * grad * grad
    first_corr = 1.0 - 0.9**10
    second_corr = 1.0 - 0.999**10
    update = new_moment1 / first_corr / (jnp.sqrt(new_moment2 / second_corr) + 1e-08)
    new_master = master - 0.01 * (update + 0.1 * master)
    return new_master, new_moment1, new_moment2


def plain_body(x_long, dv_long, x_short, dv_short, long_len, short_len, master, moment1, moment2):
    weight_shard = master.astype(BF16)
    long_rows, _, inner_part = x_long.shape
    kv_width = master.shape[2]
    short_rows, outer_part, inner_whole = x_short.shape
    piece = lax.all_gather(weight_shard, "dp", axis=0, tiled=True)
    flat_inputs = x_long.reshape(long_rows, piece.shape[0] * inner_part)
    flat_piece = piece.reshape(piece.shape[0] * inner_part, kv_width)
    partial_values = jnp.dot(flat_inputs, flat_piece, preferred_element_type=F32)
    values = lax.psum_scatter(partial_values, "tensor", scatter_dimension=0, tiled=True)
    own_rows = values.shape[0]
    row_start = lax.axis_index("tensor") * own_rows
    own_live = row_start + jnp.arange(own_rows, dtype=jnp.int32) < long_len[0]
    v_long = jnp.where(own_live[:, None], values, 0.0).astype(BF16)
    long_live = jnp.arange(long_rows, dtype=jnp.int32) < long_len[0]
    short_live = jnp.arange(short_rows, dtype=jnp.int32) < short_len[0]
    live_dv_long = jnp.where(long_live[:, None], dv_long, jnp.zeros_like(dv_long))
    live_dv_short = jnp.where(short_live[:, None], dv_short, jnp.zeros_like(dv_short))
    count = lax.axis_size("dp") * master.shape[0]
    grad_long = lax.psum_scatter(
        contract_rows(flat_inputs, live_dv_long).reshape(count, inner_part, kv_width),
        "dp",
        scatter_dimension=0,
        tiled=True,
    )
    flat_inputs = x_short.reshape(short_rows, outer_part * inner_whole)
    product = contract_rows(flat_inputs, live_dv_short).reshape(outer_part, inner_whole, kv_width)
    grad_short = lax.psum_scatter(product, "tensor", scatter_dimension=1, tiled=True)
    new_master, new_moment1, new_moment2 = adam(master, moment1, moment2, grad_long + grad_short)
    next_weight = lax.all_gather(new_master.astype(BF16), "dp", axis=0, tiled=True)
    return (v_long, new_master, new_moment1, new_moment2, next_weight)


def first_kernel(slen_hbm, llen_hbm, xs_hbm, dvs_hbm, xl_hbm, dvl_hbm, master_hbm, *refs):
    blocks, theirs, live_dv, weight, inside, live_rows = refs[:4], *refs[4:9]
    slen_ref, llen_ref, xs_ref, dvs_ref, xl_ref, dvl_ref, master_ref, wide, turned, sems = refs[9:]
    rows, outer, inner = xs_ref.shape
    chips, owned, _, long_rows = theirs.shape
    chunks = 4
    chunk = rows // chunks
    part = inner // 4
    z = lax.axis_index("tensor")
    other = 1 - lax.rem(lax.axis_index("dp"), 2)
    pairs = []
    for c in range(chunks):
        span = pl.ds(c * chunk, chunk)
        pairs.append((xs_hbm.at[span], xs_ref.at[span]))
        pairs.append((dvs_hbm.at[span], dvs_ref.at[span]))
    for c in range(chips):
        pairs.append((xl_hbm.at[pl.ds((2 * c + other) * owned, owned)], xl_ref.at[c]))
    pairs.append((dvl_hbm, dvl_ref))
    pairs.append((master_hbm, master_ref))
    pairs.append((llen_hbm, llen_ref))
    pairs.append((slen_hbm, slen_ref))
    copies = [pltpu.make_async_copy(*pair, sems.at[i]) for i, pair in enumerate(pairs)]
    for copy in copies[-2:] + copies[:-2]:
        copy.start()
    copies[-1].wait()
    for c in range(chunks):
        copies[2 * c].wait()
        copies[2 * c + 1].wait()
        span = slice(c * chunk, (c + 1) * chunk)
        wide[...] = xs_ref[span].reshape(chunk * outer, inner).astype(F32)
        for a in range(outer):
            xa = wide[pl.ds(a, chunk, outer), :].astype(BF16).T
            for j in range(4):
                turned[j, a * part : (a + 1) * part, span] = xa[j * part : (j + 1) * part]
        dv = dvs_ref[span]
        row = lax.broadcasted_iota(jnp.int32, dv.shape, 0) + c * chunk
        dvs_ref[span] = jnp.where(row < slen_ref[0], dv, jnp.zeros_like(dv))
    for k in (3, 2, 1, 0):
        x = turned[lax.bitwise_xor(z, jnp.int32(k))]
        prod = jnp.dot(x, dvs_ref[...], preferred_element_type=F32)
        blocks[k][...] = prod.reshape(outer, part, prod.shape[1]).astype(BF16)
    copies[-2].wait()
    long_len = llen_ref[0]
    for c in range(chips):
        copies[2 * chunks + c].wait()
        x = xl_ref[c]
        row = lax.broadcasted_iota(jnp.int32, x.shape, 2)
        theirs[c] = jnp.where(row < long_len, x, jnp.zeros_like(x))
    copies[-4].wait()
    dv = dvl_ref[...]
    row = lax.broadcasted_iota(jnp.int32, dv.shape, 0)
    live_dv[...] = jnp.where(row < long_len, dv, jnp.zeros_like(dv))
    copies[-3].wait()
    weight[...] = master_ref[...].astype(BF16)
    within = jnp.where(interior(), 1.0, 0.0)
    inside[...] = jnp.full(inside.shape, within, F32)
    row = lax.broadcasted_iota(jnp.int32, live_rows.shape, 0) + z * live_rows.shape[0]
    live_rows[...] = jnp.where(row < long_len, 1.0, 0.0)


def plane_steps():
    core = lax.rem(lax.axis_index("dp"), 2)
    return 0, 1 + core, 2 - core, 3


def long_kernel(x_ref, dv_ref, xs_ref, dvs_ref, *outs):
    chips, outer, inner, rows = xs_ref.shape
    me = lax.axis_index("dp")
    chip, core = me // 2, lax.rem(me, 2)
    for out, rel in reversed(list(zip(outs, plane_steps()))):
        j = lax.bitwise_xor(chip, jnp.int32(rel))
        mine = x_ref[pl.ds((2 * j + core) * outer, outer)].reshape(outer * inner, rows)
        other = xs_ref[j].reshape(outer * inner, rows)
        prod = jnp.dot(mine, dv_ref[...], preferred_element_type=F32)
        prod = prod + jnp.dot(other, dvs_ref[...], preferred_element_type=F32)
        out[...] = prod.reshape(outer, inner, prod.shape[-1]).astype(BF16)


def values_kernel(x_ref, xs_ref, *refs):
    weights, mine_ref, other_ref, acc = refs[:4], refs[-3], refs[-2], refs[-1]
    _, outer, inner, rows = xs_ref.shape
    parts, part, width = mine_ref.shape
    me = lax.axis_index("dp")
    z = lax.axis_index("tensor")
    chip, core = me // 2, lax.rem(me, 2)
    for which, out in ((0, mine_ref), (1, other_ref)):
        total = None
        for weight, rel in zip(weights, plane_steps()):
            j = lax.bitwise_xor(chip, jnp.int32(rel))
            x = xs_ref[j] if which else x_ref[pl.ds((2 * j + core) * outer, outer)]
            w = weight[...].reshape(outer * inner, width)
            term = contract_rows(x.reshape(outer * inner, rows), w)
            total = term if total is None else total + term
        acc[...] = total
        for k in range(parts):
            j = lax.bitwise_xor(z, jnp.int32(k))
            out[k] = acc[pl.ds(pl.multiple_of(j * part, part), part), :].astype(out.dtype)


def update(refs):
    own, near, inside, *terms, master, moment1, moment2 = refs
    grad = own[...].astype(F32) + near[...].astype(F32)
    grad = grad + jnp.where(interior(), inside[...].astype(F32), 0.0)
    for t in terms:
        grad = grad + t[...].astype(F32)
    return adam(master[...], moment1[...], moment2[...], grad)


def weight_kernel(*refs):
    refs[-1][...] = update(refs[:-1])[0].astype(BF16)


def state_kernel(*refs):
    for out, value in zip(refs[-3:], update(refs[:-3])):
        out[...] = value


def place_kernel(kinds, n, *refs):
    pieces, out, sems = refs[:n], refs[-2], refs[-1]
    outer = pieces[0].shape[0]
    me = lax.axis_index("dp")
    steps = plane_steps()
    copies = []
    for s, (step, core) in enumerate(kinds):
        if core and step in (1, 2):
            step = 3 - step
        rel = 2 * jnp.int32(steps[step]) + core
        owner = lax.bitwise_xor(me, rel)
        target = out.at[pl.ds(owner * outer, outer)]
        copies.append(pltpu.make_async_copy(pieces[s], target, sems.at[s]))
    for copy in copies:
        copy.start()
    for copy in copies:
        copy.wait()


def place(kinds, pieces, whole, name):
    new = isinstance(whole, jax.ShapeDtypeStruct)
    return pl.pallas_call(
        functools.partial(place_kernel, kinds, len(pieces)),
        out_shape=jax.ShapeDtypeStruct(whole.shape, whole.dtype),
        in_specs=[VMEM] * len(pieces) + [ANY] * (not new),
        out_specs=ANY,
        scratch_shapes=[pltpu.SemaphoreType.DMA((len(pieces),))],
        input_output_aliases={} if new else {len(pieces): 0},
        compiler_params=params(16),
        cost_estimate=cost(0, 2 * sum(p.size for p in pieces)),
        name=name,
    )(*pieces, *([] if new else [whole]))


def params(mib):
    return pltpu.CompilerParams(vmem_limit_bytes=mib * MIB)


def cost(flops, moved):
    return pl.CostEstimate(flops=flops, bytes_accessed=moved, transcendentals=0)


def swap(x, bit):
    n = lax.axis_size("dp")
    return lax.ppermute(x, "dp", [(i, i ^ bit) for i in range(n)])


def cross(x, turn):
    n = lax.axis_size("dp")
    return lax.ppermute(x, "dp", [(i, i ^ (2 << ((i & 1) ^ turn))) for i in range(n)])


def interior():
    z = lax.axis_index("tensor")
    return (z > 0) & (z < lax.axis_size("tensor") - 1)


def outward(x):
    return lax.ppermute(x, "tensor", [(i, i ^ 1) for i in range(lax.axis_size("tensor"))])


def inward(x):
    n, m = lax.axis_size("tensor"), lax.axis_size("dp")
    pairs = []
    for d in range(m):
        for i in range(n):
            to = (d, i ^ 3) if 0 < i < n - 1 else (d ^ 1, i)
            pairs.append((d * n + i, to[0] * n + to[1]))
    return lax.ppermute(x, ("dp", "tensor"), pairs)


def after(x, *earlier):
    return lax.optimization_barrier((x, *earlier))[0]


def plus(a, b):
    return (a.astype(F32) + b.astype(F32)).astype(BF16)


def body(x_long, dv_long, x_short, dv_short, long_len, short_len, master, moment1, moment2):
    n = lax.axis_size("dp")
    parts = lax.axis_size("tensor")
    outer, inner, width = master.shape
    rows = x_long.shape[0]
    short_rows, _, inner_whole = x_short.shape
    chips = n // 2
    own_rows = rows // parts
    aligned = (
        n & (n - 1) == 0
        and chips == 4
        and parts == 4
        and short_rows % 512 == 0
        and inner % 16 == 0
        and own_rows % 16 == 0
        and rows % 128 == 0
        and short_rows % 128 == 0
        and inner_whole % 128 == 0
        and width % 128 == 0
    )
    if not aligned:
        return plain_body(
            x_long, dv_long, x_short, dv_short, long_len, short_len, master, moment1, moment2
        )
    x_t = jnp.transpose(x_long, (1, 2, 0))
    dv_other = swap(dv_long, 1)
    block = jax.ShapeDtypeStruct((outer, inner, width), BF16)
    *blocks, theirs, live_dv, weight, end_mask, row_mask = pl.pallas_call(
        first_kernel,
        out_shape=[
            *[block] * 4,
            jax.ShapeDtypeStruct((chips, outer, inner, rows), BF16),
            jax.ShapeDtypeStruct(dv_long.shape, BF16),
            block,
            jax.ShapeDtypeStruct((1, 1, width), F32),
            jax.ShapeDtypeStruct((own_rows, width), F32),
        ],
        in_specs=[HBM] * 7,
        out_specs=[VMEM] * 9,
        scratch_shapes=[
            pltpu.SMEM((1,), jnp.int32),
            pltpu.SMEM((1,), jnp.int32),
            pltpu.VMEM(x_short.shape, BF16),
            pltpu.VMEM(dv_short.shape, BF16),
            pltpu.VMEM((chips, outer, inner, rows), BF16),
            pltpu.VMEM(dv_long.shape, BF16),
            pltpu.VMEM(master.shape, F32),
            pltpu.VMEM((short_rows // 4 * outer, inner_whole), F32),
            pltpu.VMEM((4, outer * inner, short_rows), BF16),
            pltpu.SemaphoreType.DMA((12 + chips,)),
        ],
        compiler_params=params(50),
        cost_estimate=cost(2 * short_rows * outer * inner_whole * width, 8 * MIB),
        name="first",
    )(short_len, long_len, x_short, dv_short, x_t, dv_long, master)
    within = end_mask > 0.0
    x_other = swap(theirs, 1)
    from_end = outward(blocks[3])
    weights = [weight, cross(weight, 0), cross(weight, 1)]
    long_own, long_first, long_second, long_far = pl.pallas_call(
        long_kernel,
        out_shape=[block] * 4,
        in_specs=[VMEM] * 4,
        out_specs=[VMEM] * 4,
        compiler_params=params(16),
        cost_estimate=cost(4 * rows * chips * outer * inner * width, 4 * MIB),
        name="long_grad",
    )(x_t, live_dv, x_other, dv_other)

    far_sum = cross(long_far, 1)
    second_sum = cross(long_second, 1)
    middle = outward(blocks[2])
    across_done = plus(after(blocks[2], long_own), from_end)
    across = inward(across_done)
    first_sent = plus(long_first, far_sum)
    first_sum = cross(first_sent, 0)
    inside_sent = plus(after(blocks[3], first_sent), middle)
    inside = inward(inside_sent)
    handed = after(weights[1], inside_sent)
    weights.append(cross(handed, 1))
    across = after(across, handed)
    near_sent = plus(blocks[1], jnp.where(within, across, jnp.zeros_like(across)))
    near = outward(near_sent)

    mine, other = pl.pallas_call(
        values_kernel,
        out_shape=[jax.ShapeDtypeStruct((parts, own_rows, width), t) for t in (F32, BF16)],
        in_specs=[VMEM] * 6,
        out_specs=[VMEM] * 2,
        scratch_shapes=[pltpu.VMEM((rows, width), F32)],
        compiler_params=params(16),
        cost_estimate=cost(4 * rows * chips * outer * inner * width, 6 * MIB),
        name="values",
    )(x_t, x_other, *weights)

    arrived = [after(blocks[0], mine), near, inside, long_own, second_sum, first_sum]
    arrived += [master, moment1, moment2]
    next_shard = pl.pallas_call(
        weight_kernel,
        out_shape=block,
        in_specs=[VMEM] * len(arrived),
        out_specs=VMEM,
        compiler_params=params(16),
        cost_estimate=cost(20 * outer * inner * width, 5 * MIB),
        name="next_weight",
    )(*arrived)

    gathered = [next_shard, cross(next_shard, 0), cross(next_shard, 1)]

    total = mine + swap(after(other, next_shard), 1).astype(F32)
    shares = total.astype(BF16)
    v_across_sent = plus(shares[2], outward(shares[3]))
    v_across = inward(v_across_sent)
    v_middle = outward(after(shares[2], v_across_sent))
    v_near = plus(shares[1], jnp.where(within[0], v_across, jnp.zeros_like(v_across)))
    v_inside = plus(shares[3], v_middle)
    values = total[0] + outward(v_near).astype(F32)
    values = values + jnp.where(within[0], inward(v_inside).astype(F32), 0.0)
    v_long = jnp.where(row_mask > 0.0, values, 0.0).astype(BF16)

    new_state = pl.pallas_call(
        state_kernel,
        out_shape=[jax.ShapeDtypeStruct(master.shape, F32)] * 3,
        in_specs=[VMEM] * len(arrived),
        out_specs=[VMEM] * 3,
        compiler_params=params(16),
        cost_estimate=cost(20 * outer * inner * width, 10 * MIB),
        name="new_state",
    )(after(arrived[0], shares), *arrived[1:])

    far = cross(after(gathered[1], new_state[0], v_inside), 1)
    early = [after(next_shard, new_state[0], v_long), *gathered[1:]]
    early = early + [swap(x, 1) for x in early]
    kinds = [(step, core) for core in range(2) for step in range(3)]
    whole_shape = jax.ShapeDtypeStruct((n * outer, inner, width), BF16)
    placed = place(kinds, early, whole_shape, "place_near")
    next_weight = place([(3, 0), (3, 1)], [far, swap(far, 1)], placed, "place_far")
    return (v_long, *new_state, next_weight)


def solution(mesh):
    placed = (
        P("dp", None, "tensor"),
        P("dp", None),
        P("tensor", "dp", None),
        P("tensor", None),
        P("dp"),
        P("tensor"),
        P("dp", "tensor", None),
        P("dp", "tensor", None),
        P("dp", "tensor", None),
    )
    return jax.shard_map(
        body,
        mesh=mesh,
        in_specs=placed,
        out_specs=(
            P(("dp", "tensor"), None),
            P("dp", "tensor", None),
            P("dp", "tensor", None),
            P("dp", "tensor", None),
            P(None, "tensor", None),
        ),
        check_vma=False,
    )
```

```python
import functools

import jax
import jax.numpy as jnp
from jax import lax
from jax.experimental import pallas as pl
from jax.experimental.pallas import tpu as pltpu
from jax.sharding import PartitionSpec as P

BF16 = jnp.bfloat16
F32 = jnp.float32
MIB = 1 << 20
VMEM = pl.BlockSpec(memory_space=pltpu.VMEM)
SMEM = pl.BlockSpec(memory_space=pltpu.SMEM)
ANY = pl.BlockSpec(memory_space=pl.ANY)
HBM = pl.BlockSpec(memory_space=pltpu.HBM)


def contract_rows(left, right):
    return lax.dot_general(
        left, right, (((0,), (0,)), ((), ())), preferred_element_type=jnp.float32
    )


def adam(master, moment1, moment2, grad):
    new_moment1 = 0.9 * moment1 + 0.1 * grad
    new_moment2 = 0.999 * moment2 + 0.001 * grad * grad
    first_corr = 1.0 - 0.9**10
    second_corr = 1.0 - 0.999**10
    update = new_moment1 / first_corr / (jnp.sqrt(new_moment2 / second_corr) + 1e-08)
    new_master = master - 0.01 * (update + 0.1 * master)
    return new_master, new_moment1, new_moment2


def plain_body(x_long, dv_long, x_short, dv_short, long_len, short_len, master, moment1, moment2):
    weight_shard = master.astype(BF16)
    long_rows, _, inner_part = x_long.shape
    kv_width = master.shape[2]
    short_rows, outer_part, inner_whole = x_short.shape
    piece = lax.all_gather(weight_shard, "dp", axis=0, tiled=True)
    flat_inputs = x_long.reshape(long_rows, piece.shape[0] * inner_part)
    flat_piece = piece.reshape(piece.shape[0] * inner_part, kv_width)
    partial_values = jnp.dot(flat_inputs, flat_piece, preferred_element_type=F32)
    values = lax.psum_scatter(partial_values, "tensor", scatter_dimension=0, tiled=True)
    own_rows = values.shape[0]
    row_start = lax.axis_index("tensor") * own_rows
    own_live = row_start + jnp.arange(own_rows, dtype=jnp.int32) < long_len[0]
    v_long = jnp.where(own_live[:, None], values, 0.0).astype(BF16)
    long_live = jnp.arange(long_rows, dtype=jnp.int32) < long_len[0]
    short_live = jnp.arange(short_rows, dtype=jnp.int32) < short_len[0]
    live_dv_long = jnp.where(long_live[:, None], dv_long, jnp.zeros_like(dv_long))
    live_dv_short = jnp.where(short_live[:, None], dv_short, jnp.zeros_like(dv_short))
    count = lax.axis_size("dp") * master.shape[0]
    grad_long = lax.psum_scatter(
        contract_rows(flat_inputs, live_dv_long).reshape(count, inner_part, kv_width),
        "dp",
        scatter_dimension=0,
        tiled=True,
    )
    flat_inputs = x_short.reshape(short_rows, outer_part * inner_whole)
    product = contract_rows(flat_inputs, live_dv_short).reshape(outer_part, inner_whole, kv_width)
    grad_short = lax.psum_scatter(product, "tensor", scatter_dimension=1, tiled=True)
    new_master, new_moment1, new_moment2 = adam(master, moment1, moment2, grad_long + grad_short)
    next_weight = lax.all_gather(new_master.astype(BF16), "dp", axis=0, tiled=True)
    return (v_long, new_master, new_moment1, new_moment2, next_weight)


def first_kernel(slen_hbm, llen_hbm, xs_hbm, dvs_hbm, xl_hbm, dvl_hbm, master_hbm, *refs):
    blocks, theirs, live_dv, weight, inside, live_rows = refs[:4], *refs[4:9]
    slen_ref, llen_ref, xs_ref, dvs_ref, xl_ref, dvl_ref, master_ref, wide, turned, sems = refs[9:]
    rows, outer, inner = xs_ref.shape
    chips, owned, _, long_rows = theirs.shape
    chunks = 4
    chunk = rows // chunks
    part = inner // 4
    z = lax.axis_index("tensor")
    other = 1 - lax.rem(lax.axis_index("dp"), 2)
    pairs = []
    for c in range(chunks):
        span = pl.ds(c * chunk, chunk)
        pairs.append((xs_hbm.at[span], xs_ref.at[span]))
        pairs.append((dvs_hbm.at[span], dvs_ref.at[span]))
    for c in range(chips):
        pairs.append((xl_hbm.at[pl.ds((2 * c + other) * owned, owned)], xl_ref.at[c]))
    pairs.append((dvl_hbm, dvl_ref))
    pairs.append((master_hbm, master_ref))
    pairs.append((llen_hbm, llen_ref))
    pairs.append((slen_hbm, slen_ref))
    copies = [pltpu.make_async_copy(*pair, sems.at[i]) for i, pair in enumerate(pairs)]
    for copy in copies[-2:] + copies[:-2]:
        copy.start()
    copies[-1].wait()
    for c in range(chunks):
        copies[2 * c].wait()
        copies[2 * c + 1].wait()
        span = slice(c * chunk, (c + 1) * chunk)
        wide[...] = xs_ref[span].reshape(chunk * outer, inner).astype(F32)
        for a in range(outer):
            xa = wide[pl.ds(a, chunk, outer), :].astype(BF16).T
            for j in range(4):
                turned[j, a * part : (a + 1) * part, span] = xa[j * part : (j + 1) * part]
        dv = dvs_ref[span]
        row = lax.broadcasted_iota(jnp.int32, dv.shape, 0) + c * chunk
        dvs_ref[span] = jnp.where(row < slen_ref[0], dv, jnp.zeros_like(dv))
    for k in (3, 2, 1, 0):
        x = turned[lax.bitwise_xor(z, jnp.int32(k))]
        prod = jnp.dot(x, dvs_ref[...], preferred_element_type=F32)
        blocks[k][...] = prod.reshape(outer, part, prod.shape[1]).astype(BF16)
    copies[-2].wait()
    long_len = llen_ref[0]
    for c in range(chips):
        copies[2 * chunks + c].wait()
        x = xl_ref[c]
        row = lax.broadcasted_iota(jnp.int32, x.shape, 2)
        theirs[c] = jnp.where(row < long_len, x, jnp.zeros_like(x))
    copies[-4].wait()
    dv = dvl_ref[...]
    row = lax.broadcasted_iota(jnp.int32, dv.shape, 0)
    live_dv[...] = jnp.where(row < long_len, dv, jnp.zeros_like(dv))
    copies[-3].wait()
    weight[...] = master_ref[...].astype(BF16)
    within = jnp.where(interior(), 1.0, 0.0)
    inside[...] = jnp.full(inside.shape, within, F32)
    row = lax.broadcasted_iota(jnp.int32, live_rows.shape, 0) + z * live_rows.shape[0]
    live_rows[...] = jnp.where(row < long_len, 1.0, 0.0)


def plane_steps():
    core = lax.rem(lax.axis_index("dp"), 2)
    return 0, 1 + core, 2 - core, 3


def long_kernel(x_ref, dv_ref, xs_ref, dvs_ref, *outs):
    chips, outer, inner, rows = xs_ref.shape
    me = lax.axis_index("dp")
    chip, core = me // 2, lax.rem(me, 2)
    for out, rel in reversed(list(zip(outs, plane_steps()))):
        j = lax.bitwise_xor(chip, jnp.int32(rel))
        mine = x_ref[pl.ds((2 * j + core) * outer, outer)].reshape(outer * inner, rows)
        other = xs_ref[j].reshape(outer * inner, rows)
        prod = jnp.dot(mine, dv_ref[...], preferred_element_type=F32)
        prod = prod + jnp.dot(other, dvs_ref[...], preferred_element_type=F32)
        out[...] = prod.reshape(outer, inner, prod.shape[-1]).astype(BF16)


def values_kernel(x_ref, xs_ref, *refs):
    weights, mine_ref, other_ref, acc = refs[:4], refs[-3], refs[-2], refs[-1]
    _, outer, inner, rows = xs_ref.shape
    parts, part, width = mine_ref.shape
    me = lax.axis_index("dp")
    z = lax.axis_index("tensor")
    chip, core = me // 2, lax.rem(me, 2)
    for which, out in ((0, mine_ref), (1, other_ref)):
        total = None
        for weight, rel in zip(weights, plane_steps()):
            j = lax.bitwise_xor(chip, jnp.int32(rel))
            x = xs_ref[j] if which else x_ref[pl.ds((2 * j + core) * outer, outer)]
            w = weight[...].reshape(outer * inner, width)
            term = contract_rows(x.reshape(outer * inner, rows), w)
            total = term if total is None else total + term
        acc[...] = total
        for k in range(parts):
            j = lax.bitwise_xor(z, jnp.int32(k))
            out[k] = acc[pl.ds(pl.multiple_of(j * part, part), part), :].astype(out.dtype)


def update(refs):
    own, near, inside, *terms, master, moment1, moment2 = refs
    grad = own[...].astype(F32) + near[...].astype(F32)
    grad = grad + jnp.where(interior(), inside[...].astype(F32), 0.0)
    for t in terms:
        grad = grad + t[...].astype(F32)
    return adam(master[...], moment1[...], moment2[...], grad)


def weight_kernel(*refs):
    refs[-1][...] = update(refs[:-1])[0].astype(BF16)


def state_kernel(*refs):
    for out, value in zip(refs[-3:], update(refs[:-3])):
        out[...] = value


def place_kernel(kinds, n, *refs):
    pieces, out, sems = refs[:n], refs[-2], refs[-1]
    outer = pieces[0].shape[0]
    me = lax.axis_index("dp")
    steps = plane_steps()
    copies = []
    for s, (step, core) in enumerate(kinds):
        if core and step in (1, 2):
            step = 3 - step
        rel = 2 * jnp.int32(steps[step]) + core
        owner = lax.bitwise_xor(me, rel)
        target = out.at[pl.ds(owner * outer, outer)]
        copies.append(pltpu.make_async_copy(pieces[s], target, sems.at[s]))
    for copy in copies:
        copy.start()
    for copy in copies:
        copy.wait()


def place(kinds, pieces, whole, name):
    new = isinstance(whole, jax.ShapeDtypeStruct)
    return pl.pallas_call(
        functools.partial(place_kernel, kinds, len(pieces)),
        out_shape=jax.ShapeDtypeStruct(whole.shape, whole.dtype),
        in_specs=[VMEM] * len(pieces) + [ANY] * (not new),
        out_specs=ANY,
        scratch_shapes=[pltpu.SemaphoreType.DMA((len(pieces),))],
        input_output_aliases={} if new else {len(pieces): 0},
        compiler_params=params(16),
        cost_estimate=cost(0, 2 * sum(p.size for p in pieces)),
        name=name,
    )(*pieces, *([] if new else [whole]))


def params(mib):
    return pltpu.CompilerParams(vmem_limit_bytes=mib * MIB)


def cost(flops, moved):
    return pl.CostEstimate(flops=flops, bytes_accessed=moved, transcendentals=0)


def swap(x, bit):
    n = lax.axis_size("dp")
    return lax.ppermute(x, "dp", [(i, i ^ bit) for i in range(n)])


def cross(x, turn):
    n = lax.axis_size("dp")
    return lax.ppermute(x, "dp", [(i, i ^ (2 << ((i & 1) ^ turn))) for i in range(n)])


def interior():
    z = lax.axis_index("tensor")
    return (z > 0) & (z < lax.axis_size("tensor") - 1)


def outward(x):
    return lax.ppermute(x, "tensor", [(i, i ^ 1) for i in range(lax.axis_size("tensor"))])


def inward(x):
    n, m = lax.axis_size("tensor"), lax.axis_size("dp")
    pairs = []
    for d in range(m):
        for i in range(n):
            to = (d, i ^ 3) if 0 < i < n - 1 else (d ^ 1, i)
            pairs.append((d * n + i, to[0] * n + to[1]))
    return lax.ppermute(x, ("dp", "tensor"), pairs)


def after(x, *earlier):
    return lax.optimization_barrier((x, *earlier))[0]


def plus(a, b):
    return (a.astype(F32) + b.astype(F32)).astype(BF16)


def body(x_long, dv_long, x_short, dv_short, long_len, short_len, master, moment1, moment2):
    n = lax.axis_size("dp")
    parts = lax.axis_size("tensor")
    outer, inner, width = master.shape
    rows = x_long.shape[0]
    short_rows, _, inner_whole = x_short.shape
    chips = n // 2
    own_rows = rows // parts
    aligned = (
        n & (n - 1) == 0
        and chips == 4
        and parts == 4
        and short_rows % 512 == 0
        and inner % 16 == 0
        and own_rows % 16 == 0
        and rows % 128 == 0
        and short_rows % 128 == 0
        and inner_whole % 128 == 0
        and width % 128 == 0
    )
    if not aligned:
        return plain_body(
            x_long, dv_long, x_short, dv_short, long_len, short_len, master, moment1, moment2
        )
    x_t = jnp.transpose(x_long, (1, 2, 0))
    dv_other = swap(dv_long, 1)
    block = jax.ShapeDtypeStruct((outer, inner, width), BF16)
    *blocks, theirs, live_dv, weight, end_mask, row_mask = pl.pallas_call(
        first_kernel,
        out_shape=[
            *[block] * 4,
            jax.ShapeDtypeStruct((chips, outer, inner, rows), BF16),
            jax.ShapeDtypeStruct(dv_long.shape, BF16),
            block,
            jax.ShapeDtypeStruct((1, 1, width), F32),
            jax.ShapeDtypeStruct((own_rows, width), F32),
        ],
        in_specs=[HBM] * 7,
        out_specs=[VMEM] * 9,
        scratch_shapes=[
            pltpu.SMEM((1,), jnp.int32),
            pltpu.SMEM((1,), jnp.int32),
            pltpu.VMEM(x_short.shape, BF16),
            pltpu.VMEM(dv_short.shape, BF16),
            pltpu.VMEM((chips, outer, inner, rows), BF16),
            pltpu.VMEM(dv_long.shape, BF16),
            pltpu.VMEM(master.shape, F32),
            pltpu.VMEM((short_rows // 4 * outer, inner_whole), F32),
            pltpu.VMEM((4, outer * inner, short_rows), BF16),
            pltpu.SemaphoreType.DMA((12 + chips,)),
        ],
        compiler_params=params(50),
        cost_estimate=cost(2 * short_rows * outer * inner_whole * width, 8 * MIB),
        name="first",
    )(short_len, long_len, x_short, dv_short, x_t, dv_long, master)
    within = end_mask > 0.0
    x_other = swap(theirs, 1)
    from_end = outward(blocks[3])
    weights = [weight, cross(weight, 0), cross(weight, 1)]
    long_own, long_first, long_second, long_far = pl.pallas_call(
        long_kernel,
        out_shape=[block] * 4,
        in_specs=[VMEM] * 4,
        out_specs=[VMEM] * 4,
        compiler_params=params(16),
        cost_estimate=cost(4 * rows * chips * outer * inner * width, 4 * MIB),
        name="long_grad",
    )(x_t, live_dv, x_other, dv_other)

    far_sum = cross(long_far, 1)
    second_sum = cross(long_second, 1)
    middle = outward(after(blocks[2], long_own))
    across_done = plus(after(blocks[2], long_own), from_end)
    across = inward(across_done)
    first_sent = plus(long_first, far_sum)
    first_sum = cross(first_sent, 0)
    inside_sent = plus(after(blocks[3], first_sent), middle)
    inside = inward(inside_sent)
    handed = after(weights[1], inside_sent)
    weights.append(cross(handed, 1))
    across = after(across, handed)
    near_sent = plus(blocks[1], jnp.where(within, across, jnp.zeros_like(across)))
    near = outward(near_sent)

    mine, other = pl.pallas_call(
        values_kernel,
        out_shape=[jax.ShapeDtypeStruct((parts, own_rows, width), t) for t in (F32, BF16)],
        in_specs=[VMEM] * 6,
        out_specs=[VMEM] * 2,
        scratch_shapes=[pltpu.VMEM((rows, width), F32)],
        compiler_params=params(16),
        cost_estimate=cost(4 * rows * chips * outer * inner * width, 6 * MIB),
        name="values",
    )(x_t, x_other, *weights)

    arrived = [after(blocks[0], mine), near, inside, long_own, second_sum, first_sum]
    arrived += [master, moment1, moment2]
    next_shard = pl.pallas_call(
        weight_kernel,
        out_shape=block,
        in_specs=[VMEM] * len(arrived),
        out_specs=VMEM,
        compiler_params=params(16),
        cost_estimate=cost(20 * outer * inner * width, 5 * MIB),
        name="next_weight",
    )(*arrived)

    gathered = [next_shard, cross(next_shard, 0), cross(next_shard, 1)]

    total = mine + swap(after(other, next_shard), 1).astype(F32)
    shares = total.astype(BF16)
    v_across_sent = plus(shares[2], outward(shares[3]))
    v_across = inward(v_across_sent)
    v_middle = outward(after(shares[2], v_across_sent))
    v_near = plus(shares[1], jnp.where(within[0], v_across, jnp.zeros_like(v_across)))
    v_inside = plus(shares[3], v_middle)
    values = total[0] + outward(v_near).astype(F32)
    values = values + jnp.where(within[0], inward(v_inside).astype(F32), 0.0)
    v_long = jnp.where(row_mask > 0.0, values, 0.0).astype(BF16)

    new_state = pl.pallas_call(
        state_kernel,
        out_shape=[jax.ShapeDtypeStruct(master.shape, F32)] * 3,
        in_specs=[VMEM] * len(arrived),
        out_specs=[VMEM] * 3,
        compiler_params=params(16),
        cost_estimate=cost(20 * outer * inner * width, 10 * MIB),
        name="new_state",
    )(after(arrived[0], shares), *arrived[1:])

    far = cross(gathered[1], 1)
    early = list(gathered)
    early = early + [swap(x, 1) for x in early]
    kinds = [(step, core) for core in range(2) for step in range(3)]
    whole_shape = jax.ShapeDtypeStruct((n * outer, inner, width), BF16)
    placed = place(kinds, early, whole_shape, "place_near")
    far = after(far, v_long, new_state[0], *early[3:5])
    next_weight = place([(3, 0), (3, 1)], [far, swap(far, 1)], placed, "place_far")
    return (v_long, *new_state, next_weight)


def solution(mesh):
    placed = (
        P("dp", None, "tensor"),
        P("dp", None),
        P("tensor", "dp", None),
        P("tensor", None),
        P("dp"),
        P("tensor"),
        P("dp", "tensor", None),
        P("dp", "tensor", None),
        P("dp", "tensor", None),
    )
    return jax.shard_map(
        body,
        mesh=mesh,
        in_specs=placed,
        out_specs=(
            P(("dp", "tensor"), None),
            P("dp", "tensor", None),
            P("dp", "tensor", None),
            P("dp", "tensor", None),
            P(None, "tensor", None),
        ),
        check_vma=False,
    )
```

```python
import functools

import jax
import jax.numpy as jnp
from jax import lax
from jax.experimental import pallas as pl
from jax.experimental.pallas import tpu as pltpu
from jax.sharding import PartitionSpec as P

BF16 = jnp.bfloat16
F32 = jnp.float32
MIB = 1 << 20
VMEM = pl.BlockSpec(memory_space=pltpu.VMEM)
SMEM = pl.BlockSpec(memory_space=pltpu.SMEM)
ANY = pl.BlockSpec(memory_space=pl.ANY)
HBM = pl.BlockSpec(memory_space=pltpu.HBM)


def contract_rows(left, right):
    return lax.dot_general(
        left, right, (((0,), (0,)), ((), ())), preferred_element_type=jnp.float32
    )


def adam(master, moment1, moment2, grad):
    new_moment1 = 0.9 * moment1 + 0.1 * grad
    new_moment2 = 0.999 * moment2 + 0.001 * grad * grad
    first_corr = 1.0 - 0.9**10
    second_corr = 1.0 - 0.999**10
    update = new_moment1 / first_corr / (jnp.sqrt(new_moment2 / second_corr) + 1e-08)
    new_master = master - 0.01 * (update + 0.1 * master)
    return new_master, new_moment1, new_moment2


def plain_body(x_long, dv_long, x_short, dv_short, long_len, short_len, master, moment1, moment2):
    weight_shard = master.astype(BF16)
    long_rows, _, inner_part = x_long.shape
    kv_width = master.shape[2]
    short_rows, outer_part, inner_whole = x_short.shape
    piece = lax.all_gather(weight_shard, "dp", axis=0, tiled=True)
    flat_inputs = x_long.reshape(long_rows, piece.shape[0] * inner_part)
    flat_piece = piece.reshape(piece.shape[0] * inner_part, kv_width)
    partial_values = jnp.dot(flat_inputs, flat_piece, preferred_element_type=F32)
    values = lax.psum_scatter(partial_values, "tensor", scatter_dimension=0, tiled=True)
    own_rows = values.shape[0]
    row_start = lax.axis_index("tensor") * own_rows
    own_live = row_start + jnp.arange(own_rows, dtype=jnp.int32) < long_len[0]
    v_long = jnp.where(own_live[:, None], values, 0.0).astype(BF16)
    long_live = jnp.arange(long_rows, dtype=jnp.int32) < long_len[0]
    short_live = jnp.arange(short_rows, dtype=jnp.int32) < short_len[0]
    live_dv_long = jnp.where(long_live[:, None], dv_long, jnp.zeros_like(dv_long))
    live_dv_short = jnp.where(short_live[:, None], dv_short, jnp.zeros_like(dv_short))
    count = lax.axis_size("dp") * master.shape[0]
    grad_long = lax.psum_scatter(
        contract_rows(flat_inputs, live_dv_long).reshape(count, inner_part, kv_width),
        "dp",
        scatter_dimension=0,
        tiled=True,
    )
    flat_inputs = x_short.reshape(short_rows, outer_part * inner_whole)
    product = contract_rows(flat_inputs, live_dv_short).reshape(outer_part, inner_whole, kv_width)
    grad_short = lax.psum_scatter(product, "tensor", scatter_dimension=1, tiled=True)
    new_master, new_moment1, new_moment2 = adam(master, moment1, moment2, grad_long + grad_short)
    next_weight = lax.all_gather(new_master.astype(BF16), "dp", axis=0, tiled=True)
    return (v_long, new_master, new_moment1, new_moment2, next_weight)


def first_kernel(slen_ref, llen_ref, xs_hbm, dvs_hbm, xl_hbm, *refs):
    end_block, theirs, turned, live_dv, xs_ref, dvs_ref, xl_ref, wide, sems = refs
    rows, outer, inner = xs_ref.shape
    chips, owned, _, long_rows = theirs.shape
    chunks = 4
    chunk = rows // chunks
    part = inner // 4
    z = lax.axis_index("tensor")
    other = 1 - lax.rem(lax.axis_index("dp"), 2)
    pairs = []
    for c in range(chunks):
        span = pl.ds(c * chunk, chunk)
        pairs.append((xs_hbm.at[span], xs_ref.at[span]))
        pairs.append((dvs_hbm.at[span], dvs_ref.at[span]))
    for c in range(chips):
        pairs.append((xl_hbm.at[pl.ds((2 * c + other) * owned, owned)], xl_ref.at[c]))
    copies = [pltpu.make_async_copy(*pair, sems.at[i]) for i, pair in enumerate(pairs)]
    for copy in copies:
        copy.start()
    for c in range(chunks):
        copies[2 * c].wait()
        copies[2 * c + 1].wait()
        span = slice(c * chunk, (c + 1) * chunk)
        wide[...] = xs_ref[span].reshape(chunk * outer, inner).astype(F32)
        for a in range(outer):
            xa = wide[pl.ds(a, chunk, outer), :].astype(BF16).T
            for j in range(4):
                turned[j, a * part : (a + 1) * part, span] = xa[j * part : (j + 1) * part]
        dv = dvs_ref[span]
        row = lax.broadcasted_iota(jnp.int32, dv.shape, 0) + c * chunk
        live_dv[span] = jnp.where(row < slen_ref[0], dv, jnp.zeros_like(dv))
    end_block[...] = short_block(3, turned, live_dv).reshape(end_block.shape).astype(BF16)
    for c in range(chips):
        copies[2 * chunks + c].wait()
        x = xl_ref[c]
        row = lax.broadcasted_iota(jnp.int32, x.shape, 2)
        theirs[c] = jnp.where(row < llen_ref[0], x, jnp.zeros_like(x))


def short_block(k, turned, live_dv):
    x = turned[lax.bitwise_xor(lax.axis_index("tensor"), jnp.int32(k))]
    return jnp.dot(x, live_dv[...], preferred_element_type=F32)


def second_kernel(llen_ref, turned, live_dvs, dvl_ref, master_ref, *outs):
    blocks, (live_dv, weight, inside, live_rows) = outs[:3], outs[3:]
    for k in (2, 1, 0):
        blocks[k][...] = short_block(k, turned, live_dvs).reshape(blocks[k].shape).astype(BF16)
    long_len = llen_ref[0]
    dv = dvl_ref[...]
    row = lax.broadcasted_iota(jnp.int32, dv.shape, 0)
    live_dv[...] = jnp.where(row < long_len, dv, jnp.zeros_like(dv))
    weight[...] = master_ref[...].astype(BF16)
    inside[...] = jnp.full(inside.shape, jnp.where(interior(), 1.0, 0.0), F32)
    row = lax.broadcasted_iota(jnp.int32, live_rows.shape, 0)
    row = row + lax.axis_index("tensor") * live_rows.shape[0]
    live_rows[...] = jnp.where(row < long_len, 1.0, 0.0)


def plane_steps():
    core = lax.rem(lax.axis_index("dp"), 2)
    return 0, 1 + core, 2 - core, 3


def long_kernel(x_ref, dv_ref, xs_ref, dvs_ref, *outs):
    chips, outer, inner, rows = xs_ref.shape
    me = lax.axis_index("dp")
    chip, core = me // 2, lax.rem(me, 2)
    for out, rel in reversed(list(zip(outs, plane_steps()))):
        j = lax.bitwise_xor(chip, jnp.int32(rel))
        mine = x_ref[pl.ds((2 * j + core) * outer, outer)].reshape(outer * inner, rows)
        other = xs_ref[j].reshape(outer * inner, rows)
        prod = jnp.dot(mine, dv_ref[...], preferred_element_type=F32)
        prod = prod + jnp.dot(other, dvs_ref[...], preferred_element_type=F32)
        out[...] = prod.reshape(outer, inner, prod.shape[-1]).astype(BF16)


def values_kernel(x_ref, xs_ref, *refs):
    weights, mine_ref, other_ref, acc = refs[:4], refs[-3], refs[-2], refs[-1]
    _, outer, inner, rows = xs_ref.shape
    parts, part, width = mine_ref.shape
    me = lax.axis_index("dp")
    z = lax.axis_index("tensor")
    chip, core = me // 2, lax.rem(me, 2)
    for which, out in ((0, mine_ref), (1, other_ref)):
        total = None
        for weight, rel in zip(weights, plane_steps()):
            j = lax.bitwise_xor(chip, jnp.int32(rel))
            x = xs_ref[j] if which else x_ref[pl.ds((2 * j + core) * outer, outer)]
            w = weight[...].reshape(outer * inner, width)
            term = contract_rows(x.reshape(outer * inner, rows), w)
            total = term if total is None else total + term
        acc[...] = total
        for k in range(parts):
            j = lax.bitwise_xor(z, jnp.int32(k))
            out[k] = acc[pl.ds(pl.multiple_of(j * part, part), part), :].astype(out.dtype)


def update(refs):
    own, near, inside, *terms, master, moment1, moment2 = refs
    grad = own[...].astype(F32) + near[...].astype(F32)
    grad = grad + jnp.where(interior(), inside[...].astype(F32), 0.0)
    for t in terms:
        grad = grad + t[...].astype(F32)
    return adam(master[...], moment1[...], moment2[...], grad)


def weight_kernel(*refs):
    refs[-1][...] = update(refs[:-1])[0].astype(BF16)


def state_kernel(*refs):
    for out, value in zip(refs[-3:], update(refs[:-3])):
        out[...] = value


def place_kernel(kinds, n, outer, *refs):
    pieces, out, sems = refs[:n], refs[-2], refs[-1]
    me = lax.axis_index("dp")
    steps = plane_steps()
    copies = []
    for s, (i, start, step, core) in enumerate(kinds):
        if core and step in (1, 2):
            step = 3 - step
        owner = lax.bitwise_xor(me, 2 * jnp.int32(steps[step]) + core)
        source = pieces[i].at[pl.ds(start, outer)]
        target = out.at[pl.ds(owner * outer, outer)]
        copies.append(pltpu.make_async_copy(source, target, sems.at[s]))
    for copy in copies:
        copy.start()
    for copy in copies:
        copy.wait()


def place(kinds, pieces, outer, whole, name):
    new = isinstance(whole, jax.ShapeDtypeStruct)
    return pl.pallas_call(
        functools.partial(place_kernel, kinds, len(pieces), outer),
        out_shape=jax.ShapeDtypeStruct(whole.shape, whole.dtype),
        in_specs=[VMEM] * len(pieces) + [ANY] * (not new),
        out_specs=ANY,
        scratch_shapes=[pltpu.SemaphoreType.DMA((len(kinds),))],
        input_output_aliases={} if new else {len(pieces): 0},
        compiler_params=params(16),
        cost_estimate=cost(0, 2 * sum(p.size for p in pieces)),
        name=name,
    )(*pieces, *([] if new else [whole]))


def params(mib):
    return pltpu.CompilerParams(vmem_limit_bytes=mib * MIB)


def cost(flops, moved):
    return pl.CostEstimate(flops=flops, bytes_accessed=moved, transcendentals=0)


def swap(x, bit):
    n = lax.axis_size("dp")
    return lax.ppermute(x, "dp", [(i, i ^ bit) for i in range(n)])


def cross(x, turn):
    n = lax.axis_size("dp")
    return lax.ppermute(x, "dp", [(i, i ^ (2 << ((i & 1) ^ turn))) for i in range(n)])


def interior():
    z = lax.axis_index("tensor")
    return (z > 0) & (z < lax.axis_size("tensor") - 1)


def outward(x):
    return lax.ppermute(x, "tensor", [(i, i ^ 1) for i in range(lax.axis_size("tensor"))])


def inward(x):
    n, m = lax.axis_size("tensor"), lax.axis_size("dp")
    pairs = []
    for d in range(m):
        for i in range(n):
            to = (d, i ^ 3) if 0 < i < n - 1 else (d ^ 1, i)
            pairs.append((d * n + i, to[0] * n + to[1]))
    return lax.ppermute(x, ("dp", "tensor"), pairs)


def after(x, *earlier):
    return lax.optimization_barrier((x, *earlier))[0]


def plus(a, b):
    return (a.astype(F32) + b.astype(F32)).astype(BF16)


def body(x_long, dv_long, x_short, dv_short, long_len, short_len, master, moment1, moment2):
    n = lax.axis_size("dp")
    parts = lax.axis_size("tensor")
    outer, inner, width = master.shape
    rows = x_long.shape[0]
    short_rows, _, inner_whole = x_short.shape
    chips = n // 2
    own_rows = rows // parts
    aligned = (
        n & (n - 1) == 0
        and chips == 4
        and parts == 4
        and short_rows % 512 == 0
        and inner % 16 == 0
        and own_rows % 16 == 0
        and rows % 128 == 0
        and short_rows % 128 == 0
        and inner_whole % 128 == 0
        and width % 128 == 0
    )
    if not aligned:
        return plain_body(
            x_long, dv_long, x_short, dv_short, long_len, short_len, master, moment1, moment2
        )
    x_t = jnp.transpose(x_long, (1, 2, 0))
    dv_other = swap(dv_long, 1)
    block = jax.ShapeDtypeStruct((outer, inner, width), BF16)
    end_block, theirs, turned, live_dvs = pl.pallas_call(
        first_kernel,
        out_shape=[
            block,
            jax.ShapeDtypeStruct((chips, outer, inner, rows), BF16),
            jax.ShapeDtypeStruct((4, outer * inner, short_rows), BF16),
            jax.ShapeDtypeStruct(dv_short.shape, BF16),
        ],
        in_specs=[SMEM, SMEM] + [HBM] * 3,
        out_specs=[VMEM] * 4,
        scratch_shapes=[
            pltpu.VMEM(x_short.shape, BF16),
            pltpu.VMEM(dv_short.shape, BF16),
            pltpu.VMEM((chips, outer, inner, rows), BF16),
            pltpu.VMEM((short_rows // 4 * outer, inner_whole), F32),
            pltpu.SemaphoreType.DMA((8 + chips,)),
        ],
        compiler_params=params(50),
        cost_estimate=cost(short_rows * outer * inner_whole * width, 6 * MIB),
        name="first",
    )(short_len, long_len, x_short, dv_short, x_t)
    *blocks, live_dv, weight, end_mask, row_mask = pl.pallas_call(
        second_kernel,
        out_shape=[
            *[block] * 3,
            jax.ShapeDtypeStruct(dv_long.shape, BF16),
            block,
            jax.ShapeDtypeStruct((1, 1, width), F32),
            jax.ShapeDtypeStruct((own_rows, width), F32),
        ],
        in_specs=[SMEM] + [VMEM] * 4,
        out_specs=[VMEM] * 7,
        compiler_params=params(16),
        cost_estimate=cost(short_rows * outer * inner_whole * width, 6 * MIB),
        name="second",
    )(long_len, turned, live_dvs, dv_long, master)
    blocks.append(end_block)
    within = end_mask > 0.0
    x_other = swap(theirs, 1)
    from_end = outward(blocks[3])
    weight = after(weight, x_other)
    weights = [weight, cross(weight, 0), cross(weight, 1)]
    long_own, long_first, long_second, long_far = pl.pallas_call(
        long_kernel,
        out_shape=[block] * 4,
        in_specs=[VMEM] * 4,
        out_specs=[VMEM] * 4,
        compiler_params=params(16),
        cost_estimate=cost(4 * rows * chips * outer * inner * width, 4 * MIB),
        name="long_grad",
    )(x_t, live_dv, x_other, dv_other)

    far_sum = cross(long_far, 1)
    second_sum = cross(long_second, 1)
    middle = outward(after(blocks[2], long_own))
    across_done = plus(after(blocks[2], long_own), from_end)
    across = inward(across_done)
    first_sent = plus(long_first, far_sum)
    first_sum = cross(first_sent, 0)
    inside_sent = plus(after(blocks[3], first_sent), middle)
    inside = inward(inside_sent)
    handed = after(weights[1], inside_sent)
    weights.append(cross(handed, 1))
    across = after(across, handed)
    near_sent = plus(blocks[1], jnp.where(within, across, jnp.zeros_like(across)))
    near = outward(near_sent)

    mine, other = pl.pallas_call(
        values_kernel,
        out_shape=[jax.ShapeDtypeStruct((parts, own_rows, width), t) for t in (F32, BF16)],
        in_specs=[VMEM] * 6,
        out_specs=[VMEM] * 2,
        scratch_shapes=[pltpu.VMEM((rows, width), F32)],
        compiler_params=params(16),
        cost_estimate=cost(4 * rows * chips * outer * inner * width, 6 * MIB),
        name="values",
    )(x_t, x_other, *weights)

    arrived = [after(blocks[0], mine), near, inside, long_own, second_sum, first_sum]
    arrived += [master, moment1, moment2]
    next_shard = pl.pallas_call(
        weight_kernel,
        out_shape=block,
        in_specs=[VMEM] * len(arrived),
        out_specs=VMEM,
        compiler_params=params(16),
        cost_estimate=cost(20 * outer * inner * width, 5 * MIB),
        name="next_weight",
    )(*arrived)

    gathered = [next_shard, cross(next_shard, 0), cross(next_shard, 1)]

    total = mine + swap(after(other, next_shard), 1).astype(F32)
    shares = total.astype(BF16)
    v_across_sent = plus(shares[2], outward(shares[3]))
    v_across = inward(v_across_sent)
    v_middle = outward(after(shares[2], v_across_sent))
    v_near = plus(shares[1], jnp.where(within[0], v_across, jnp.zeros_like(v_across)))
    v_inside = plus(shares[3], v_middle)
    values = total[0] + outward(v_near).astype(F32)
    values = values + jnp.where(within[0], inward(v_inside).astype(F32), 0.0)
    v_long = jnp.where(row_mask > 0.0, values, 0.0).astype(BF16)

    new_state = pl.pallas_call(
        state_kernel,
        out_shape=[jax.ShapeDtypeStruct(master.shape, F32)] * 3,
        in_specs=[VMEM] * len(arrived),
        out_specs=[VMEM] * 3,
        compiler_params=params(16),
        cost_estimate=cost(20 * outer * inner * width, 10 * MIB),
        name="new_state",
    )(after(arrived[0], shares), *arrived[1:])

    far = cross(gathered[1], 1)
    two = jnp.concatenate([next_shard, gathered[1]])
    late = [swap(after(two, new_state[0]), 1), swap(after(gathered[2], new_state[0]), 1)]
    early = [*gathered, *late]
    kinds = [(0, 0, 0, 0), (1, 0, 1, 0), (2, 0, 2, 0), (3, 0, 0, 1), (3, outer, 1, 1), (4, 0, 2, 1)]
    whole_shape = jax.ShapeDtypeStruct((n * outer, inner, width), BF16)
    placed = place(kinds, early, outer, whole_shape, "place_near")
    far = after(far, v_long, new_state[0])
    next_weight = place([(0, 0, 3, 0), (1, 0, 3, 1)], [far, swap(far, 1)], outer, placed, "place_far")
    return (v_long, *new_state, next_weight)


def solution(mesh):
    placed = (
        P("dp", None, "tensor"),
        P("dp", None),
        P("tensor", "dp", None),
        P("tensor", None),
        P("dp"),
        P("tensor"),
        P("dp", "tensor", None),
        P("dp", "tensor", None),
        P("dp", "tensor", None),
    )
    return jax.shard_map(
        body,
        mesh=mesh,
        in_specs=placed,
        out_specs=(
            P(("dp", "tensor"), None),
            P("dp", "tensor", None),
            P("dp", "tensor", None),
            P("dp", "tensor", None),
            P(None, "tensor", None),
        ),
        check_vma=False,
    )
```

```python
import functools

import jax
import jax.numpy as jnp
from jax import lax
from jax.experimental import pallas as pl
from jax.experimental.pallas import tpu as pltpu
from jax.sharding import PartitionSpec as P

BF16 = jnp.bfloat16
F32 = jnp.float32
MIB = 1 << 20
VMEM = pl.BlockSpec(memory_space=pltpu.VMEM)
SMEM = pl.BlockSpec(memory_space=pltpu.SMEM)
ANY = pl.BlockSpec(memory_space=pl.ANY)
HBM = pl.BlockSpec(memory_space=pltpu.HBM)


def contract_rows(left, right):
    return lax.dot_general(
        left, right, (((0,), (0,)), ((), ())), preferred_element_type=jnp.float32
    )


def adam(master, moment1, moment2, grad):
    new_moment1 = 0.9 * moment1 + 0.1 * grad
    new_moment2 = 0.999 * moment2 + 0.001 * grad * grad
    first_corr = 1.0 - 0.9**10
    second_corr = 1.0 - 0.999**10
    update = new_moment1 / first_corr / (jnp.sqrt(new_moment2 / second_corr) + 1e-08)
    new_master = master - 0.01 * (update + 0.1 * master)
    return new_master, new_moment1, new_moment2


def plain_body(x_long, dv_long, x_short, dv_short, long_len, short_len, master, moment1, moment2):
    weight_shard = master.astype(BF16)
    long_rows, _, inner_part = x_long.shape
    kv_width = master.shape[2]
    short_rows, outer_part, inner_whole = x_short.shape
    piece = lax.all_gather(weight_shard, "dp", axis=0, tiled=True)
    flat_inputs = x_long.reshape(long_rows, piece.shape[0] * inner_part)
    flat_piece = piece.reshape(piece.shape[0] * inner_part, kv_width)
    partial_values = jnp.dot(flat_inputs, flat_piece, preferred_element_type=F32)
    values = lax.psum_scatter(partial_values, "tensor", scatter_dimension=0, tiled=True)
    own_rows = values.shape[0]
    row_start = lax.axis_index("tensor") * own_rows
    own_live = row_start + jnp.arange(own_rows, dtype=jnp.int32) < long_len[0]
    v_long = jnp.where(own_live[:, None], values, 0.0).astype(BF16)
    long_live = jnp.arange(long_rows, dtype=jnp.int32) < long_len[0]
    short_live = jnp.arange(short_rows, dtype=jnp.int32) < short_len[0]
    live_dv_long = jnp.where(long_live[:, None], dv_long, jnp.zeros_like(dv_long))
    live_dv_short = jnp.where(short_live[:, None], dv_short, jnp.zeros_like(dv_short))
    count = lax.axis_size("dp") * master.shape[0]
    grad_long = lax.psum_scatter(
        contract_rows(flat_inputs, live_dv_long).reshape(count, inner_part, kv_width),
        "dp",
        scatter_dimension=0,
        tiled=True,
    )
    flat_inputs = x_short.reshape(short_rows, outer_part * inner_whole)
    product = contract_rows(flat_inputs, live_dv_short).reshape(outer_part, inner_whole, kv_width)
    grad_short = lax.psum_scatter(product, "tensor", scatter_dimension=1, tiled=True)
    new_master, new_moment1, new_moment2 = adam(master, moment1, moment2, grad_long + grad_short)
    next_weight = lax.all_gather(new_master.astype(BF16), "dp", axis=0, tiled=True)
    return (v_long, new_master, new_moment1, new_moment2, next_weight)


def first_kernel(slen_ref, llen_ref, xs_hbm, dvs_hbm, xl_hbm, dvl_hbm, master_hbm, *refs):
    end_block, mid_block, turned, live_dv, theirs, live_dvl, weight, inside, live_rows = refs[:9]
    xs_ref, dvs_ref, xl_ref, dvl_ref, master_ref, wide, sems = refs[9:]
    rows, outer, inner = xs_ref.shape
    chips, owned, _, long_rows = theirs.shape
    chunks = 4
    chunk = rows // chunks
    part = inner // 4
    z = lax.axis_index("tensor")
    other = 1 - lax.rem(lax.axis_index("dp"), 2)
    pairs = []
    for c in range(chunks):
        span = pl.ds(c * chunk, chunk)
        pairs.append((xs_hbm.at[span], xs_ref.at[span]))
        pairs.append((dvs_hbm.at[span], dvs_ref.at[span]))
    for c in range(chips):
        pairs.append((xl_hbm.at[pl.ds((2 * c + other) * owned, owned)], xl_ref.at[c]))
    pairs.append((dvl_hbm, dvl_ref))
    pairs.append((master_hbm, master_ref))
    copies = [pltpu.make_async_copy(*pair, sems.at[i]) for i, pair in enumerate(pairs)]
    for copy in copies:
        copy.start()
    for c in range(chunks):
        copies[2 * c].wait()
        copies[2 * c + 1].wait()
        span = slice(c * chunk, (c + 1) * chunk)
        wide[...] = xs_ref[span].reshape(chunk * outer, inner).astype(F32)
        for a in range(outer):
            xa = wide[pl.ds(a, chunk, outer), :].astype(BF16).T
            for j in range(4):
                turned[j, a * part : (a + 1) * part, span] = xa[j * part : (j + 1) * part]
        dv = dvs_ref[span]
        row = lax.broadcasted_iota(jnp.int32, dv.shape, 0) + c * chunk
        live_dv[span] = jnp.where(row < slen_ref[0], dv, jnp.zeros_like(dv))
    for k, out in ((3, end_block), (2, mid_block)):
        out[...] = short_block(k, turned, live_dv).reshape(out.shape).astype(BF16)
    for c in range(chips):
        copies[2 * chunks + c].wait()
        x = xl_ref[c]
        row = lax.broadcasted_iota(jnp.int32, x.shape, 2)
        theirs[c] = jnp.where(row < llen_ref[0], x, jnp.zeros_like(x))
    copies[-2].wait()
    dv = dvl_ref[...]
    row = lax.broadcasted_iota(jnp.int32, dv.shape, 0)
    live_dvl[...] = jnp.where(row < llen_ref[0], dv, jnp.zeros_like(dv))
    copies[-1].wait()
    weight[...] = master_ref[...].astype(BF16)
    inside[...] = jnp.full(inside.shape, jnp.where(interior(), 1.0, 0.0), F32)
    row = lax.broadcasted_iota(jnp.int32, live_rows.shape, 0) + z * live_rows.shape[0]
    live_rows[...] = jnp.where(row < llen_ref[0], 1.0, 0.0)


def short_block(k, turned, live_dv):
    x = turned[lax.bitwise_xor(lax.axis_index("tensor"), jnp.int32(k))]
    return jnp.dot(x, live_dv[...], preferred_element_type=F32)


def second_kernel(turned, live_dv, *blocks):
    for k in (1, 0):
        blocks[k][...] = short_block(k, turned, live_dv).reshape(blocks[k].shape).astype(BF16)


def plane_steps():
    core = lax.rem(lax.axis_index("dp"), 2)
    return 0, 1 + core, 2 - core, 3


def long_kernel(x_ref, dv_ref, xs_ref, dvs_ref, *outs):
    chips, outer, inner, rows = xs_ref.shape
    me = lax.axis_index("dp")
    chip, core = me // 2, lax.rem(me, 2)
    for out, rel in reversed(list(zip(outs, plane_steps()))):
        j = lax.bitwise_xor(chip, jnp.int32(rel))
        mine = x_ref[pl.ds((2 * j + core) * outer, outer)].reshape(outer * inner, rows)
        other = xs_ref[j].reshape(outer * inner, rows)
        prod = jnp.dot(mine, dv_ref[...], preferred_element_type=F32)
        prod = prod + jnp.dot(other, dvs_ref[...], preferred_element_type=F32)
        out[...] = prod.reshape(outer, inner, prod.shape[-1]).astype(BF16)


def values_kernel(x_ref, xs_ref, *refs):
    weights, mine_ref, other_ref, acc = refs[:4], refs[-3], refs[-2], refs[-1]
    _, outer, inner, rows = xs_ref.shape
    parts, part, width = mine_ref.shape
    me = lax.axis_index("dp")
    z = lax.axis_index("tensor")
    chip, core = me // 2, lax.rem(me, 2)
    for which, out in ((0, mine_ref), (1, other_ref)):
        total = None
        for weight, rel in zip(weights, plane_steps()):
            j = lax.bitwise_xor(chip, jnp.int32(rel))
            x = xs_ref[j] if which else x_ref[pl.ds((2 * j + core) * outer, outer)]
            w = weight[...].reshape(outer * inner, width)
            term = contract_rows(x.reshape(outer * inner, rows), w)
            total = term if total is None else total + term
        acc[...] = total
        for k in range(parts):
            j = lax.bitwise_xor(z, jnp.int32(k))
            out[k] = acc[pl.ds(pl.multiple_of(j * part, part), part), :].astype(out.dtype)


def update(refs):
    own, near, inside, *terms, master, moment1, moment2 = refs
    grad = own[...].astype(F32) + near[...].astype(F32)
    grad = grad + jnp.where(interior(), inside[...].astype(F32), 0.0)
    for t in terms:
        grad = grad + t[...].astype(F32)
    return adam(master[...], moment1[...], moment2[...], grad)


def weight_kernel(*refs):
    refs[-1][...] = update(refs[:-1])[0].astype(BF16)


def state_kernel(*refs):
    for out, value in zip(refs[-3:], update(refs[:-3])):
        out[...] = value


def place_kernel(kinds, n, outer, *refs):
    pieces, out, sems = refs[:n], refs[-2], refs[-1]
    me = lax.axis_index("dp")
    steps = plane_steps()
    copies = []
    for s, (i, start, step, core) in enumerate(kinds):
        if core and step in (1, 2):
            step = 3 - step
        owner = lax.bitwise_xor(me, 2 * jnp.int32(steps[step]) + core)
        source = pieces[i].at[pl.ds(start, outer)]
        target = out.at[pl.ds(owner * outer, outer)]
        copies.append(pltpu.make_async_copy(source, target, sems.at[s]))
    for copy in copies:
        copy.start()
    for copy in copies:
        copy.wait()


def place(kinds, pieces, outer, whole, name):
    new = isinstance(whole, jax.ShapeDtypeStruct)
    return pl.pallas_call(
        functools.partial(place_kernel, kinds, len(pieces), outer),
        out_shape=jax.ShapeDtypeStruct(whole.shape, whole.dtype),
        in_specs=[VMEM] * len(pieces) + [ANY] * (not new),
        out_specs=ANY,
        scratch_shapes=[pltpu.SemaphoreType.DMA((len(kinds),))],
        input_output_aliases={} if new else {len(pieces): 0},
        compiler_params=params(16),
        cost_estimate=cost(0, 2 * sum(p.size for p in pieces)),
        name=name,
    )(*pieces, *([] if new else [whole]))


def params(mib):
    return pltpu.CompilerParams(vmem_limit_bytes=mib * MIB)


def cost(flops, moved):
    return pl.CostEstimate(flops=flops, bytes_accessed=moved, transcendentals=0)


def swap(x, bit):
    n = lax.axis_size("dp")
    return lax.ppermute(x, "dp", [(i, i ^ bit) for i in range(n)])


def cross(x, turn):
    n = lax.axis_size("dp")
    return lax.ppermute(x, "dp", [(i, i ^ (2 << ((i & 1) ^ turn))) for i in range(n)])


def interior():
    z = lax.axis_index("tensor")
    return (z > 0) & (z < lax.axis_size("tensor") - 1)


def outward(x):
    return lax.ppermute(x, "tensor", [(i, i ^ 1) for i in range(lax.axis_size("tensor"))])


def inward(x):
    n, m = lax.axis_size("tensor"), lax.axis_size("dp")
    pairs = []
    for d in range(m):
        for i in range(n):
            to = (d, i ^ 3) if 0 < i < n - 1 else (d ^ 1, i)
            pairs.append((d * n + i, to[0] * n + to[1]))
    return lax.ppermute(x, ("dp", "tensor"), pairs)


def after(x, *earlier):
    return lax.optimization_barrier((x, *earlier))[0]


def plus(a, b):
    return (a.astype(F32) + b.astype(F32)).astype(BF16)


def body(x_long, dv_long, x_short, dv_short, long_len, short_len, master, moment1, moment2):
    n = lax.axis_size("dp")
    parts = lax.axis_size("tensor")
    outer, inner, width = master.shape
    rows = x_long.shape[0]
    short_rows, _, inner_whole = x_short.shape
    chips = n // 2
    own_rows = rows // parts
    aligned = (
        n & (n - 1) == 0
        and chips == 4
        and parts == 4
        and short_rows % 512 == 0
        and inner % 16 == 0
        and own_rows % 16 == 0
        and rows % 128 == 0
        and short_rows % 128 == 0
        and inner_whole % 128 == 0
        and width % 128 == 0
    )
    if not aligned:
        return plain_body(
            x_long, dv_long, x_short, dv_short, long_len, short_len, master, moment1, moment2
        )
    x_t = jnp.transpose(x_long, (1, 2, 0))
    dv_other = swap(dv_long, 1)
    block = jax.ShapeDtypeStruct((outer, inner, width), BF16)
    end_block, mid_block, turned, live_dvs, theirs, live_dv, weight, end_mask, row_mask = pl.pallas_call(
        first_kernel,
        out_shape=[
            block,
            block,
            jax.ShapeDtypeStruct((4, outer * inner, short_rows), BF16),
            jax.ShapeDtypeStruct(dv_short.shape, BF16),
            jax.ShapeDtypeStruct((chips, outer, inner, rows), BF16),
            jax.ShapeDtypeStruct(dv_long.shape, BF16),
            block,
            jax.ShapeDtypeStruct((1, 1, width), F32),
            jax.ShapeDtypeStruct((own_rows, width), F32),
        ],
        in_specs=[SMEM, SMEM] + [HBM] * 5,
        out_specs=[VMEM] * 9,
        scratch_shapes=[
            pltpu.VMEM(x_short.shape, BF16),
            pltpu.VMEM(dv_short.shape, BF16),
            pltpu.VMEM((chips, outer, inner, rows), BF16),
            pltpu.VMEM(dv_long.shape, BF16),
            pltpu.VMEM(master.shape, F32),
            pltpu.VMEM((short_rows // 4 * outer, inner_whole), F32),
            pltpu.SemaphoreType.DMA((10 + chips,)),
        ],
        compiler_params=params(50),
        cost_estimate=cost(short_rows * outer * inner_whole * width, 8 * MIB),
        name="first",
    )(short_len, long_len, x_short, dv_short, x_t, dv_long, master)
    blocks = pl.pallas_call(
        second_kernel,
        out_shape=[block] * 2,
        in_specs=[VMEM] * 2,
        out_specs=[VMEM] * 2,
        compiler_params=params(16),
        cost_estimate=cost(short_rows * outer * inner_whole * width, 4 * MIB),
        name="second",
    )(turned, live_dvs)
    blocks = [*blocks, mid_block, end_block]
    within = end_mask > 0.0
    x_other = swap(theirs, 1)
    from_end = outward(blocks[3])
    second_weight, first_weight = cross(weight, 1), cross(weight, 0)
    long_own, long_first, long_second, long_far = pl.pallas_call(
        long_kernel,
        out_shape=[block] * 4,
        in_specs=[VMEM] * 4,
        out_specs=[VMEM] * 4,
        compiler_params=params(16),
        cost_estimate=cost(4 * rows * chips * outer * inner * width, 4 * MIB),
        name="long_grad",
    )(x_t, live_dv, x_other, dv_other)

    far_sum = cross(long_far, 1)
    second_sum = cross(long_second, 1)
    middle = outward(after(blocks[2], long_own))
    across_sent = plus(after(blocks[2], long_own), from_end)
    across = inward(across_sent)
    first_sent = plus(long_first, far_sum)
    first_sum = cross(first_sent, 0)
    handed = after(second_weight, first_weight, first_sent)
    far_weight = cross(handed, 0)
    inside_sent = plus(after(blocks[3], handed), middle)
    inside = inward(inside_sent)
    across = after(across, inside_sent)
    near_sent = plus(blocks[1], jnp.where(within, across, jnp.zeros_like(across)))
    near = outward(near_sent)

    mine, other = pl.pallas_call(
        values_kernel,
        out_shape=[jax.ShapeDtypeStruct((parts, own_rows, width), t) for t in (F32, BF16)],
        in_specs=[VMEM] * 6,
        out_specs=[VMEM] * 2,
        scratch_shapes=[pltpu.VMEM((rows, width), F32)],
        compiler_params=params(16),
        cost_estimate=cost(4 * rows * chips * outer * inner * width, 6 * MIB),
        name="values",
    )(x_t, x_other, weight, first_weight, second_weight, far_weight)

    arrived = [after(blocks[0], mine), near, inside, long_own, second_sum, first_sum]
    arrived += [master, moment1, moment2]
    next_shard = pl.pallas_call(
        weight_kernel,
        out_shape=block,
        in_specs=[VMEM] * len(arrived),
        out_specs=VMEM,
        compiler_params=params(16),
        cost_estimate=cost(20 * outer * inner * width, 5 * MIB),
        name="next_weight",
    )(*arrived)

    gathered = [next_shard, cross(next_shard, 0), cross(next_shard, 1)]

    total = mine + after(swap(other, 1), next_shard).astype(F32)
    shares = total.astype(BF16)
    v_across_sent = plus(shares[2], outward(shares[3]))
    v_across = inward(v_across_sent)
    v_middle = outward(after(shares[2], v_across_sent))
    v_near = plus(shares[1], jnp.where(within[0], v_across, jnp.zeros_like(v_across)))
    v_inside = plus(shares[3], v_middle)
    values = total[0] + outward(v_near).astype(F32)
    values = values + jnp.where(within[0], inward(v_inside).astype(F32), 0.0)
    v_long = jnp.where(row_mask > 0.0, values, 0.0).astype(BF16)

    new_state = pl.pallas_call(
        state_kernel,
        out_shape=[jax.ShapeDtypeStruct(master.shape, F32)] * 3,
        in_specs=[VMEM] * len(arrived),
        out_specs=[VMEM] * 3,
        compiler_params=params(16),
        cost_estimate=cost(20 * outer * inner * width, 10 * MIB),
        name="new_state",
    )(after(arrived[0], shares), *arrived[1:])

    far = cross(gathered[1], 1)
    two = jnp.concatenate([next_shard, gathered[1]])
    late = [swap(after(two, new_state[0]), 1), swap(after(gathered[2], new_state[0]), 1)]
    early = [*gathered, *late]
    kinds = [(0, 0, 0, 0), (1, 0, 1, 0), (2, 0, 2, 0), (3, 0, 0, 1), (3, outer, 1, 1), (4, 0, 2, 1)]
    whole_shape = jax.ShapeDtypeStruct((n * outer, inner, width), BF16)
    placed = place(kinds, early, outer, whole_shape, "place_near")
    far = after(far, v_long, new_state[0])
    next_weight = place([(0, 0, 3, 0), (1, 0, 3, 1)], [far, swap(far, 1)], outer, placed, "place_far")
    return (v_long, *new_state, next_weight)


def solution(mesh):
    placed = (
        P("dp", None, "tensor"),
        P("dp", None),
        P("tensor", "dp", None),
        P("tensor", None),
        P("dp"),
        P("tensor"),
        P("dp", "tensor", None),
        P("dp", "tensor", None),
        P("dp", "tensor", None),
    )
    return jax.shard_map(
        body,
        mesh=mesh,
        in_specs=placed,
        out_specs=(
            P(("dp", "tensor"), None),
            P("dp", "tensor", None),
            P("dp", "tensor", None),
            P("dp", "tensor", None),
            P(None, "tensor", None),
        ),
        check_vma=False,
    )
```

```python
import functools

import jax
import jax.numpy as jnp
from jax import lax
from jax.experimental import pallas as pl
from jax.experimental.pallas import tpu as pltpu
from jax.sharding import PartitionSpec as P

BF16 = jnp.bfloat16
F32 = jnp.float32
MIB = 1 << 20
VMEM = pl.BlockSpec(memory_space=pltpu.VMEM)
SMEM = pl.BlockSpec(memory_space=pltpu.SMEM)
ANY = pl.BlockSpec(memory_space=pl.ANY)
HBM = pl.BlockSpec(memory_space=pltpu.HBM)


def contract_rows(left, right):
    return lax.dot_general(
        left, right, (((0,), (0,)), ((), ())), preferred_element_type=jnp.float32
    )


def adam(master, moment1, moment2, grad):
    new_moment1 = 0.9 * moment1 + 0.1 * grad
    new_moment2 = 0.999 * moment2 + 0.001 * grad * grad
    first_corr = 1.0 - 0.9**10
    second_corr = 1.0 - 0.999**10
    update = new_moment1 / first_corr / (jnp.sqrt(new_moment2 / second_corr) + 1e-08)
    new_master = master - 0.01 * (update + 0.1 * master)
    return new_master, new_moment1, new_moment2


def plain_body(x_long, dv_long, x_short, dv_short, long_len, short_len, master, moment1, moment2):
    weight_shard = master.astype(BF16)
    long_rows, _, inner_part = x_long.shape
    kv_width = master.shape[2]
    short_rows, outer_part, inner_whole = x_short.shape
    piece = lax.all_gather(weight_shard, "dp", axis=0, tiled=True)
    flat_inputs = x_long.reshape(long_rows, piece.shape[0] * inner_part)
    flat_piece = piece.reshape(piece.shape[0] * inner_part, kv_width)
    partial_values = jnp.dot(flat_inputs, flat_piece, preferred_element_type=F32)
    values = lax.psum_scatter(partial_values, "tensor", scatter_dimension=0, tiled=True)
    own_rows = values.shape[0]
    row_start = lax.axis_index("tensor") * own_rows
    own_live = row_start + jnp.arange(own_rows, dtype=jnp.int32) < long_len[0]
    v_long = jnp.where(own_live[:, None], values, 0.0).astype(BF16)
    long_live = jnp.arange(long_rows, dtype=jnp.int32) < long_len[0]
    short_live = jnp.arange(short_rows, dtype=jnp.int32) < short_len[0]
    live_dv_long = jnp.where(long_live[:, None], dv_long, jnp.zeros_like(dv_long))
    live_dv_short = jnp.where(short_live[:, None], dv_short, jnp.zeros_like(dv_short))
    count = lax.axis_size("dp") * master.shape[0]
    grad_long = lax.psum_scatter(
        contract_rows(flat_inputs, live_dv_long).reshape(count, inner_part, kv_width),
        "dp",
        scatter_dimension=0,
        tiled=True,
    )
    flat_inputs = x_short.reshape(short_rows, outer_part * inner_whole)
    product = contract_rows(flat_inputs, live_dv_short).reshape(outer_part, inner_whole, kv_width)
    grad_short = lax.psum_scatter(product, "tensor", scatter_dimension=1, tiled=True)
    new_master, new_moment1, new_moment2 = adam(master, moment1, moment2, grad_long + grad_short)
    next_weight = lax.all_gather(new_master.astype(BF16), "dp", axis=0, tiled=True)
    return (v_long, new_master, new_moment1, new_moment2, next_weight)


def first_kernel(slen_hbm, llen_hbm, xs_hbm, dvs_hbm, xl_hbm, dvl_hbm, master_hbm, *refs):
    blocks, theirs, live_dv, weight, inside, live_rows = refs[:4], *refs[4:9]
    slen_ref, llen_ref, xs_ref, dvs_ref, xl_ref, dvl_ref, master_ref, wide, turned, sems = refs[9:]
    rows, outer, inner = xs_ref.shape
    chips, owned, _, long_rows = theirs.shape
    chunks = 4
    chunk = rows // chunks
    part = inner // 4
    z = lax.axis_index("tensor")
    other = 1 - lax.rem(lax.axis_index("dp"), 2)
    pairs = []
    for c in range(chunks):
        span = pl.ds(c * chunk, chunk)
        pairs.append((xs_hbm.at[span], xs_ref.at[span]))
        pairs.append((dvs_hbm.at[span], dvs_ref.at[span]))
    for c in range(chips):
        pairs.append((xl_hbm.at[pl.ds((2 * c + other) * owned, owned)], xl_ref.at[c]))
    pairs.append((dvl_hbm, dvl_ref))
    pairs.append((master_hbm, master_ref))
    pairs.append((llen_hbm, llen_ref))
    pairs.append((slen_hbm, slen_ref))
    copies = [pltpu.make_async_copy(*pair, sems.at[i]) for i, pair in enumerate(pairs)]
    for copy in copies[-2:] + copies[:-2]:
        copy.start()
    copies[-1].wait()
    for c in range(chunks):
        copies[2 * c].wait()
        copies[2 * c + 1].wait()
        span = slice(c * chunk, (c + 1) * chunk)
        wide[...] = xs_ref[span].reshape(chunk * outer, inner).astype(F32)
        for a in range(outer):
            xa = wide[pl.ds(a, chunk, outer), :].astype(BF16).T
            for j in range(4):
                turned[j, a * part : (a + 1) * part, span] = xa[j * part : (j + 1) * part]
        dv = dvs_ref[span]
        row = lax.broadcasted_iota(jnp.int32, dv.shape, 0) + c * chunk
        dvs_ref[span] = jnp.where(row < slen_ref[0], dv, jnp.zeros_like(dv))
    for k in (3, 2, 1, 0):
        x = turned[lax.bitwise_xor(z, jnp.int32(k))]
        prod = jnp.dot(x, dvs_ref[...], preferred_element_type=F32)
        blocks[k][...] = prod.reshape(outer, part, prod.shape[1]).astype(BF16)
    copies[-2].wait()
    long_len = llen_ref[0]
    for c in range(chips):
        copies[2 * chunks + c].wait()
        x = xl_ref[c]
        row = lax.broadcasted_iota(jnp.int32, x.shape, 2)
        theirs[c] = jnp.where(row < long_len, x, jnp.zeros_like(x))
    copies[-4].wait()
    dv = dvl_ref[...]
    row = lax.broadcasted_iota(jnp.int32, dv.shape, 0)
    live_dv[...] = jnp.where(row < long_len, dv, jnp.zeros_like(dv))
    copies[-3].wait()
    weight[...] = master_ref[...].astype(BF16)
    within = jnp.where(interior(), 1.0, 0.0)
    inside[...] = jnp.full(inside.shape, within, F32)
    row = lax.broadcasted_iota(jnp.int32, live_rows.shape, 0) + z * live_rows.shape[0]
    live_rows[...] = jnp.where(row < long_len, 1.0, 0.0)


def plane_steps():
    core = lax.rem(lax.axis_index("dp"), 2)
    return 0, 1 + core, 2 - core, 3


def long_kernel(x_ref, dv_ref, xs_ref, dvs_ref, *outs):
    chips, outer, inner, rows = xs_ref.shape
    me = lax.axis_index("dp")
    chip, core = me // 2, lax.rem(me, 2)
    for out, rel in reversed(list(zip(outs, plane_steps()))):
        j = lax.bitwise_xor(chip, jnp.int32(rel))
        mine = x_ref[pl.ds((2 * j + core) * outer, outer)].reshape(outer * inner, rows)
        other = xs_ref[j].reshape(outer * inner, rows)
        prod = jnp.dot(mine, dv_ref[...], preferred_element_type=F32)
        prod = prod + jnp.dot(other, dvs_ref[...], preferred_element_type=F32)
        out[...] = prod.reshape(outer, inner, prod.shape[-1]).astype(BF16)


def values_kernel(x_ref, xs_ref, *refs):
    weights, mine_ref, other_ref, acc = refs[:4], refs[-3], refs[-2], refs[-1]
    _, outer, inner, rows = xs_ref.shape
    parts, part, width = mine_ref.shape
    me = lax.axis_index("dp")
    z = lax.axis_index("tensor")
    chip, core = me // 2, lax.rem(me, 2)
    for which, out in ((0, mine_ref), (1, other_ref)):
        total = None
        for weight, rel in zip(weights, plane_steps()):
            j = lax.bitwise_xor(chip, jnp.int32(rel))
            x = xs_ref[j] if which else x_ref[pl.ds((2 * j + core) * outer, outer)]
            w = weight[...].reshape(outer * inner, width)
            term = contract_rows(x.reshape(outer * inner, rows), w)
            total = term if total is None else total + term
        acc[...] = total
        for k in range(parts):
            j = lax.bitwise_xor(z, jnp.int32(k))
            out[k] = acc[pl.ds(pl.multiple_of(j * part, part), part), :].astype(out.dtype)


def update(refs):
    own, near, inside, *terms, master, moment1, moment2 = refs
    grad = own[...].astype(F32) + near[...].astype(F32)
    grad = grad + jnp.where(interior(), inside[...].astype(F32), 0.0)
    for t in terms:
        grad = grad + t[...].astype(F32)
    return adam(master[...], moment1[...], moment2[...], grad)


def weight_kernel(*refs):
    refs[-1][...] = update(refs[:-1])[0].astype(BF16)


def state_kernel(*refs):
    for out, value in zip(refs[-3:], update(refs[:-3])):
        out[...] = value


def place_kernel(kinds, n, outer, *refs):
    pieces, out, sems = refs[:n], refs[-2], refs[-1]
    me = lax.axis_index("dp")
    steps = plane_steps()
    copies = []
    for s, (i, start, step, core) in enumerate(kinds):
        if core and step in (1, 2):
            step = 3 - step
        owner = lax.bitwise_xor(me, 2 * jnp.int32(steps[step]) + core)
        source = pieces[i].at[pl.ds(start, outer)]
        target = out.at[pl.ds(owner * outer, outer)]
        copies.append(pltpu.make_async_copy(source, target, sems.at[s]))
    for copy in copies:
        copy.start()
    for copy in copies:
        copy.wait()


def place(kinds, pieces, outer, whole, name):
    new = isinstance(whole, jax.ShapeDtypeStruct)
    return pl.pallas_call(
        functools.partial(place_kernel, kinds, len(pieces), outer),
        out_shape=jax.ShapeDtypeStruct(whole.shape, whole.dtype),
        in_specs=[VMEM] * len(pieces) + [ANY] * (not new),
        out_specs=ANY,
        scratch_shapes=[pltpu.SemaphoreType.DMA((len(kinds),))],
        input_output_aliases={} if new else {len(pieces): 0},
        compiler_params=params(16),
        cost_estimate=cost(0, 2 * sum(p.size for p in pieces)),
        name=name,
    )(*pieces, *([] if new else [whole]))


def params(mib):
    return pltpu.CompilerParams(vmem_limit_bytes=mib * MIB)


def cost(flops, moved):
    return pl.CostEstimate(flops=flops, bytes_accessed=moved, transcendentals=0)


def swap(x, bit):
    n = lax.axis_size("dp")
    return lax.ppermute(x, "dp", [(i, i ^ bit) for i in range(n)])


def cross(x, turn):
    n = lax.axis_size("dp")
    return lax.ppermute(x, "dp", [(i, i ^ (2 << ((i & 1) ^ turn))) for i in range(n)])


def interior():
    z = lax.axis_index("tensor")
    return (z > 0) & (z < lax.axis_size("tensor") - 1)


def outward(x):
    return lax.ppermute(x, "tensor", [(i, i ^ 1) for i in range(lax.axis_size("tensor"))])


def inward(x):
    n, m = lax.axis_size("tensor"), lax.axis_size("dp")
    pairs = []
    for d in range(m):
        for i in range(n):
            to = (d, i ^ 3) if 0 < i < n - 1 else (d ^ 1, i)
            pairs.append((d * n + i, to[0] * n + to[1]))
    return lax.ppermute(x, ("dp", "tensor"), pairs)


def after(x, *earlier):
    return lax.optimization_barrier((x, *earlier))[0]


def plus(a, b):
    return (a.astype(F32) + b.astype(F32)).astype(BF16)


def body(x_long, dv_long, x_short, dv_short, long_len, short_len, master, moment1, moment2):
    n = lax.axis_size("dp")
    parts = lax.axis_size("tensor")
    outer, inner, width = master.shape
    rows = x_long.shape[0]
    short_rows, _, inner_whole = x_short.shape
    chips = n // 2
    own_rows = rows // parts
    aligned = (
        n & (n - 1) == 0
        and chips == 4
        and parts == 4
        and short_rows % 512 == 0
        and inner % 16 == 0
        and own_rows % 16 == 0
        and rows % 128 == 0
        and short_rows % 128 == 0
        and inner_whole % 128 == 0
        and width % 128 == 0
    )
    if not aligned:
        return plain_body(
            x_long, dv_long, x_short, dv_short, long_len, short_len, master, moment1, moment2
        )
    x_t = jnp.transpose(x_long, (1, 2, 0))
    dv_other = swap(dv_long, 1)
    block = jax.ShapeDtypeStruct((outer, inner, width), BF16)
    *blocks, theirs, live_dv, weight, end_mask, row_mask = pl.pallas_call(
        first_kernel,
        out_shape=[
            *[block] * 4,
            jax.ShapeDtypeStruct((chips, outer, inner, rows), BF16),
            jax.ShapeDtypeStruct(dv_long.shape, BF16),
            block,
            jax.ShapeDtypeStruct((1, 1, width), F32),
            jax.ShapeDtypeStruct((own_rows, width), F32),
        ],
        in_specs=[HBM] * 7,
        out_specs=[VMEM] * 9,
        scratch_shapes=[
            pltpu.SMEM((1,), jnp.int32),
            pltpu.SMEM((1,), jnp.int32),
            pltpu.VMEM(x_short.shape, BF16),
            pltpu.VMEM(dv_short.shape, BF16),
            pltpu.VMEM((chips, outer, inner, rows), BF16),
            pltpu.VMEM(dv_long.shape, BF16),
            pltpu.VMEM(master.shape, F32),
            pltpu.VMEM((short_rows // 4 * outer, inner_whole), F32),
            pltpu.VMEM((4, outer * inner, short_rows), BF16),
            pltpu.SemaphoreType.DMA((12 + chips,)),
        ],
        compiler_params=params(50),
        cost_estimate=cost(2 * short_rows * outer * inner_whole * width, 8 * MIB),
        name="first",
    )(short_len, long_len, x_short, dv_short, x_t, dv_long, master)
    within = end_mask > 0.0
    x_other = swap(theirs, 1)
    from_end = outward(blocks[3])
    second_weight, first_weight = cross(weight, 1), cross(weight, 0)
    long_own, long_first, long_second, long_far = pl.pallas_call(
        long_kernel,
        out_shape=[block] * 4,
        in_specs=[VMEM] * 4,
        out_specs=[VMEM] * 4,
        compiler_params=params(16),
        cost_estimate=cost(4 * rows * chips * outer * inner * width, 4 * MIB),
        name="long_grad",
    )(x_t, live_dv, x_other, dv_other)

    far_sum = cross(long_far, 1)
    second_sum = cross(long_second, 1)
    middle = outward(after(blocks[2], long_own))
    across_sent = plus(after(blocks[2], long_own), from_end)
    across = inward(across_sent)
    first_sent = plus(long_first, far_sum)
    first_sum = cross(first_sent, 0)
    handed = after(second_weight, first_weight, first_sent)
    far_weight = cross(handed, 0)
    inside_sent = plus(after(blocks[3], handed), middle)
    inside = inward(inside_sent)
    across = after(across, inside_sent)
    near_sent = plus(blocks[1], jnp.where(within, across, jnp.zeros_like(across)))
    near = outward(near_sent)

    mine, other = pl.pallas_call(
        values_kernel,
        out_shape=[jax.ShapeDtypeStruct((parts, own_rows, width), t) for t in (F32, BF16)],
        in_specs=[VMEM] * 6,
        out_specs=[VMEM] * 2,
        scratch_shapes=[pltpu.VMEM((rows, width), F32)],
        compiler_params=params(16),
        cost_estimate=cost(4 * rows * chips * outer * inner * width, 6 * MIB),
        name="values",
    )(x_t, x_other, weight, first_weight, second_weight, far_weight)

    arrived = [after(blocks[0], mine), near, inside, long_own, second_sum, first_sum]
    arrived += [master, moment1, moment2]
    next_shard = pl.pallas_call(
        weight_kernel,
        out_shape=block,
        in_specs=[VMEM] * len(arrived),
        out_specs=VMEM,
        compiler_params=params(16),
        cost_estimate=cost(20 * outer * inner * width, 5 * MIB),
        name="next_weight",
    )(*arrived)

    gathered = [next_shard, cross(next_shard, 0), cross(next_shard, 1)]

    total = mine + after(swap(other, 1), next_shard).astype(F32)
    shares = total.astype(BF16)
    v_across_sent = plus(shares[2], outward(shares[3]))
    v_across = inward(v_across_sent)
    v_middle = outward(after(shares[2], v_across_sent))
    v_near = plus(shares[1], jnp.where(within[0], v_across, jnp.zeros_like(v_across)))
    v_inside = plus(shares[3], v_middle)
    values = total[0] + outward(v_near).astype(F32)
    values = values + jnp.where(within[0], inward(v_inside).astype(F32), 0.0)
    v_long = jnp.where(row_mask > 0.0, values, 0.0).astype(BF16)

    new_state = pl.pallas_call(
        state_kernel,
        out_shape=[jax.ShapeDtypeStruct(master.shape, F32)] * 3,
        in_specs=[VMEM] * len(arrived),
        out_specs=[VMEM] * 3,
        compiler_params=params(16),
        cost_estimate=cost(20 * outer * inner * width, 10 * MIB),
        name="new_state",
    )(after(arrived[0], shares), *arrived[1:])

    far = cross(gathered[1], 1)
    early = list(gathered)
    early = early + [swap(x, 1) for x in early]
    kinds = [(i, 0, i % 3, i // 3) for i in range(6)]
    whole_shape = jax.ShapeDtypeStruct((n * outer, inner, width), BF16)
    placed = place(kinds, early, outer, whole_shape, "place_near")
    far = after(far, v_long, new_state[0])
    next_weight = place([(0, 0, 3, 0), (1, 0, 3, 1)], [far, swap(far, 1)], outer, placed, "place_far")
    return (v_long, *new_state, next_weight)


def solution(mesh):
    placed = (
        P("dp", None, "tensor"),
        P("dp", None),
        P("tensor", "dp", None),
        P("tensor", None),
        P("dp"),
        P("tensor"),
        P("dp", "tensor", None),
        P("dp", "tensor", None),
        P("dp", "tensor", None),
    )
    return jax.shard_map(
        body,
        mesh=mesh,
        in_specs=placed,
        out_specs=(
            P(("dp", "tensor"), None),
            P("dp", "tensor", None),
            P("dp", "tensor", None),
            P("dp", "tensor", None),
            P(None, "tensor", None),
        ),
        check_vma=False,
    )
```

```python
import functools

import jax
import jax.numpy as jnp
from jax import lax
from jax.experimental import pallas as pl
from jax.experimental.pallas import tpu as pltpu
from jax.sharding import PartitionSpec as P

BF16 = jnp.bfloat16
F32 = jnp.float32
MIB = 1 << 20
VMEM = pl.BlockSpec(memory_space=pltpu.VMEM)
SMEM = pl.BlockSpec(memory_space=pltpu.SMEM)
ANY = pl.BlockSpec(memory_space=pl.ANY)
HBM = pl.BlockSpec(memory_space=pltpu.HBM)


def contract_rows(left, right):
    return lax.dot_general(
        left, right, (((0,), (0,)), ((), ())), preferred_element_type=jnp.float32
    )


def adam(master, moment1, moment2, grad):
    new_moment1 = 0.9 * moment1 + 0.1 * grad
    new_moment2 = 0.999 * moment2 + 0.001 * grad * grad
    first_corr = 1.0 - 0.9**10
    second_corr = 1.0 - 0.999**10
    update = new_moment1 / first_corr / (jnp.sqrt(new_moment2 / second_corr) + 1e-08)
    new_master = master - 0.01 * (update + 0.1 * master)
    return new_master, new_moment1, new_moment2


def plain_body(x_long, dv_long, x_short, dv_short, long_len, short_len, master, moment1, moment2):
    weight_shard = master.astype(BF16)
    long_rows, _, inner_part = x_long.shape
    kv_width = master.shape[2]
    short_rows, outer_part, inner_whole = x_short.shape
    piece = lax.all_gather(weight_shard, "dp", axis=0, tiled=True)
    flat_inputs = x_long.reshape(long_rows, piece.shape[0] * inner_part)
    flat_piece = piece.reshape(piece.shape[0] * inner_part, kv_width)
    partial_values = jnp.dot(flat_inputs, flat_piece, preferred_element_type=F32)
    values = lax.psum_scatter(partial_values, "tensor", scatter_dimension=0, tiled=True)
    own_rows = values.shape[0]
    row_start = lax.axis_index("tensor") * own_rows
    own_live = row_start + jnp.arange(own_rows, dtype=jnp.int32) < long_len[0]
    v_long = jnp.where(own_live[:, None], values, 0.0).astype(BF16)
    long_live = jnp.arange(long_rows, dtype=jnp.int32) < long_len[0]
    short_live = jnp.arange(short_rows, dtype=jnp.int32) < short_len[0]
    live_dv_long = jnp.where(long_live[:, None], dv_long, jnp.zeros_like(dv_long))
    live_dv_short = jnp.where(short_live[:, None], dv_short, jnp.zeros_like(dv_short))
    count = lax.axis_size("dp") * master.shape[0]
    grad_long = lax.psum_scatter(
        contract_rows(flat_inputs, live_dv_long).reshape(count, inner_part, kv_width),
        "dp",
        scatter_dimension=0,
        tiled=True,
    )
    flat_inputs = x_short.reshape(short_rows, outer_part * inner_whole)
    product = contract_rows(flat_inputs, live_dv_short).reshape(outer_part, inner_whole, kv_width)
    grad_short = lax.psum_scatter(product, "tensor", scatter_dimension=1, tiled=True)
    new_master, new_moment1, new_moment2 = adam(master, moment1, moment2, grad_long + grad_short)
    next_weight = lax.all_gather(new_master.astype(BF16), "dp", axis=0, tiled=True)
    return (v_long, new_master, new_moment1, new_moment2, next_weight)


def first_kernel(slen_hbm, llen_hbm, xs_hbm, dvs_hbm, xl_hbm, dvl_hbm, master_hbm, *refs):
    blocks, theirs, live_dv, weight, inside, live_rows = refs[:4], *refs[4:9]
    slen_ref, llen_ref, xs_ref, dvs_ref, xl_ref, dvl_ref, master_ref, wide, turned, sems = refs[9:]
    rows, outer, inner = xs_ref.shape
    chips, owned, _, long_rows = theirs.shape
    chunks = 4
    chunk = rows // chunks
    part = inner // 4
    z = lax.axis_index("tensor")
    other = 1 - lax.rem(lax.axis_index("dp"), 2)
    pairs = []
    for c in range(chunks):
        span = pl.ds(c * chunk, chunk)
        pairs.append((xs_hbm.at[span], xs_ref.at[span]))
        pairs.append((dvs_hbm.at[span], dvs_ref.at[span]))
    for c in range(chips):
        pairs.append((xl_hbm.at[pl.ds((2 * c + other) * owned, owned)], xl_ref.at[c]))
    pairs.append((dvl_hbm, dvl_ref))
    pairs.append((master_hbm, master_ref))
    pairs.append((llen_hbm, llen_ref))
    pairs.append((slen_hbm, slen_ref))
    copies = [pltpu.make_async_copy(*pair, sems.at[i]) for i, pair in enumerate(pairs)]
    for copy in copies[-2:] + copies[:-2]:
        copy.start()
    copies[-1].wait()
    for c in range(chunks):
        copies[2 * c].wait()
        copies[2 * c + 1].wait()
        span = slice(c * chunk, (c + 1) * chunk)
        wide[...] = xs_ref[span].reshape(chunk * outer, inner).astype(F32)
        for a in range(outer):
            xa = wide[pl.ds(a, chunk, outer), :].astype(BF16).T
            for j in range(4):
                turned[j, a * part : (a + 1) * part, span] = xa[j * part : (j + 1) * part]
        dv = dvs_ref[span]
        row = lax.broadcasted_iota(jnp.int32, dv.shape, 0) + c * chunk
        dvs_ref[span] = jnp.where(row < slen_ref[0], dv, jnp.zeros_like(dv))
    for k in (3, 2, 1, 0):
        x = turned[lax.bitwise_xor(z, jnp.int32(k))]
        prod = jnp.dot(x, dvs_ref[...], preferred_element_type=F32)
        blocks[k][...] = prod.reshape(outer, part, prod.shape[1]).astype(BF16)
    copies[-2].wait()
    long_len = llen_ref[0]
    for c in range(chips):
        copies[2 * chunks + c].wait()
        x = xl_ref[c]
        row = lax.broadcasted_iota(jnp.int32, x.shape, 2)
        theirs[c] = jnp.where(row < long_len, x, jnp.zeros_like(x))
    copies[-4].wait()
    dv = dvl_ref[...]
    row = lax.broadcasted_iota(jnp.int32, dv.shape, 0)
    live_dv[...] = jnp.where(row < long_len, dv, jnp.zeros_like(dv))
    copies[-3].wait()
    weight[...] = master_ref[...].astype(BF16)
    within = jnp.where(interior(), 1.0, 0.0)
    inside[...] = jnp.full(inside.shape, within, F32)
    row = lax.broadcasted_iota(jnp.int32, live_rows.shape, 0) + z * live_rows.shape[0]
    live_rows[...] = jnp.where(row < long_len, 1.0, 0.0)


def plane_steps():
    core = lax.rem(lax.axis_index("dp"), 2)
    return 0, 1 + core, 2 - core, 3


def long_kernel(x_ref, dv_ref, xs_ref, dvs_ref, *outs):
    chips, outer, inner, rows = xs_ref.shape
    me = lax.axis_index("dp")
    chip, core = me // 2, lax.rem(me, 2)
    for out, rel in reversed(list(zip(outs, plane_steps()))):
        j = lax.bitwise_xor(chip, jnp.int32(rel))
        mine = x_ref[pl.ds((2 * j + core) * outer, outer)].reshape(outer * inner, rows)
        other = xs_ref[j].reshape(outer * inner, rows)
        prod = jnp.dot(mine, dv_ref[...], preferred_element_type=F32)
        prod = prod + jnp.dot(other, dvs_ref[...], preferred_element_type=F32)
        out[...] = prod.reshape(outer, inner, prod.shape[-1]).astype(BF16)


def values_kernel(x_ref, xs_ref, *refs):
    weights, mine_ref, other_ref, acc = refs[:4], refs[-3], refs[-2], refs[-1]
    _, outer, inner, rows = xs_ref.shape
    parts, part, width = mine_ref.shape
    me = lax.axis_index("dp")
    z = lax.axis_index("tensor")
    chip, core = me // 2, lax.rem(me, 2)
    for which, out in ((0, mine_ref), (1, other_ref)):
        total = None
        for weight, rel in zip(weights, plane_steps()):
            j = lax.bitwise_xor(chip, jnp.int32(rel))
            x = xs_ref[j] if which else x_ref[pl.ds((2 * j + core) * outer, outer)]
            w = weight[...].reshape(outer * inner, width)
            term = contract_rows(x.reshape(outer * inner, rows), w)
            total = term if total is None else total + term
        acc[...] = total
        for k in range(parts):
            j = lax.bitwise_xor(z, jnp.int32(k))
            out[k] = acc[pl.ds(pl.multiple_of(j * part, part), part), :].astype(out.dtype)


def update(refs):
    own, near, inside, *terms, master, moment1, moment2 = refs
    grad = own[...].astype(F32) + near[...].astype(F32)
    grad = grad + jnp.where(interior(), inside[...].astype(F32), 0.0)
    for t in terms:
        grad = grad + t[...].astype(F32)
    return adam(master[...], moment1[...], moment2[...], grad)


def weight_kernel(*refs):
    refs[-1][...] = update(refs[:-1])[0].astype(BF16)


def state_kernel(*refs):
    for out, value in zip(refs[-3:], update(refs[:-3])):
        out[...] = value


def place_kernel(kinds, n, outer, *refs):
    pieces, out, sems = refs[:n], refs[-2], refs[-1]
    me = lax.axis_index("dp")
    steps = plane_steps()
    copies = []
    for s, (i, start, step, core) in enumerate(kinds):
        if core and step in (1, 2):
            step = 3 - step
        owner = lax.bitwise_xor(me, 2 * jnp.int32(steps[step]) + core)
        source = pieces[i].at[pl.ds(start, outer)]
        target = out.at[pl.ds(owner * outer, outer)]
        copies.append(pltpu.make_async_copy(source, target, sems.at[s]))
    for copy in copies:
        copy.start()
    for copy in copies:
        copy.wait()


def place(kinds, pieces, outer, whole, name):
    new = isinstance(whole, jax.ShapeDtypeStruct)
    return pl.pallas_call(
        functools.partial(place_kernel, kinds, len(pieces), outer),
        out_shape=jax.ShapeDtypeStruct(whole.shape, whole.dtype),
        in_specs=[VMEM] * len(pieces) + [ANY] * (not new),
        out_specs=ANY,
        scratch_shapes=[pltpu.SemaphoreType.DMA((len(kinds),))],
        input_output_aliases={} if new else {len(pieces): 0},
        compiler_params=params(16),
        cost_estimate=cost(0, 2 * sum(p.size for p in pieces)),
        name=name,
    )(*pieces, *([] if new else [whole]))


def params(mib):
    return pltpu.CompilerParams(vmem_limit_bytes=mib * MIB)


def cost(flops, moved):
    return pl.CostEstimate(flops=flops, bytes_accessed=moved, transcendentals=0)


def swap(x, bit):
    n = lax.axis_size("dp")
    return lax.ppermute(x, "dp", [(i, i ^ bit) for i in range(n)])


def cross(x, turn):
    n = lax.axis_size("dp")
    return lax.ppermute(x, "dp", [(i, i ^ (2 << ((i & 1) ^ turn))) for i in range(n)])


def interior():
    z = lax.axis_index("tensor")
    return (z > 0) & (z < lax.axis_size("tensor") - 1)


def outward(x):
    return lax.ppermute(x, "tensor", [(i, i ^ 1) for i in range(lax.axis_size("tensor"))])


def inward(x):
    n, m = lax.axis_size("tensor"), lax.axis_size("dp")
    pairs = []
    for d in range(m):
        for i in range(n):
            to = (d, i ^ 3) if 0 < i < n - 1 else (d ^ 1, i)
            pairs.append((d * n + i, to[0] * n + to[1]))
    return lax.ppermute(x, ("dp", "tensor"), pairs)


def after(x, *earlier):
    return lax.optimization_barrier((x, *earlier))[0]


def plus(a, b):
    return (a.astype(F32) + b.astype(F32)).astype(BF16)


def body(x_long, dv_long, x_short, dv_short, long_len, short_len, master, moment1, moment2):
    n = lax.axis_size("dp")
    parts = lax.axis_size("tensor")
    outer, inner, width = master.shape
    rows = x_long.shape[0]
    short_rows, _, inner_whole = x_short.shape
    chips = n // 2
    own_rows = rows // parts
    aligned = (
        n & (n - 1) == 0
        and chips == 4
        and parts == 4
        and short_rows % 512 == 0
        and inner % 16 == 0
        and own_rows % 16 == 0
        and rows % 128 == 0
        and short_rows % 128 == 0
        and inner_whole % 128 == 0
        and width % 128 == 0
    )
    if not aligned:
        return plain_body(
            x_long, dv_long, x_short, dv_short, long_len, short_len, master, moment1, moment2
        )
    x_t = jnp.transpose(x_long, (1, 2, 0))
    dv_other = swap(dv_long, 1)
    block = jax.ShapeDtypeStruct((outer, inner, width), BF16)
    *blocks, theirs, live_dv, weight, end_mask, row_mask = pl.pallas_call(
        first_kernel,
        out_shape=[
            *[block] * 4,
            jax.ShapeDtypeStruct((chips, outer, inner, rows), BF16),
            jax.ShapeDtypeStruct(dv_long.shape, BF16),
            block,
            jax.ShapeDtypeStruct((1, 1, width), F32),
            jax.ShapeDtypeStruct((own_rows, width), F32),
        ],
        in_specs=[HBM] * 7,
        out_specs=[VMEM] * 9,
        scratch_shapes=[
            pltpu.SMEM((1,), jnp.int32),
            pltpu.SMEM((1,), jnp.int32),
            pltpu.VMEM(x_short.shape, BF16),
            pltpu.VMEM(dv_short.shape, BF16),
            pltpu.VMEM((chips, outer, inner, rows), BF16),
            pltpu.VMEM(dv_long.shape, BF16),
            pltpu.VMEM(master.shape, F32),
            pltpu.VMEM((short_rows // 4 * outer, inner_whole), F32),
            pltpu.VMEM((4, outer * inner, short_rows), BF16),
            pltpu.SemaphoreType.DMA((12 + chips,)),
        ],
        compiler_params=params(50),
        cost_estimate=cost(2 * short_rows * outer * inner_whole * width, 8 * MIB),
        name="first",
    )(short_len, long_len, x_short, dv_short, x_t, dv_long, master)
    within = end_mask > 0.0
    x_other = swap(theirs, 1)
    from_end = outward(blocks[3])
    second_weight, first_weight = cross(weight, 1), cross(weight, 0)
    long_own, long_first, long_second, long_far = pl.pallas_call(
        long_kernel,
        out_shape=[block] * 4,
        in_specs=[VMEM] * 4,
        out_specs=[VMEM] * 4,
        compiler_params=params(16),
        cost_estimate=cost(4 * rows * chips * outer * inner * width, 4 * MIB),
        name="long_grad",
    )(x_t, live_dv, x_other, dv_other)

    far_sum = cross(long_far, 1)
    second_sum = cross(long_second, 1)
    middle = outward(after(blocks[2], long_own))
    across_sent = plus(after(blocks[2], long_own), from_end)
    across = inward(across_sent)
    first_sent = plus(long_first, far_sum)
    first_sum = cross(first_sent, 0)
    handed = after(second_weight, first_weight, first_sent)
    far_weight = cross(handed, 0)
    inside_sent = plus(after(blocks[3], handed), middle)
    inside = inward(inside_sent)
    across = after(across, inside_sent)
    near_sent = plus(blocks[1], jnp.where(within, across, jnp.zeros_like(across)))
    near = outward(near_sent)

    mine, other = pl.pallas_call(
        values_kernel,
        out_shape=[jax.ShapeDtypeStruct((parts, own_rows, width), t) for t in (F32, BF16)],
        in_specs=[VMEM] * 6,
        out_specs=[VMEM] * 2,
        scratch_shapes=[pltpu.VMEM((rows, width), F32)],
        compiler_params=params(16),
        cost_estimate=cost(4 * rows * chips * outer * inner * width, 6 * MIB),
        name="values",
    )(x_t, x_other, weight, first_weight, second_weight, far_weight)

    arrived = [after(blocks[0], mine), near, inside, long_own, second_sum, first_sum]
    arrived += [master, moment1, moment2]
    next_shard = pl.pallas_call(
        weight_kernel,
        out_shape=block,
        in_specs=[VMEM] * len(arrived),
        out_specs=VMEM,
        compiler_params=params(16),
        cost_estimate=cost(20 * outer * inner * width, 5 * MIB),
        name="next_weight",
    )(*arrived)

    gathered = [next_shard, cross(next_shard, 0), cross(next_shard, 1)]

    total = mine + after(swap(other, 1), next_shard).astype(F32)
    shares = total.astype(BF16)
    v_across_sent = plus(shares[2], outward(shares[3]))
    v_across = inward(v_across_sent)
    v_middle = outward(after(shares[2], v_across_sent))
    v_near = plus(shares[1], jnp.where(within[0], v_across, jnp.zeros_like(v_across)))
    v_inside = plus(shares[3], v_middle)
    values = total[0] + outward(v_near).astype(F32)
    values = values + jnp.where(within[0], inward(v_inside).astype(F32), 0.0)
    v_long = jnp.where(row_mask > 0.0, values, 0.0).astype(BF16)

    new_state = pl.pallas_call(
        state_kernel,
        out_shape=[jax.ShapeDtypeStruct(master.shape, F32)] * 3,
        in_specs=[VMEM] * len(arrived),
        out_specs=[VMEM] * 3,
        compiler_params=params(16),
        cost_estimate=cost(20 * outer * inner * width, 10 * MIB),
        name="new_state",
    )(after(arrived[0], shares), *arrived[1:])

    far = cross(gathered[1], 1)
    early = list(gathered)
    early = early + [swap(x, 1) for x in early]
    kinds = [(i, 0, i % 3, i // 3) for i in range(6)]
    whole_shape = jax.ShapeDtypeStruct((n * outer, inner, width), BF16)
    placed = place(kinds, early, outer, whole_shape, "place_near")
    far = after(far, v_long, new_state[0], early[3])
    next_weight = place([(0, 0, 3, 0), (1, 0, 3, 1)], [far, swap(far, 1)], outer, placed, "place_far")
    return (v_long, *new_state, next_weight)


def solution(mesh):
    placed = (
        P("dp", None, "tensor"),
        P("dp", None),
        P("tensor", "dp", None),
        P("tensor", None),
        P("dp"),
        P("tensor"),
        P("dp", "tensor", None),
        P("dp", "tensor", None),
        P("dp", "tensor", None),
    )
    return jax.shard_map(
        body,
        mesh=mesh,
        in_specs=placed,
        out_specs=(
            P(("dp", "tensor"), None),
            P("dp", "tensor", None),
            P("dp", "tensor", None),
            P("dp", "tensor", None),
            P(None, "tensor", None),
        ),
        check_vma=False,
    )
```

```python
import functools

import jax
import jax.numpy as jnp
from jax import lax
from jax.experimental import pallas as pl
from jax.experimental.pallas import tpu as pltpu
from jax.sharding import PartitionSpec as P

BF16 = jnp.bfloat16
F32 = jnp.float32
MIB = 1 << 20
VMEM = pl.BlockSpec(memory_space=pltpu.VMEM)
SMEM = pl.BlockSpec(memory_space=pltpu.SMEM)
ANY = pl.BlockSpec(memory_space=pl.ANY)
HBM = pl.BlockSpec(memory_space=pltpu.HBM)


def contract_rows(left, right):
    return lax.dot_general(
        left, right, (((0,), (0,)), ((), ())), preferred_element_type=jnp.float32
    )


def adam(master, moment1, moment2, grad):
    new_moment1 = 0.9 * moment1 + 0.1 * grad
    new_moment2 = 0.999 * moment2 + 0.001 * grad * grad
    first_corr = 1.0 - 0.9**10
    second_corr = 1.0 - 0.999**10
    update = new_moment1 / first_corr / (jnp.sqrt(new_moment2 / second_corr) + 1e-08)
    new_master = master - 0.01 * (update + 0.1 * master)
    return new_master, new_moment1, new_moment2


def plain_body(x_long, dv_long, x_short, dv_short, long_len, short_len, master, moment1, moment2):
    weight_shard = master.astype(BF16)
    long_rows, _, inner_part = x_long.shape
    kv_width = master.shape[2]
    short_rows, outer_part, inner_whole = x_short.shape
    piece = lax.all_gather(weight_shard, "dp", axis=0, tiled=True)
    flat_inputs = x_long.reshape(long_rows, piece.shape[0] * inner_part)
    flat_piece = piece.reshape(piece.shape[0] * inner_part, kv_width)
    partial_values = jnp.dot(flat_inputs, flat_piece, preferred_element_type=F32)
    values = lax.psum_scatter(partial_values, "tensor", scatter_dimension=0, tiled=True)
    own_rows = values.shape[0]
    row_start = lax.axis_index("tensor") * own_rows
    own_live = row_start + jnp.arange(own_rows, dtype=jnp.int32) < long_len[0]
    v_long = jnp.where(own_live[:, None], values, 0.0).astype(BF16)
    long_live = jnp.arange(long_rows, dtype=jnp.int32) < long_len[0]
    short_live = jnp.arange(short_rows, dtype=jnp.int32) < short_len[0]
    live_dv_long = jnp.where(long_live[:, None], dv_long, jnp.zeros_like(dv_long))
    live_dv_short = jnp.where(short_live[:, None], dv_short, jnp.zeros_like(dv_short))
    count = lax.axis_size("dp") * master.shape[0]
    grad_long = lax.psum_scatter(
        contract_rows(flat_inputs, live_dv_long).reshape(count, inner_part, kv_width),
        "dp",
        scatter_dimension=0,
        tiled=True,
    )
    flat_inputs = x_short.reshape(short_rows, outer_part * inner_whole)
    product = contract_rows(flat_inputs, live_dv_short).reshape(outer_part, inner_whole, kv_width)
    grad_short = lax.psum_scatter(product, "tensor", scatter_dimension=1, tiled=True)
    new_master, new_moment1, new_moment2 = adam(master, moment1, moment2, grad_long + grad_short)
    next_weight = lax.all_gather(new_master.astype(BF16), "dp", axis=0, tiled=True)
    return (v_long, new_master, new_moment1, new_moment2, next_weight)


def short_copies(xs_hbm, dvs_hbm, xs_ref, dvs_ref):
    chunks = 4
    chunk = xs_ref.shape[0] // chunks
    spans = [pl.ds(c * chunk, chunk) for c in range(chunks)]
    return [
        (hbm.at[span], ref.at[span])
        for span in spans
        for hbm, ref in ((xs_hbm, xs_ref), (dvs_hbm, dvs_ref))
    ]


def short_blocks(copies, short_len, xs_ref, dvs_ref, wide, turned, blocks):
    rows, outer, inner = xs_ref.shape
    chunks = len(copies) // 2
    chunk = rows // chunks
    part = inner // 4
    for c in range(chunks):
        copies[2 * c].wait()
        copies[2 * c + 1].wait()
        span = slice(c * chunk, (c + 1) * chunk)
        wide[...] = xs_ref[span].reshape(chunk * outer, inner).astype(F32)
        for a in range(outer):
            xa = wide[pl.ds(a, chunk, outer), :].astype(BF16).T
            for j in range(4):
                turned[j, a * part : (a + 1) * part, span] = xa[j * part : (j + 1) * part]
        dv = dvs_ref[span]
        row = lax.broadcasted_iota(jnp.int32, dv.shape, 0) + c * chunk
        dvs_ref[span] = jnp.where(row < short_len, dv, jnp.zeros_like(dv))
    for k, out in blocks.items():
        x = turned[lax.bitwise_xor(lax.axis_index("tensor"), jnp.int32(k))]
        prod = jnp.dot(x, dvs_ref[...], preferred_element_type=F32)
        out[...] = prod.reshape(out.shape).astype(BF16)


def first_kernel(slen_ref, llen_ref, xs_hbm, dvs_hbm, xl_hbm, dvl_hbm, master_hbm, *refs):
    end_block, theirs, live_dv, weight, inside, live_rows = refs[:6]
    xs_ref, dvs_ref, xl_ref, dvl_ref, master_ref, wide, turned, sems = refs[6:]
    chips, owned, _, _ = theirs.shape
    other = 1 - lax.rem(lax.axis_index("dp"), 2)
    pairs = short_copies(xs_hbm, dvs_hbm, xs_ref, dvs_ref)
    short = len(pairs)
    for c in range(chips):
        pairs.append((xl_hbm.at[pl.ds((2 * c + other) * owned, owned)], xl_ref.at[c]))
    pairs.append((dvl_hbm, dvl_ref))
    pairs.append((master_hbm, master_ref))
    copies = [pltpu.make_async_copy(*pair, sems.at[i]) for i, pair in enumerate(pairs)]
    for copy in copies:
        copy.start()
    short_blocks(copies[:short], slen_ref[0], xs_ref, dvs_ref, wide, turned, {3: end_block})
    long_len = llen_ref[0]
    for c in range(chips):
        copies[short + c].wait()
        x = xl_ref[c]
        row = lax.broadcasted_iota(jnp.int32, x.shape, 2)
        theirs[c] = jnp.where(row < long_len, x, jnp.zeros_like(x))
    copies[-2].wait()
    dv = dvl_ref[...]
    row = lax.broadcasted_iota(jnp.int32, dv.shape, 0)
    live_dv[...] = jnp.where(row < long_len, dv, jnp.zeros_like(dv))
    copies[-1].wait()
    weight[...] = master_ref[...].astype(BF16)
    inside[...] = jnp.full(inside.shape, jnp.where(interior(), 1.0, 0.0), F32)
    row = lax.broadcasted_iota(jnp.int32, live_rows.shape, 0)
    row = row + lax.axis_index("tensor") * live_rows.shape[0]
    live_rows[...] = jnp.where(row < long_len, 1.0, 0.0)


def second_kernel(slen_ref, xs_hbm, dvs_hbm, *refs):
    outs, (xs_ref, dvs_ref, wide, turned, sems) = refs[:3], refs[3:]
    pairs = short_copies(xs_hbm, dvs_hbm, xs_ref, dvs_ref)
    copies = [pltpu.make_async_copy(*pair, sems.at[i]) for i, pair in enumerate(pairs)]
    for copy in copies:
        copy.start()
    blocks = {k: outs[k] for k in (2, 1, 0)}
    short_blocks(copies, slen_ref[0], xs_ref, dvs_ref, wide, turned, blocks)


def plane_steps():
    core = lax.rem(lax.axis_index("dp"), 2)
    return 0, 1 + core, 2 - core, 3


def long_kernel(x_ref, dv_ref, xs_ref, dvs_ref, *outs):
    chips, outer, inner, rows = xs_ref.shape
    me = lax.axis_index("dp")
    chip, core = me // 2, lax.rem(me, 2)
    for out, rel in reversed(list(zip(outs, plane_steps()))):
        j = lax.bitwise_xor(chip, jnp.int32(rel))
        mine = x_ref[pl.ds((2 * j + core) * outer, outer)].reshape(outer * inner, rows)
        other = xs_ref[j].reshape(outer * inner, rows)
        prod = jnp.dot(mine, dv_ref[...], preferred_element_type=F32)
        prod = prod + jnp.dot(other, dvs_ref[...], preferred_element_type=F32)
        out[...] = prod.reshape(outer, inner, prod.shape[-1]).astype(BF16)


def values_kernel(x_ref, xs_ref, *refs):
    weights, mine_ref, other_ref, acc = refs[:4], refs[-3], refs[-2], refs[-1]
    _, outer, inner, rows = xs_ref.shape
    parts, part, width = mine_ref.shape
    me = lax.axis_index("dp")
    z = lax.axis_index("tensor")
    chip, core = me // 2, lax.rem(me, 2)
    for which, out in ((0, mine_ref), (1, other_ref)):
        total = None
        for weight, rel in zip(weights, plane_steps()):
            j = lax.bitwise_xor(chip, jnp.int32(rel))
            x = xs_ref[j] if which else x_ref[pl.ds((2 * j + core) * outer, outer)]
            w = weight[...].reshape(outer * inner, width)
            term = contract_rows(x.reshape(outer * inner, rows), w)
            total = term if total is None else total + term
        acc[...] = total
        for k in range(parts):
            j = lax.bitwise_xor(z, jnp.int32(k))
            out[k] = acc[pl.ds(pl.multiple_of(j * part, part), part), :].astype(out.dtype)


def update(refs):
    own, near, inside, *terms, master, moment1, moment2 = refs
    grad = own[...].astype(F32) + near[...].astype(F32)
    grad = grad + jnp.where(interior(), inside[...].astype(F32), 0.0)
    for t in terms:
        grad = grad + t[...].astype(F32)
    return adam(master[...], moment1[...], moment2[...], grad)


def weight_kernel(*refs):
    refs[-1][...] = update(refs[:-1])[0].astype(BF16)


def state_kernel(*refs):
    for out, value in zip(refs[-3:], update(refs[:-3])):
        out[...] = value


def place_kernel(kinds, n, outer, *refs):
    pieces, out, sems = refs[:n], refs[-2], refs[-1]
    me = lax.axis_index("dp")
    steps = plane_steps()
    copies = []
    for s, (i, start, step, core) in enumerate(kinds):
        if core and step in (1, 2):
            step = 3 - step
        owner = lax.bitwise_xor(me, 2 * jnp.int32(steps[step]) + core)
        source = pieces[i].at[pl.ds(start, outer)]
        target = out.at[pl.ds(owner * outer, outer)]
        copies.append(pltpu.make_async_copy(source, target, sems.at[s]))
    for copy in copies:
        copy.start()
    for copy in copies:
        copy.wait()


def place(kinds, pieces, outer, whole, name):
    new = isinstance(whole, jax.ShapeDtypeStruct)
    return pl.pallas_call(
        functools.partial(place_kernel, kinds, len(pieces), outer),
        out_shape=jax.ShapeDtypeStruct(whole.shape, whole.dtype),
        in_specs=[VMEM] * len(pieces) + [ANY] * (not new),
        out_specs=ANY,
        scratch_shapes=[pltpu.SemaphoreType.DMA((len(kinds),))],
        input_output_aliases={} if new else {len(pieces): 0},
        compiler_params=params(16),
        cost_estimate=cost(0, 2 * sum(p.size for p in pieces)),
        name=name,
    )(*pieces, *([] if new else [whole]))


def params(mib):
    return pltpu.CompilerParams(vmem_limit_bytes=mib * MIB)


def cost(flops, moved):
    return pl.CostEstimate(flops=flops, bytes_accessed=moved, transcendentals=0)


def swap(x, bit):
    n = lax.axis_size("dp")
    return lax.ppermute(x, "dp", [(i, i ^ bit) for i in range(n)])


def cross(x, turn):
    n = lax.axis_size("dp")
    return lax.ppermute(x, "dp", [(i, i ^ (2 << ((i & 1) ^ turn))) for i in range(n)])


def interior():
    z = lax.axis_index("tensor")
    return (z > 0) & (z < lax.axis_size("tensor") - 1)


def outward(x):
    return lax.ppermute(x, "tensor", [(i, i ^ 1) for i in range(lax.axis_size("tensor"))])


def inward(x):
    n, m = lax.axis_size("tensor"), lax.axis_size("dp")
    pairs = []
    for d in range(m):
        for i in range(n):
            to = (d, i ^ 3) if 0 < i < n - 1 else (d ^ 1, i)
            pairs.append((d * n + i, to[0] * n + to[1]))
    return lax.ppermute(x, ("dp", "tensor"), pairs)


def after(x, *earlier):
    return lax.optimization_barrier((x, *earlier))[0]


def plus(a, b):
    return (a.astype(F32) + b.astype(F32)).astype(BF16)


def body(x_long, dv_long, x_short, dv_short, long_len, short_len, master, moment1, moment2):
    n = lax.axis_size("dp")
    parts = lax.axis_size("tensor")
    outer, inner, width = master.shape
    rows = x_long.shape[0]
    short_rows, _, inner_whole = x_short.shape
    chips = n // 2
    own_rows = rows // parts
    aligned = (
        n & (n - 1) == 0
        and chips == 4
        and parts == 4
        and short_rows % 512 == 0
        and inner % 16 == 0
        and own_rows % 16 == 0
        and rows % 128 == 0
        and short_rows % 128 == 0
        and inner_whole % 128 == 0
        and width % 128 == 0
    )
    if not aligned:
        return plain_body(
            x_long, dv_long, x_short, dv_short, long_len, short_len, master, moment1, moment2
        )
    x_t = jnp.transpose(x_long, (1, 2, 0))
    dv_other = swap(dv_long, 1)
    block = jax.ShapeDtypeStruct((outer, inner, width), BF16)
    short_scratch = [pltpu.VMEM(x_short.shape, BF16), pltpu.VMEM(dv_short.shape, BF16)]
    turn_scratch = [
        pltpu.VMEM((short_rows // 4 * outer, inner_whole), F32),
        pltpu.VMEM((4, outer * inner, short_rows), BF16),
    ]
    end_block, theirs, live_dv, weight, end_mask, row_mask = pl.pallas_call(
        first_kernel,
        out_shape=[
            block,
            jax.ShapeDtypeStruct((chips, outer, inner, rows), BF16),
            jax.ShapeDtypeStruct(dv_long.shape, BF16),
            block,
            jax.ShapeDtypeStruct((1, 1, width), F32),
            jax.ShapeDtypeStruct((own_rows, width), F32),
        ],
        in_specs=[SMEM, SMEM] + [HBM] * 5,
        out_specs=[VMEM] * 6,
        scratch_shapes=[
            *short_scratch,
            pltpu.VMEM((chips, outer, inner, rows), BF16),
            pltpu.VMEM(dv_long.shape, BF16),
            pltpu.VMEM(master.shape, F32),
            *turn_scratch,
            pltpu.SemaphoreType.DMA((10 + chips,)),
        ],
        compiler_params=params(52),
        cost_estimate=cost(short_rows * outer * inner_whole * width, 8 * MIB),
        name="first",
    )(short_len, long_len, x_short, dv_short, x_t, dv_long, master)
    blocks = pl.pallas_call(
        second_kernel,
        out_shape=[block] * 3,
        in_specs=[SMEM] + [HBM] * 2,
        out_specs=[VMEM] * 3,
        scratch_shapes=[*short_scratch, *turn_scratch, pltpu.SemaphoreType.DMA((8,))],
        compiler_params=params(40),
        cost_estimate=cost(2 * short_rows * outer * inner_whole * width, 4 * MIB),
        name="second",
    )(short_len, x_short, dv_short)
    blocks = [*blocks, end_block]
    within = end_mask > 0.0
    x_other = swap(theirs, 1)
    from_end = outward(blocks[3])
    second_weight, first_weight = cross(weight, 1), cross(weight, 0)
    long_own, long_first, long_second, long_far = pl.pallas_call(
        long_kernel,
        out_shape=[block] * 4,
        in_specs=[VMEM] * 4,
        out_specs=[VMEM] * 4,
        compiler_params=params(16),
        cost_estimate=cost(4 * rows * chips * outer * inner * width, 4 * MIB),
        name="long_grad",
    )(x_t, live_dv, x_other, dv_other)

    far_sum = cross(long_far, 1)
    second_sum = cross(long_second, 1)
    middle = outward(after(blocks[2], long_own))
    across_sent = plus(after(blocks[2], long_own), from_end)
    across = inward(across_sent)
    first_sent = plus(long_first, far_sum)
    first_sum = cross(first_sent, 0)
    handed = after(second_weight, first_weight, first_sent)
    far_weight = cross(handed, 0)
    inside_sent = plus(after(blocks[3], handed), middle)
    inside = inward(inside_sent)
    across = after(across, inside_sent)
    near_sent = plus(blocks[1], jnp.where(within, across, jnp.zeros_like(across)))
    near = outward(near_sent)

    mine, other = pl.pallas_call(
        values_kernel,
        out_shape=[jax.ShapeDtypeStruct((parts, own_rows, width), t) for t in (F32, BF16)],
        in_specs=[VMEM] * 6,
        out_specs=[VMEM] * 2,
        scratch_shapes=[pltpu.VMEM((rows, width), F32)],
        compiler_params=params(16),
        cost_estimate=cost(4 * rows * chips * outer * inner * width, 6 * MIB),
        name="values",
    )(x_t, x_other, weight, first_weight, second_weight, far_weight)

    arrived = [after(blocks[0], mine), near, inside, long_own, second_sum, first_sum]
    arrived += [master, moment1, moment2]
    next_shard = pl.pallas_call(
        weight_kernel,
        out_shape=block,
        in_specs=[VMEM] * len(arrived),
        out_specs=VMEM,
        compiler_params=params(16),
        cost_estimate=cost(20 * outer * inner * width, 5 * MIB),
        name="next_weight",
    )(*arrived)

    gathered = [next_shard, cross(next_shard, 0), cross(next_shard, 1)]

    total = mine + after(swap(other, 1), next_shard).astype(F32)
    shares = total.astype(BF16)
    v_across_sent = plus(shares[2], outward(shares[3]))
    v_across = inward(v_across_sent)
    v_middle = outward(after(shares[2], v_across_sent))
    v_near = plus(shares[1], jnp.where(within[0], v_across, jnp.zeros_like(v_across)))
    v_inside = plus(shares[3], v_middle)
    values = total[0] + outward(v_near).astype(F32)
    values = values + jnp.where(within[0], inward(v_inside).astype(F32), 0.0)
    v_long = jnp.where(row_mask > 0.0, values, 0.0).astype(BF16)

    new_state = pl.pallas_call(
        state_kernel,
        out_shape=[jax.ShapeDtypeStruct(master.shape, F32)] * 3,
        in_specs=[VMEM] * len(arrived),
        out_specs=[VMEM] * 3,
        compiler_params=params(16),
        cost_estimate=cost(20 * outer * inner * width, 10 * MIB),
        name="new_state",
    )(after(arrived[0], shares), *arrived[1:])

    far = cross(gathered[1], 1)
    early = list(gathered)
    early = early + [swap(x, 1) for x in early]
    kinds = [(i, 0, i % 3, i // 3) for i in range(6)]
    whole_shape = jax.ShapeDtypeStruct((n * outer, inner, width), BF16)
    placed = place(kinds, early, outer, whole_shape, "place_near")
    far = after(far, v_long, new_state[0], early[3])
    next_weight = place([(0, 0, 3, 0), (1, 0, 3, 1)], [far, swap(far, 1)], outer, placed, "place_far")
    return (v_long, *new_state, next_weight)


def solution(mesh):
    placed = (
        P("dp", None, "tensor"),
        P("dp", None),
        P("tensor", "dp", None),
        P("tensor", None),
        P("dp"),
        P("tensor"),
        P("dp", "tensor", None),
        P("dp", "tensor", None),
        P("dp", "tensor", None),
    )
    return jax.shard_map(
        body,
        mesh=mesh,
        in_specs=placed,
        out_specs=(
            P(("dp", "tensor"), None),
            P("dp", "tensor", None),
            P("dp", "tensor", None),
            P("dp", "tensor", None),
            P(None, "tensor", None),
        ),
        check_vma=False,
    )
```

```python
import functools

import jax
import jax.numpy as jnp
from jax import lax
from jax.experimental import pallas as pl
from jax.experimental.pallas import tpu as pltpu
from jax.sharding import PartitionSpec as P

BF16 = jnp.bfloat16
F32 = jnp.float32
MIB = 1 << 20
VMEM = pl.BlockSpec(memory_space=pltpu.VMEM)
SMEM = pl.BlockSpec(memory_space=pltpu.SMEM)
ANY = pl.BlockSpec(memory_space=pl.ANY)
HBM = pl.BlockSpec(memory_space=pltpu.HBM)


def contract_rows(left, right):
    return lax.dot_general(
        left, right, (((0,), (0,)), ((), ())), preferred_element_type=jnp.float32
    )


def adam(master, moment1, moment2, grad):
    new_moment1 = 0.9 * moment1 + 0.1 * grad
    new_moment2 = 0.999 * moment2 + 0.001 * grad * grad
    first_corr = 1.0 - 0.9**10
    second_corr = 1.0 - 0.999**10
    update = new_moment1 / first_corr / (jnp.sqrt(new_moment2 / second_corr) + 1e-08)
    new_master = master - 0.01 * (update + 0.1 * master)
    return new_master, new_moment1, new_moment2


def plain_body(x_long, dv_long, x_short, dv_short, long_len, short_len, master, moment1, moment2):
    weight_shard = master.astype(BF16)
    long_rows, _, inner_part = x_long.shape
    kv_width = master.shape[2]
    short_rows, outer_part, inner_whole = x_short.shape
    piece = lax.all_gather(weight_shard, "dp", axis=0, tiled=True)
    flat_inputs = x_long.reshape(long_rows, piece.shape[0] * inner_part)
    flat_piece = piece.reshape(piece.shape[0] * inner_part, kv_width)
    partial_values = jnp.dot(flat_inputs, flat_piece, preferred_element_type=F32)
    values = lax.psum_scatter(partial_values, "tensor", scatter_dimension=0, tiled=True)
    own_rows = values.shape[0]
    row_start = lax.axis_index("tensor") * own_rows
    own_live = row_start + jnp.arange(own_rows, dtype=jnp.int32) < long_len[0]
    v_long = jnp.where(own_live[:, None], values, 0.0).astype(BF16)
    long_live = jnp.arange(long_rows, dtype=jnp.int32) < long_len[0]
    short_live = jnp.arange(short_rows, dtype=jnp.int32) < short_len[0]
    live_dv_long = jnp.where(long_live[:, None], dv_long, jnp.zeros_like(dv_long))
    live_dv_short = jnp.where(short_live[:, None], dv_short, jnp.zeros_like(dv_short))
    count = lax.axis_size("dp") * master.shape[0]
    grad_long = lax.psum_scatter(
        contract_rows(flat_inputs, live_dv_long).reshape(count, inner_part, kv_width),
        "dp",
        scatter_dimension=0,
        tiled=True,
    )
    flat_inputs = x_short.reshape(short_rows, outer_part * inner_whole)
    product = contract_rows(flat_inputs, live_dv_short).reshape(outer_part, inner_whole, kv_width)
    grad_short = lax.psum_scatter(product, "tensor", scatter_dimension=1, tiled=True)
    new_master, new_moment1, new_moment2 = adam(master, moment1, moment2, grad_long + grad_short)
    next_weight = lax.all_gather(new_master.astype(BF16), "dp", axis=0, tiled=True)
    return (v_long, new_master, new_moment1, new_moment2, next_weight)


def short_copies(xs_hbm, dvs_hbm, xs_ref, dvs_ref):
    chunks = 4
    chunk = xs_ref.shape[0] // chunks
    spans = [pl.ds(c * chunk, chunk) for c in range(chunks)]
    return [
        (hbm.at[span], ref.at[span])
        for span in spans
        for hbm, ref in ((xs_hbm, xs_ref), (dvs_hbm, dvs_ref))
    ]


def short_block(k, turned, live_dv, out):
    x = turned[lax.bitwise_xor(lax.axis_index("tensor"), jnp.int32(k))]
    prod = jnp.dot(x, live_dv[...], preferred_element_type=F32)
    out[...] = prod.reshape(out.shape).astype(BF16)


def first_kernel(slen_ref, llen_ref, xs_hbm, dvs_hbm, xl_hbm, *refs):
    end_block, turned, live_dv, theirs, xs_ref, dvs_ref, xl_ref, wide, sems = refs
    rows, outer, inner = xs_ref.shape
    chips, owned, _, _ = theirs.shape
    part = inner // 4
    other = 1 - lax.rem(lax.axis_index("dp"), 2)
    pairs = short_copies(xs_hbm, dvs_hbm, xs_ref, dvs_ref)
    short = len(pairs)
    for c in range(chips):
        pairs.append((xl_hbm.at[pl.ds((2 * c + other) * owned, owned)], xl_ref.at[c]))
    copies = [pltpu.make_async_copy(*pair, sems.at[i]) for i, pair in enumerate(pairs)]
    for copy in copies:
        copy.start()
    chunk = rows // (short // 2)
    for c in range(short // 2):
        copies[2 * c].wait()
        copies[2 * c + 1].wait()
        span = slice(c * chunk, (c + 1) * chunk)
        wide[...] = xs_ref[span].reshape(chunk * outer, inner).astype(F32)
        for a in range(outer):
            xa = wide[pl.ds(a, chunk, outer), :].astype(BF16).T
            for j in range(4):
                turned[j, a * part : (a + 1) * part, span] = xa[j * part : (j + 1) * part]
        dv = dvs_ref[span]
        row = lax.broadcasted_iota(jnp.int32, dv.shape, 0) + c * chunk
        live_dv[span] = jnp.where(row < slen_ref[0], dv, jnp.zeros_like(dv))
    short_block(3, turned, live_dv, end_block)
    for c in range(chips):
        copies[short + c].wait()
        x = xl_ref[c]
        row = lax.broadcasted_iota(jnp.int32, x.shape, 2)
        theirs[c] = jnp.where(row < llen_ref[0], x, jnp.zeros_like(x))


def own_kernel(llen_ref, dvl_hbm, master_hbm, *refs):
    live_dv, weight, inside, live_rows, dvl_ref, master_ref, sems = refs
    copies = [
        pltpu.make_async_copy(dvl_hbm, dvl_ref, sems.at[0]),
        pltpu.make_async_copy(master_hbm, master_ref, sems.at[1]),
    ]
    for copy in copies:
        copy.start()
    long_len = llen_ref[0]
    inside[...] = jnp.full(inside.shape, jnp.where(interior(), 1.0, 0.0), F32)
    row = lax.broadcasted_iota(jnp.int32, live_rows.shape, 0)
    row = row + lax.axis_index("tensor") * live_rows.shape[0]
    live_rows[...] = jnp.where(row < long_len, 1.0, 0.0)
    copies[0].wait()
    dv = dvl_ref[...]
    row = lax.broadcasted_iota(jnp.int32, dv.shape, 0)
    live_dv[...] = jnp.where(row < long_len, dv, jnp.zeros_like(dv))
    copies[1].wait()
    weight[...] = master_ref[...].astype(BF16)


def second_kernel(turned, live_dv, *blocks):
    for k in (2, 1, 0):
        short_block(k, turned, live_dv, blocks[k])


def plane_steps():
    core = lax.rem(lax.axis_index("dp"), 2)
    return 0, 1 + core, 2 - core, 3


def long_kernel(x_ref, dv_ref, xs_ref, dvs_ref, *outs):
    chips, outer, inner, rows = xs_ref.shape
    me = lax.axis_index("dp")
    chip, core = me // 2, lax.rem(me, 2)
    for out, rel in reversed(list(zip(outs, plane_steps()))):
        j = lax.bitwise_xor(chip, jnp.int32(rel))
        mine = x_ref[pl.ds((2 * j + core) * outer, outer)].reshape(outer * inner, rows)
        other = xs_ref[j].reshape(outer * inner, rows)
        prod = jnp.dot(mine, dv_ref[...], preferred_element_type=F32)
        prod = prod + jnp.dot(other, dvs_ref[...], preferred_element_type=F32)
        out[...] = prod.reshape(outer, inner, prod.shape[-1]).astype(BF16)


def values_kernel(x_ref, xs_ref, *refs):
    weights, mine_ref, other_ref, acc = refs[:4], refs[-3], refs[-2], refs[-1]
    _, outer, inner, rows = xs_ref.shape
    parts, part, width = mine_ref.shape
    me = lax.axis_index("dp")
    z = lax.axis_index("tensor")
    chip, core = me // 2, lax.rem(me, 2)
    for which, out in ((0, mine_ref), (1, other_ref)):
        total = None
        for weight, rel in zip(weights, plane_steps()):
            j = lax.bitwise_xor(chip, jnp.int32(rel))
            x = xs_ref[j] if which else x_ref[pl.ds((2 * j + core) * outer, outer)]
            w = weight[...].reshape(outer * inner, width)
            term = contract_rows(x.reshape(outer * inner, rows), w)
            total = term if total is None else total + term
        acc[...] = total
        for k in range(parts):
            j = lax.bitwise_xor(z, jnp.int32(k))
            out[k] = acc[pl.ds(pl.multiple_of(j * part, part), part), :].astype(out.dtype)


def update(refs):
    own, near, inside, *terms, master, moment1, moment2 = refs
    grad = own[...].astype(F32) + near[...].astype(F32)
    grad = grad + jnp.where(interior(), inside[...].astype(F32), 0.0)
    for t in terms:
        grad = grad + t[...].astype(F32)
    return adam(master[...], moment1[...], moment2[...], grad)


def weight_kernel(*refs):
    refs[-1][...] = update(refs[:-1])[0].astype(BF16)


def state_kernel(*refs):
    for out, value in zip(refs[-3:], update(refs[:-3])):
        out[...] = value


def place_kernel(kinds, n, outer, *refs):
    pieces, out, sems = refs[:n], refs[-2], refs[-1]
    me = lax.axis_index("dp")
    steps = plane_steps()
    copies = []
    for s, (i, start, step, core) in enumerate(kinds):
        if core and step in (1, 2):
            step = 3 - step
        owner = lax.bitwise_xor(me, 2 * jnp.int32(steps[step]) + core)
        source = pieces[i].at[pl.ds(start, outer)]
        target = out.at[pl.ds(owner * outer, outer)]
        copies.append(pltpu.make_async_copy(source, target, sems.at[s]))
    for copy in copies:
        copy.start()
    for copy in copies:
        copy.wait()


def place(kinds, pieces, outer, whole, name):
    new = isinstance(whole, jax.ShapeDtypeStruct)
    return pl.pallas_call(
        functools.partial(place_kernel, kinds, len(pieces), outer),
        out_shape=jax.ShapeDtypeStruct(whole.shape, whole.dtype),
        in_specs=[VMEM] * len(pieces) + [ANY] * (not new),
        out_specs=ANY,
        scratch_shapes=[pltpu.SemaphoreType.DMA((len(kinds),))],
        input_output_aliases={} if new else {len(pieces): 0},
        compiler_params=params(16),
        cost_estimate=cost(0, 2 * sum(p.size for p in pieces)),
        name=name,
    )(*pieces, *([] if new else [whole]))


def params(mib):
    return pltpu.CompilerParams(vmem_limit_bytes=mib * MIB)


def cost(flops, moved):
    return pl.CostEstimate(flops=flops, bytes_accessed=moved, transcendentals=0)


def swap(x, bit):
    n = lax.axis_size("dp")
    return lax.ppermute(x, "dp", [(i, i ^ bit) for i in range(n)])


def cross(x, turn):
    n = lax.axis_size("dp")
    return lax.ppermute(x, "dp", [(i, i ^ (2 << ((i & 1) ^ turn))) for i in range(n)])


def interior():
    z = lax.axis_index("tensor")
    return (z > 0) & (z < lax.axis_size("tensor") - 1)


def outward(x):
    return lax.ppermute(x, "tensor", [(i, i ^ 1) for i in range(lax.axis_size("tensor"))])


def inward(x):
    n, m = lax.axis_size("tensor"), lax.axis_size("dp")
    pairs = []
    for d in range(m):
        for i in range(n):
            to = (d, i ^ 3) if 0 < i < n - 1 else (d ^ 1, i)
            pairs.append((d * n + i, to[0] * n + to[1]))
    return lax.ppermute(x, ("dp", "tensor"), pairs)


def after(x, *earlier):
    return lax.optimization_barrier((x, *earlier))[0]


def plus(a, b):
    return (a.astype(F32) + b.astype(F32)).astype(BF16)


def body(x_long, dv_long, x_short, dv_short, long_len, short_len, master, moment1, moment2):
    n = lax.axis_size("dp")
    parts = lax.axis_size("tensor")
    outer, inner, width = master.shape
    rows = x_long.shape[0]
    short_rows, _, inner_whole = x_short.shape
    chips = n // 2
    own_rows = rows // parts
    aligned = (
        n & (n - 1) == 0
        and chips == 4
        and parts == 4
        and short_rows % 512 == 0
        and inner % 16 == 0
        and own_rows % 16 == 0
        and rows % 128 == 0
        and short_rows % 128 == 0
        and inner_whole % 128 == 0
        and width % 128 == 0
    )
    if not aligned:
        return plain_body(
            x_long, dv_long, x_short, dv_short, long_len, short_len, master, moment1, moment2
        )
    x_t = jnp.transpose(x_long, (1, 2, 0))
    dv_other = swap(dv_long, 1)
    block = jax.ShapeDtypeStruct((outer, inner, width), BF16)
    end_block, turned, live_dvs, theirs = pl.pallas_call(
        first_kernel,
        out_shape=[
            block,
            jax.ShapeDtypeStruct((4, outer * inner, short_rows), BF16),
            jax.ShapeDtypeStruct(dv_short.shape, BF16),
            jax.ShapeDtypeStruct((chips, outer, inner, rows), BF16),
        ],
        in_specs=[SMEM, SMEM] + [HBM] * 3,
        out_specs=[VMEM] * 4,
        scratch_shapes=[
            pltpu.VMEM(x_short.shape, BF16),
            pltpu.VMEM(dv_short.shape, BF16),
            pltpu.VMEM((chips, outer, inner, rows), BF16),
            pltpu.VMEM((short_rows // 4 * outer, inner_whole), F32),
            pltpu.SemaphoreType.DMA((8 + chips,)),
        ],
        compiler_params=params(50),
        cost_estimate=cost(short_rows * outer * inner_whole * width, 6 * MIB),
        name="first",
    )(short_len, long_len, x_short, dv_short, x_t)
    live_dv, weight, end_mask, row_mask = pl.pallas_call(
        own_kernel,
        out_shape=[
            jax.ShapeDtypeStruct(dv_long.shape, BF16),
            block,
            jax.ShapeDtypeStruct((1, 1, width), F32),
            jax.ShapeDtypeStruct((own_rows, width), F32),
        ],
        in_specs=[SMEM] + [HBM] * 2,
        out_specs=[VMEM] * 4,
        scratch_shapes=[
            pltpu.VMEM(dv_long.shape, BF16),
            pltpu.VMEM(master.shape, F32),
            pltpu.SemaphoreType.DMA((2,)),
        ],
        compiler_params=params(53),
        cost_estimate=cost(0, 3 * MIB),
        name="own",
    )(long_len, dv_long, master)
    blocks = pl.pallas_call(
        second_kernel,
        out_shape=[block] * 3,
        in_specs=[VMEM] * 2,
        out_specs=[VMEM] * 3,
        compiler_params=params(16),
        cost_estimate=cost(short_rows * outer * inner_whole * width, 4 * MIB),
        name="second",
    )(turned, live_dvs)
    blocks = [*blocks, end_block]
    within = end_mask > 0.0
    x_other = swap(theirs, 1)
    from_end = outward(blocks[3])
    second_weight, first_weight = cross(weight, 1), cross(weight, 0)
    long_own, long_first, long_second, long_far = pl.pallas_call(
        long_kernel,
        out_shape=[block] * 4,
        in_specs=[VMEM] * 4,
        out_specs=[VMEM] * 4,
        compiler_params=params(16),
        cost_estimate=cost(4 * rows * chips * outer * inner * width, 4 * MIB),
        name="long_grad",
    )(x_t, live_dv, x_other, dv_other)

    far_sum = cross(long_far, 1)
    middle = outward(after(blocks[2], long_own))
    across_sent = plus(after(blocks[2], long_own), from_end)
    across = inward(across_sent)
    second_sum = cross(after(long_second, across_sent), 1)
    first_sent = plus(long_first, far_sum)
    first_sum = cross(first_sent, 0)
    handed = after(second_weight, first_weight, first_sent)
    far_weight = cross(handed, 0)
    inside_sent = plus(after(blocks[3], handed), middle)
    inside = inward(inside_sent)
    across = after(across, inside_sent)
    near_sent = plus(blocks[1], jnp.where(within, across, jnp.zeros_like(across)))
    near = outward(near_sent)

    mine, other = pl.pallas_call(
        values_kernel,
        out_shape=[jax.ShapeDtypeStruct((parts, own_rows, width), t) for t in (F32, BF16)],
        in_specs=[VMEM] * 6,
        out_specs=[VMEM] * 2,
        scratch_shapes=[pltpu.VMEM((rows, width), F32)],
        compiler_params=params(16),
        cost_estimate=cost(4 * rows * chips * outer * inner * width, 6 * MIB),
        name="values",
    )(x_t, x_other, weight, first_weight, second_weight, far_weight)

    arrived = [after(blocks[0], mine), near, inside, long_own, second_sum, first_sum]
    arrived += [master, moment1, moment2]
    next_shard = pl.pallas_call(
        weight_kernel,
        out_shape=block,
        in_specs=[VMEM] * len(arrived),
        out_specs=VMEM,
        compiler_params=params(16),
        cost_estimate=cost(20 * outer * inner * width, 5 * MIB),
        name="next_weight",
    )(*arrived)

    gathered = [next_shard, cross(next_shard, 0), cross(next_shard, 1)]

    total = mine + after(swap(other, 1), next_shard).astype(F32)
    shares = total.astype(BF16)
    v_across_sent = plus(shares[2], outward(shares[3]))
    v_across = inward(v_across_sent)
    v_middle = outward(after(shares[2], v_across_sent))
    v_near = plus(shares[1], jnp.where(within[0], v_across, jnp.zeros_like(v_across)))
    v_inside = plus(shares[3], v_middle)
    values = total[0] + outward(v_near).astype(F32)
    values = values + jnp.where(within[0], inward(v_inside).astype(F32), 0.0)
    v_long = jnp.where(row_mask > 0.0, values, 0.0).astype(BF16)

    new_state = pl.pallas_call(
        state_kernel,
        out_shape=[jax.ShapeDtypeStruct(master.shape, F32)] * 3,
        in_specs=[VMEM] * len(arrived),
        out_specs=[VMEM] * 3,
        compiler_params=params(16),
        cost_estimate=cost(20 * outer * inner * width, 10 * MIB),
        name="new_state",
    )(after(arrived[0], shares), *arrived[1:])

    far = cross(gathered[1], 1)
    early = list(gathered)
    early = early + [swap(x, 1) for x in early]
    kinds = [(i, 0, i % 3, i // 3) for i in range(6)]
    whole_shape = jax.ShapeDtypeStruct((n * outer, inner, width), BF16)
    placed = place(kinds, early, outer, whole_shape, "place_near")
    far = after(far, v_long, new_state[0], early[3])
    next_weight = place([(0, 0, 3, 0), (1, 0, 3, 1)], [far, swap(far, 1)], outer, placed, "place_far")
    return (v_long, *new_state, next_weight)


def solution(mesh):
    placed = (
        P("dp", None, "tensor"),
        P("dp", None),
        P("tensor", "dp", None),
        P("tensor", None),
        P("dp"),
        P("tensor"),
        P("dp", "tensor", None),
        P("dp", "tensor", None),
        P("dp", "tensor", None),
    )
    return jax.shard_map(
        body,
        mesh=mesh,
        in_specs=placed,
        out_specs=(
            P(("dp", "tensor"), None),
            P("dp", "tensor", None),
            P("dp", "tensor", None),
            P("dp", "tensor", None),
            P(None, "tensor", None),
        ),
        check_vma=False,
    )
```

```python
import functools

import jax
import jax.numpy as jnp
from jax import lax
from jax.experimental import pallas as pl
from jax.experimental.pallas import tpu as pltpu
from jax.sharding import PartitionSpec as P

BF16 = jnp.bfloat16
F32 = jnp.float32
MIB = 1 << 20
VMEM = pl.BlockSpec(memory_space=pltpu.VMEM)
SMEM = pl.BlockSpec(memory_space=pltpu.SMEM)
ANY = pl.BlockSpec(memory_space=pl.ANY)
HBM = pl.BlockSpec(memory_space=pltpu.HBM)


def contract_rows(left, right):
    return lax.dot_general(
        left, right, (((0,), (0,)), ((), ())), preferred_element_type=jnp.float32
    )


def adam(master, moment1, moment2, grad):
    new_moment1 = 0.9 * moment1 + 0.1 * grad
    new_moment2 = 0.999 * moment2 + 0.001 * grad * grad
    first_corr = 1.0 - 0.9**10
    second_corr = 1.0 - 0.999**10
    update = new_moment1 / first_corr / (jnp.sqrt(new_moment2 / second_corr) + 1e-08)
    new_master = master - 0.01 * (update + 0.1 * master)
    return new_master, new_moment1, new_moment2


def plain_body(x_long, dv_long, x_short, dv_short, long_len, short_len, master, moment1, moment2):
    weight_shard = master.astype(BF16)
    long_rows, _, inner_part = x_long.shape
    kv_width = master.shape[2]
    short_rows, outer_part, inner_whole = x_short.shape
    piece = lax.all_gather(weight_shard, "dp", axis=0, tiled=True)
    flat_inputs = x_long.reshape(long_rows, piece.shape[0] * inner_part)
    flat_piece = piece.reshape(piece.shape[0] * inner_part, kv_width)
    partial_values = jnp.dot(flat_inputs, flat_piece, preferred_element_type=F32)
    values = lax.psum_scatter(partial_values, "tensor", scatter_dimension=0, tiled=True)
    own_rows = values.shape[0]
    row_start = lax.axis_index("tensor") * own_rows
    own_live = row_start + jnp.arange(own_rows, dtype=jnp.int32) < long_len[0]
    v_long = jnp.where(own_live[:, None], values, 0.0).astype(BF16)
    long_live = jnp.arange(long_rows, dtype=jnp.int32) < long_len[0]
    short_live = jnp.arange(short_rows, dtype=jnp.int32) < short_len[0]
    live_dv_long = jnp.where(long_live[:, None], dv_long, jnp.zeros_like(dv_long))
    live_dv_short = jnp.where(short_live[:, None], dv_short, jnp.zeros_like(dv_short))
    count = lax.axis_size("dp") * master.shape[0]
    grad_long = lax.psum_scatter(
        contract_rows(flat_inputs, live_dv_long).reshape(count, inner_part, kv_width),
        "dp",
        scatter_dimension=0,
        tiled=True,
    )
    flat_inputs = x_short.reshape(short_rows, outer_part * inner_whole)
    product = contract_rows(flat_inputs, live_dv_short).reshape(outer_part, inner_whole, kv_width)
    grad_short = lax.psum_scatter(product, "tensor", scatter_dimension=1, tiled=True)
    new_master, new_moment1, new_moment2 = adam(master, moment1, moment2, grad_long + grad_short)
    next_weight = lax.all_gather(new_master.astype(BF16), "dp", axis=0, tiled=True)
    return (v_long, new_master, new_moment1, new_moment2, next_weight)


def first_kernel(slen_hbm, llen_hbm, xs_hbm, dvs_hbm, xl_hbm, dvl_hbm, master_hbm, *refs):
    blocks, theirs, live_dv, weight, inside, live_rows = refs[:4], *refs[4:9]
    slen_ref, llen_ref, xs_ref, dvs_ref, xl_ref, dvl_ref, master_ref, wide, turned, sems = refs[9:]
    rows, outer, inner = xs_ref.shape
    chips, owned, _, long_rows = theirs.shape
    chunks = 4
    chunk = rows // chunks
    part = inner // 4
    z = lax.axis_index("tensor")
    other = 1 - lax.rem(lax.axis_index("dp"), 2)
    pairs = []
    for c in range(chunks):
        span = pl.ds(c * chunk, chunk)
        pairs.append((xs_hbm.at[span], xs_ref.at[span]))
        pairs.append((dvs_hbm.at[span], dvs_ref.at[span]))
    for c in range(chips):
        pairs.append((xl_hbm.at[pl.ds((2 * c + other) * owned, owned)], xl_ref.at[c]))
    pairs.append((dvl_hbm, dvl_ref))
    pairs.append((master_hbm, master_ref))
    pairs.append((llen_hbm, llen_ref))
    pairs.append((slen_hbm, slen_ref))
    copies = [pltpu.make_async_copy(*pair, sems.at[i]) for i, pair in enumerate(pairs)]
    for copy in copies[-2:] + copies[: 2 * chunks]:
        copy.start()
    copies[-1].wait()
    for c in range(chunks):
        copies[2 * c].wait()
        copies[2 * c + 1].wait()
        if c == 0:
            for copy in copies[2 * chunks : -2]:
                copy.start()
        span = slice(c * chunk, (c + 1) * chunk)
        wide[...] = xs_ref[span].reshape(chunk * outer, inner).astype(F32)
        for a in range(outer):
            xa = wide[pl.ds(a, chunk, outer), :].astype(BF16).T
            for j in range(4):
                k = lax.bitwise_xor(z, jnp.int32(j))
                turned[k, a * part : (a + 1) * part, span] = xa[j * part : (j + 1) * part]
        dv = dvs_ref[span]
        row = lax.broadcasted_iota(jnp.int32, dv.shape, 0) + c * chunk
        dvs_ref[span] = jnp.where(row < slen_ref[0], dv, jnp.zeros_like(dv))
    x = turned[...].reshape(4 * outer * part, rows)
    prod = jnp.dot(x, dvs_ref[...], preferred_element_type=F32)
    prod = prod.reshape(4, outer, part, prod.shape[1])
    for k in range(4):
        blocks[k][...] = prod[k].astype(BF16)
    copies[-2].wait()
    long_len = llen_ref[0]
    for c in range(chips):
        copies[2 * chunks + c].wait()
        x = xl_ref[c]
        row = lax.broadcasted_iota(jnp.int32, x.shape, 2)
        theirs[c] = jnp.where(row < long_len, x, jnp.zeros_like(x))
    copies[-4].wait()
    dv = dvl_ref[...]
    row = lax.broadcasted_iota(jnp.int32, dv.shape, 0)
    live_dv[...] = jnp.where(row < long_len, dv, jnp.zeros_like(dv))
    copies[-3].wait()
    weight[...] = master_ref[...].astype(BF16)
    within = jnp.where(interior(), 1.0, 0.0)
    inside[...] = jnp.full(inside.shape, within, F32)
    row = lax.broadcasted_iota(jnp.int32, live_rows.shape, 0) + z * live_rows.shape[0]
    live_rows[...] = jnp.where(row < long_len, 1.0, 0.0)


def plane_steps():
    core = lax.rem(lax.axis_index("dp"), 2)
    return 0, 1 + core, 2 - core, 3


def long_kernel(x_ref, dv_ref, xs_ref, dvs_ref, *outs):
    chips, outer, inner, rows = xs_ref.shape
    me = lax.axis_index("dp")
    chip, core = me // 2, lax.rem(me, 2)
    for out, rel in reversed(list(zip(outs, plane_steps()))):
        j = lax.bitwise_xor(chip, jnp.int32(rel))
        mine = x_ref[pl.ds((2 * j + core) * outer, outer)].reshape(outer * inner, rows)
        other = xs_ref[j].reshape(outer * inner, rows)
        prod = jnp.dot(mine, dv_ref[...], preferred_element_type=F32)
        prod = prod + jnp.dot(other, dvs_ref[...], preferred_element_type=F32)
        out[...] = prod.reshape(outer, inner, prod.shape[-1]).astype(BF16)


def values_kernel(x_ref, xs_ref, *refs):
    weights, mine_ref, other_ref, acc = refs[:4], refs[-3], refs[-2], refs[-1]
    _, outer, inner, rows = xs_ref.shape
    parts, part, width = mine_ref.shape
    me = lax.axis_index("dp")
    z = lax.axis_index("tensor")
    chip, core = me // 2, lax.rem(me, 2)
    for which, out in ((0, mine_ref), (1, other_ref)):
        total = None
        for weight, rel in zip(weights, plane_steps()):
            j = lax.bitwise_xor(chip, jnp.int32(rel))
            x = xs_ref[j] if which else x_ref[pl.ds((2 * j + core) * outer, outer)]
            w = weight[...].reshape(outer * inner, width)
            term = contract_rows(x.reshape(outer * inner, rows), w)
            total = term if total is None else total + term
        acc[...] = total
        for k in range(parts):
            j = lax.bitwise_xor(z, jnp.int32(k))
            out[k] = acc[pl.ds(pl.multiple_of(j * part, part), part), :].astype(out.dtype)


def update(refs):
    own, near, inside, *terms, master, moment1, moment2 = refs
    grad = own[...].astype(F32) + near[...].astype(F32)
    grad = grad + jnp.where(interior(), inside[...].astype(F32), 0.0)
    for t in terms:
        grad = grad + t[...].astype(F32)
    return adam(master[...], moment1[...], moment2[...], grad)


def weight_kernel(*refs):
    refs[-1][...] = update(refs[:-1])[0].astype(BF16)


def state_kernel(*refs):
    for out, value in zip(refs[-3:], update(refs[:-3])):
        out[...] = value


def place_kernel(kinds, n, outer, *refs):
    pieces, out, sems = refs[:n], refs[-2], refs[-1]
    me = lax.axis_index("dp")
    steps = plane_steps()
    copies = []
    for s, (i, start, step, core) in enumerate(kinds):
        if core and step in (1, 2):
            step = 3 - step
        owner = lax.bitwise_xor(me, 2 * jnp.int32(steps[step]) + core)
        source = pieces[i].at[pl.ds(start, outer)]
        target = out.at[pl.ds(owner * outer, outer)]
        copies.append(pltpu.make_async_copy(source, target, sems.at[s]))
    for copy in copies:
        copy.start()
    for copy in copies:
        copy.wait()


def place(kinds, pieces, outer, whole, name):
    new = isinstance(whole, jax.ShapeDtypeStruct)
    return pl.pallas_call(
        functools.partial(place_kernel, kinds, len(pieces), outer),
        out_shape=jax.ShapeDtypeStruct(whole.shape, whole.dtype),
        in_specs=[VMEM] * len(pieces) + [ANY] * (not new),
        out_specs=ANY,
        scratch_shapes=[pltpu.SemaphoreType.DMA((len(kinds),))],
        input_output_aliases={} if new else {len(pieces): 0},
        compiler_params=params(16),
        cost_estimate=cost(0, 2 * sum(p.size for p in pieces)),
        name=name,
    )(*pieces, *([] if new else [whole]))


def params(mib):
    return pltpu.CompilerParams(vmem_limit_bytes=mib * MIB)


def cost(flops, moved):
    return pl.CostEstimate(flops=flops, bytes_accessed=moved, transcendentals=0)


def swap(x, bit):
    n = lax.axis_size("dp")
    return lax.ppermute(x, "dp", [(i, i ^ bit) for i in range(n)])


def cross(x, turn):
    n = lax.axis_size("dp")
    return lax.ppermute(x, "dp", [(i, i ^ (2 << ((i & 1) ^ turn))) for i in range(n)])


def interior():
    z = lax.axis_index("tensor")
    return (z > 0) & (z < lax.axis_size("tensor") - 1)


def outward(x):
    return lax.ppermute(x, "tensor", [(i, i ^ 1) for i in range(lax.axis_size("tensor"))])


def inward(x):
    n, m = lax.axis_size("tensor"), lax.axis_size("dp")
    pairs = []
    for d in range(m):
        for i in range(n):
            to = (d, i ^ 3) if 0 < i < n - 1 else (d ^ 1, i)
            pairs.append((d * n + i, to[0] * n + to[1]))
    return lax.ppermute(x, ("dp", "tensor"), pairs)


def after(x, *earlier):
    return lax.optimization_barrier((x, *earlier))[0]


def plus(a, b):
    return (a.astype(F32) + b.astype(F32)).astype(BF16)


def body(x_long, dv_long, x_short, dv_short, long_len, short_len, master, moment1, moment2):
    n = lax.axis_size("dp")
    parts = lax.axis_size("tensor")
    outer, inner, width = master.shape
    rows = x_long.shape[0]
    short_rows, _, inner_whole = x_short.shape
    chips = n // 2
    own_rows = rows // parts
    aligned = (
        n & (n - 1) == 0
        and chips == 4
        and parts == 4
        and short_rows % 512 == 0
        and inner % 16 == 0
        and own_rows % 16 == 0
        and rows % 128 == 0
        and short_rows % 128 == 0
        and inner_whole % 128 == 0
        and width % 128 == 0
    )
    if not aligned:
        return plain_body(
            x_long, dv_long, x_short, dv_short, long_len, short_len, master, moment1, moment2
        )
    x_t = jnp.transpose(x_long, (1, 2, 0))
    dv_other = swap(dv_long, 1)
    block = jax.ShapeDtypeStruct((outer, inner, width), BF16)
    *blocks, theirs, live_dv, weight, end_mask, row_mask = pl.pallas_call(
        first_kernel,
        out_shape=[
            *[block] * 4,
            jax.ShapeDtypeStruct((chips, outer, inner, rows), BF16),
            jax.ShapeDtypeStruct(dv_long.shape, BF16),
            block,
            jax.ShapeDtypeStruct((1, 1, width), F32),
            jax.ShapeDtypeStruct((own_rows, width), F32),
        ],
        in_specs=[HBM] * 7,
        out_specs=[VMEM] * 9,
        scratch_shapes=[
            pltpu.SMEM((1,), jnp.int32),
            pltpu.SMEM((1,), jnp.int32),
            pltpu.VMEM(x_short.shape, BF16),
            pltpu.VMEM(dv_short.shape, BF16),
            pltpu.VMEM((chips, outer, inner, rows), BF16),
            pltpu.VMEM(dv_long.shape, BF16),
            pltpu.VMEM(master.shape, F32),
            pltpu.VMEM((short_rows // 4 * outer, inner_whole), F32),
            pltpu.VMEM((4, outer * inner, short_rows), BF16),
            pltpu.SemaphoreType.DMA((12 + chips,)),
        ],
        compiler_params=params(50),
        cost_estimate=cost(2 * short_rows * outer * inner_whole * width, 8 * MIB),
        name="first",
    )(short_len, long_len, x_short, dv_short, x_t, dv_long, master)
    within = end_mask > 0.0
    x_other = swap(theirs, 1)
    from_end = outward(blocks[3])
    second_weight, first_weight = cross(weight, 1), cross(weight, 0)
    long_own, long_first, long_second, long_far = pl.pallas_call(
        long_kernel,
        out_shape=[block] * 4,
        in_specs=[VMEM] * 4,
        out_specs=[VMEM] * 4,
        compiler_params=params(16),
        cost_estimate=cost(4 * rows * chips * outer * inner * width, 4 * MIB),
        name="long_grad",
    )(x_t, live_dv, x_other, dv_other)

    far_sum = cross(long_far, 1)
    second_sum = cross(long_second, 1)
    middle = outward(after(blocks[2], long_own))
    across_sent = plus(after(blocks[2], long_own), from_end)
    across = inward(across_sent)
    first_sent = plus(long_first, far_sum)
    first_sum = cross(first_sent, 0)
    handed = after(second_weight, first_weight, first_sent)
    far_weight = cross(handed, 0)
    inside_sent = plus(after(blocks[3], handed), middle)
    inside = inward(inside_sent)
    across = after(across, inside_sent)
    near_sent = plus(blocks[1], jnp.where(within, across, jnp.zeros_like(across)))
    near = outward(near_sent)

    mine, other = pl.pallas_call(
        values_kernel,
        out_shape=[jax.ShapeDtypeStruct((parts, own_rows, width), t) for t in (F32, BF16)],
        in_specs=[VMEM] * 6,
        out_specs=[VMEM] * 2,
        scratch_shapes=[pltpu.VMEM((rows, width), F32)],
        compiler_params=params(16),
        cost_estimate=cost(4 * rows * chips * outer * inner * width, 6 * MIB),
        name="values",
    )(x_t, x_other, weight, first_weight, second_weight, far_weight)

    arrived = [after(blocks[0], mine), near, inside, long_own, second_sum, first_sum]
    arrived += [master, moment1, moment2]
    next_shard = pl.pallas_call(
        weight_kernel,
        out_shape=block,
        in_specs=[VMEM] * len(arrived),
        out_specs=VMEM,
        compiler_params=params(16),
        cost_estimate=cost(20 * outer * inner * width, 5 * MIB),
        name="next_weight",
    )(*arrived)

    gathered = [next_shard, cross(next_shard, 0), cross(next_shard, 1)]

    total = mine + after(swap(other, 1), next_shard).astype(F32)
    shares = total.astype(BF16)
    v_across_sent = plus(shares[2], outward(shares[3]))
    v_across = inward(v_across_sent)
    v_middle = outward(after(shares[2], v_across_sent))
    v_near = plus(shares[1], jnp.where(within[0], v_across, jnp.zeros_like(v_across)))
    v_inside = plus(shares[3], v_middle)
    values = total[0] + outward(v_near).astype(F32)
    values = values + jnp.where(within[0], inward(v_inside).astype(F32), 0.0)
    v_long = jnp.where(row_mask > 0.0, values, 0.0).astype(BF16)

    new_state = pl.pallas_call(
        state_kernel,
        out_shape=[jax.ShapeDtypeStruct(master.shape, F32)] * 3,
        in_specs=[VMEM] * len(arrived),
        out_specs=[VMEM] * 3,
        compiler_params=params(16),
        cost_estimate=cost(20 * outer * inner * width, 10 * MIB),
        name="new_state",
    )(after(arrived[0], shares), *arrived[1:])

    far = cross(gathered[1], 1)
    early = list(gathered)
    early = early + [swap(x, 1) for x in early]
    kinds = [(i, 0, i % 3, i // 3) for i in range(6)]
    whole_shape = jax.ShapeDtypeStruct((n * outer, inner, width), BF16)
    placed = place(kinds, early, outer, whole_shape, "place_near")
    far = after(far, v_long, new_state[0], early[3])
    next_weight = place([(0, 0, 3, 0), (1, 0, 3, 1)], [far, swap(far, 1)], outer, placed, "place_far")
    return (v_long, *new_state, next_weight)


def solution(mesh):
    placed = (
        P("dp", None, "tensor"),
        P("dp", None),
        P("tensor", "dp", None),
        P("tensor", None),
        P("dp"),
        P("tensor"),
        P("dp", "tensor", None),
        P("dp", "tensor", None),
        P("dp", "tensor", None),
    )
    return jax.shard_map(
        body,
        mesh=mesh,
        in_specs=placed,
        out_specs=(
            P(("dp", "tensor"), None),
            P("dp", "tensor", None),
            P("dp", "tensor", None),
            P("dp", "tensor", None),
            P(None, "tensor", None),
        ),
        check_vma=False,
    )
```

```python
import functools

import jax
import jax.numpy as jnp
from jax import lax
from jax.experimental import pallas as pl
from jax.experimental.pallas import tpu as pltpu
from jax.sharding import PartitionSpec as P

BF16 = jnp.bfloat16
F32 = jnp.float32
MIB = 1 << 20
VMEM = pl.BlockSpec(memory_space=pltpu.VMEM)
SMEM = pl.BlockSpec(memory_space=pltpu.SMEM)
ANY = pl.BlockSpec(memory_space=pl.ANY)
HBM = pl.BlockSpec(memory_space=pltpu.HBM)


def contract_rows(left, right):
    return lax.dot_general(
        left, right, (((0,), (0,)), ((), ())), preferred_element_type=jnp.float32
    )


def adam(master, moment1, moment2, grad):
    new_moment1 = 0.9 * moment1 + 0.1 * grad
    new_moment2 = 0.999 * moment2 + 0.001 * grad * grad
    first_corr = 1.0 - 0.9**10
    second_corr = 1.0 - 0.999**10
    update = new_moment1 / first_corr / (jnp.sqrt(new_moment2 / second_corr) + 1e-08)
    new_master = master - 0.01 * (update + 0.1 * master)
    return new_master, new_moment1, new_moment2


def plain_body(x_long, dv_long, x_short, dv_short, long_len, short_len, master, moment1, moment2):
    weight_shard = master.astype(BF16)
    long_rows, _, inner_part = x_long.shape
    kv_width = master.shape[2]
    short_rows, outer_part, inner_whole = x_short.shape
    piece = lax.all_gather(weight_shard, "dp", axis=0, tiled=True)
    flat_inputs = x_long.reshape(long_rows, piece.shape[0] * inner_part)
    flat_piece = piece.reshape(piece.shape[0] * inner_part, kv_width)
    partial_values = jnp.dot(flat_inputs, flat_piece, preferred_element_type=F32)
    values = lax.psum_scatter(partial_values, "tensor", scatter_dimension=0, tiled=True)
    own_rows = values.shape[0]
    row_start = lax.axis_index("tensor") * own_rows
    own_live = row_start + jnp.arange(own_rows, dtype=jnp.int32) < long_len[0]
    v_long = jnp.where(own_live[:, None], values, 0.0).astype(BF16)
    long_live = jnp.arange(long_rows, dtype=jnp.int32) < long_len[0]
    short_live = jnp.arange(short_rows, dtype=jnp.int32) < short_len[0]
    live_dv_long = jnp.where(long_live[:, None], dv_long, jnp.zeros_like(dv_long))
    live_dv_short = jnp.where(short_live[:, None], dv_short, jnp.zeros_like(dv_short))
    count = lax.axis_size("dp") * master.shape[0]
    grad_long = lax.psum_scatter(
        contract_rows(flat_inputs, live_dv_long).reshape(count, inner_part, kv_width),
        "dp",
        scatter_dimension=0,
        tiled=True,
    )
    flat_inputs = x_short.reshape(short_rows, outer_part * inner_whole)
    product = contract_rows(flat_inputs, live_dv_short).reshape(outer_part, inner_whole, kv_width)
    grad_short = lax.psum_scatter(product, "tensor", scatter_dimension=1, tiled=True)
    new_master, new_moment1, new_moment2 = adam(master, moment1, moment2, grad_long + grad_short)
    next_weight = lax.all_gather(new_master.astype(BF16), "dp", axis=0, tiled=True)
    return (v_long, new_master, new_moment1, new_moment2, next_weight)


def first_kernel(slen_hbm, llen_hbm, xs_hbm, dvs_hbm, xl_hbm, dvl_hbm, *refs):
    blocks, theirs, live_dv, inside, live_rows = refs[:4], *refs[4:8]
    slen_ref, llen_ref, xs_ref, dvs_ref, xl_ref, dvl_ref, wide, turned, sems = refs[8:]
    rows, outer, inner = xs_ref.shape
    chips, owned, _, long_rows = theirs.shape
    chunks = 4
    chunk = rows // chunks
    part = inner // 4
    z = lax.axis_index("tensor")
    other = 1 - lax.rem(lax.axis_index("dp"), 2)
    pairs = []
    for c in range(chunks):
        span = pl.ds(c * chunk, chunk)
        pairs.append((xs_hbm.at[span], xs_ref.at[span]))
        pairs.append((dvs_hbm.at[span], dvs_ref.at[span]))
    for c in range(chips):
        pairs.append((xl_hbm.at[pl.ds((2 * c + other) * owned, owned)], xl_ref.at[c]))
    pairs.append((dvl_hbm, dvl_ref))
    pairs.append((llen_hbm, llen_ref))
    pairs.append((slen_hbm, slen_ref))
    copies = [pltpu.make_async_copy(*pair, sems.at[i]) for i, pair in enumerate(pairs)]
    for copy in copies[-2:] + copies[:-2]:
        copy.start()
    copies[-1].wait()
    for c in range(chunks):
        copies[2 * c].wait()
        copies[2 * c + 1].wait()
        span = slice(c * chunk, (c + 1) * chunk)
        wide[...] = xs_ref[span].reshape(chunk * outer, inner).astype(F32)
        for a in range(outer):
            xa = wide[pl.ds(a, chunk, outer), :].astype(BF16).T
            for j in range(4):
                turned[j, a * part : (a + 1) * part, span] = xa[j * part : (j + 1) * part]
        dv = dvs_ref[span]
        row = lax.broadcasted_iota(jnp.int32, dv.shape, 0) + c * chunk
        dvs_ref[span] = jnp.where(row < slen_ref[0], dv, jnp.zeros_like(dv))
    for k in (3, 2, 1, 0):
        x = turned[lax.bitwise_xor(z, jnp.int32(k))]
        prod = jnp.dot(x, dvs_ref[...], preferred_element_type=F32)
        blocks[k][...] = prod.reshape(outer, part, prod.shape[1]).astype(BF16)
    copies[-2].wait()
    long_len = llen_ref[0]
    for c in range(chips):
        copies[2 * chunks + c].wait()
        x = xl_ref[c]
        row = lax.broadcasted_iota(jnp.int32, x.shape, 2)
        theirs[c] = jnp.where(row < long_len, x, jnp.zeros_like(x))
    copies[-3].wait()
    dv = dvl_ref[...]
    row = lax.broadcasted_iota(jnp.int32, dv.shape, 0)
    live_dv[...] = jnp.where(row < long_len, dv, jnp.zeros_like(dv))
    within = jnp.where(interior(), 1.0, 0.0)
    inside[...] = jnp.full(inside.shape, within, F32)
    row = lax.broadcasted_iota(jnp.int32, live_rows.shape, 0) + z * live_rows.shape[0]
    live_rows[...] = jnp.where(row < long_len, 1.0, 0.0)


def plane_steps():
    core = lax.rem(lax.axis_index("dp"), 2)
    return 0, 1 + core, 2 - core, 3


def long_kernel(x_ref, dv_ref, xs_ref, dvs_ref, master_hbm, *refs):
    outs, weight, master_ref, sem = refs[:4], *refs[4:]
    copy = pltpu.make_async_copy(master_hbm, master_ref, sem)
    copy.start()
    chips, outer, inner, rows = xs_ref.shape
    me = lax.axis_index("dp")
    chip, core = me // 2, lax.rem(me, 2)
    for out, rel in reversed(list(zip(outs, plane_steps()))):
        j = lax.bitwise_xor(chip, jnp.int32(rel))
        mine = x_ref[pl.ds((2 * j + core) * outer, outer)].reshape(outer * inner, rows)
        other = xs_ref[j].reshape(outer * inner, rows)
        prod = jnp.dot(mine, dv_ref[...], preferred_element_type=F32)
        prod = prod + jnp.dot(other, dvs_ref[...], preferred_element_type=F32)
        out[...] = prod.reshape(outer, inner, prod.shape[-1]).astype(BF16)
    copy.wait()
    weight[...] = master_ref[...].astype(BF16)


def values_kernel(x_ref, xs_ref, *refs):
    weights, mine_ref, other_ref, acc = refs[:4], refs[-3], refs[-2], refs[-1]
    _, outer, inner, rows = xs_ref.shape
    parts, part, width = mine_ref.shape
    me = lax.axis_index("dp")
    z = lax.axis_index("tensor")
    chip, core = me // 2, lax.rem(me, 2)
    for which, out in ((0, mine_ref), (1, other_ref)):
        total = None
        for weight, rel in zip(weights, plane_steps()):
            j = lax.bitwise_xor(chip, jnp.int32(rel))
            x = xs_ref[j] if which else x_ref[pl.ds((2 * j + core) * outer, outer)]
            w = weight[...].reshape(outer * inner, width)
            term = contract_rows(x.reshape(outer * inner, rows), w)
            total = term if total is None else total + term
        acc[...] = total
        for k in range(parts):
            j = lax.bitwise_xor(z, jnp.int32(k))
            out[k] = acc[pl.ds(pl.multiple_of(j * part, part), part), :].astype(out.dtype)


def update(refs):
    own, near, inside, *terms, master, moment1, moment2 = refs
    grad = own[...].astype(F32) + near[...].astype(F32)
    grad = grad + jnp.where(interior(), inside[...].astype(F32), 0.0)
    for t in terms:
        grad = grad + t[...].astype(F32)
    return adam(master[...], moment1[...], moment2[...], grad)


def weight_kernel(*refs):
    refs[-1][...] = update(refs[:-1])[0].astype(BF16)


def state_kernel(*refs):
    for out, value in zip(refs[-3:], update(refs[:-3])):
        out[...] = value


def place_kernel(kinds, n, outer, *refs):
    pieces, out, sems = refs[:n], refs[-2], refs[-1]
    me = lax.axis_index("dp")
    steps = plane_steps()
    copies = []
    for s, (i, start, step, core) in enumerate(kinds):
        if core and step in (1, 2):
            step = 3 - step
        owner = lax.bitwise_xor(me, 2 * jnp.int32(steps[step]) + core)
        source = pieces[i].at[pl.ds(start, outer)]
        target = out.at[pl.ds(owner * outer, outer)]
        copies.append(pltpu.make_async_copy(source, target, sems.at[s]))
    for copy in copies:
        copy.start()
    for copy in copies:
        copy.wait()


def place(kinds, pieces, outer, whole, name):
    new = isinstance(whole, jax.ShapeDtypeStruct)
    return pl.pallas_call(
        functools.partial(place_kernel, kinds, len(pieces), outer),
        out_shape=jax.ShapeDtypeStruct(whole.shape, whole.dtype),
        in_specs=[VMEM] * len(pieces) + [ANY] * (not new),
        out_specs=ANY,
        scratch_shapes=[pltpu.SemaphoreType.DMA((len(kinds),))],
        input_output_aliases={} if new else {len(pieces): 0},
        compiler_params=params(16),
        cost_estimate=cost(0, 2 * sum(p.size for p in pieces)),
        name=name,
    )(*pieces, *([] if new else [whole]))


def params(mib):
    return pltpu.CompilerParams(vmem_limit_bytes=mib * MIB)


def cost(flops, moved):
    return pl.CostEstimate(flops=flops, bytes_accessed=moved, transcendentals=0)


def swap(x, bit):
    n = lax.axis_size("dp")
    return lax.ppermute(x, "dp", [(i, i ^ bit) for i in range(n)])


def cross(x, turn):
    n = lax.axis_size("dp")
    return lax.ppermute(x, "dp", [(i, i ^ (2 << ((i & 1) ^ turn))) for i in range(n)])


def interior():
    z = lax.axis_index("tensor")
    return (z > 0) & (z < lax.axis_size("tensor") - 1)


def outward(x):
    return lax.ppermute(x, "tensor", [(i, i ^ 1) for i in range(lax.axis_size("tensor"))])


def inward(x):
    n, m = lax.axis_size("tensor"), lax.axis_size("dp")
    pairs = []
    for d in range(m):
        for i in range(n):
            to = (d, i ^ 3) if 0 < i < n - 1 else (d ^ 1, i)
            pairs.append((d * n + i, to[0] * n + to[1]))
    return lax.ppermute(x, ("dp", "tensor"), pairs)


def after(x, *earlier):
    return lax.optimization_barrier((x, *earlier))[0]


def plus(a, b):
    return (a.astype(F32) + b.astype(F32)).astype(BF16)


def body(x_long, dv_long, x_short, dv_short, long_len, short_len, master, moment1, moment2):
    n = lax.axis_size("dp")
    parts = lax.axis_size("tensor")
    outer, inner, width = master.shape
    rows = x_long.shape[0]
    short_rows, _, inner_whole = x_short.shape
    chips = n // 2
    own_rows = rows // parts
    aligned = (
        n & (n - 1) == 0
        and chips == 4
        and parts == 4
        and short_rows % 512 == 0
        and inner % 16 == 0
        and own_rows % 16 == 0
        and rows % 128 == 0
        and short_rows % 128 == 0
        and inner_whole % 128 == 0
        and width % 128 == 0
    )
    if not aligned:
        return plain_body(
            x_long, dv_long, x_short, dv_short, long_len, short_len, master, moment1, moment2
        )
    x_t = jnp.transpose(x_long, (1, 2, 0))
    dv_other = swap(dv_long, 1)
    block = jax.ShapeDtypeStruct((outer, inner, width), BF16)
    *blocks, theirs, live_dv, end_mask, row_mask = pl.pallas_call(
        first_kernel,
        out_shape=[
            *[block] * 4,
            jax.ShapeDtypeStruct((chips, outer, inner, rows), BF16),
            jax.ShapeDtypeStruct(dv_long.shape, BF16),
            jax.ShapeDtypeStruct((1, 1, width), F32),
            jax.ShapeDtypeStruct((own_rows, width), F32),
        ],
        in_specs=[HBM] * 6,
        out_specs=[VMEM] * 8,
        scratch_shapes=[
            pltpu.SMEM((1,), jnp.int32),
            pltpu.SMEM((1,), jnp.int32),
            pltpu.VMEM(x_short.shape, BF16),
            pltpu.VMEM(dv_short.shape, BF16),
            pltpu.VMEM((chips, outer, inner, rows), BF16),
            pltpu.VMEM(dv_long.shape, BF16),
            pltpu.VMEM((short_rows // 4 * outer, inner_whole), F32),
            pltpu.VMEM((4, outer * inner, short_rows), BF16),
            pltpu.SemaphoreType.DMA((11 + chips,)),
        ],
        compiler_params=params(51),
        cost_estimate=cost(2 * short_rows * outer * inner_whole * width, 8 * MIB),
        name="first",
    )(short_len, long_len, x_short, dv_short, x_t, dv_long)
    within = end_mask > 0.0
    x_other = swap(theirs, 1)
    from_end = outward(blocks[3])
    long_own, long_first, long_second, long_far, weight = pl.pallas_call(
        long_kernel,
        out_shape=[block] * 5,
        in_specs=[VMEM] * 4 + [HBM],
        out_specs=[VMEM] * 5,
        scratch_shapes=[pltpu.VMEM(master.shape, F32), pltpu.SemaphoreType.DMA],
        compiler_params=params(50),
        cost_estimate=cost(4 * rows * chips * outer * inner * width, 4 * MIB),
        name="long_grad",
    )(x_t, live_dv, x_other, dv_other, master)
    second_weight, first_weight = cross(weight, 1), cross(weight, 0)

    far_sum = cross(long_far, 1)
    second_sum = cross(long_second, 1)
    middle = outward(after(blocks[2], long_own))
    across_sent = plus(after(blocks[2], long_own), from_end)
    across = inward(across_sent)
    first_sent = plus(long_first, far_sum)
    first_sum = cross(first_sent, 0)
    handed = after(second_weight, first_weight, first_sent)
    far_weight = cross(handed, 0)
    inside_sent = plus(after(blocks[3], handed), middle)
    inside = inward(inside_sent)
    across = after(across, inside_sent)
    near_sent = plus(blocks[1], jnp.where(within, across, jnp.zeros_like(across)))
    near = outward(near_sent)

    mine, other = pl.pallas_call(
        values_kernel,
        out_shape=[jax.ShapeDtypeStruct((parts, own_rows, width), t) for t in (F32, BF16)],
        in_specs=[VMEM] * 6,
        out_specs=[VMEM] * 2,
        scratch_shapes=[pltpu.VMEM((rows, width), F32)],
        compiler_params=params(16),
        cost_estimate=cost(4 * rows * chips * outer * inner * width, 6 * MIB),
        name="values",
    )(x_t, x_other, weight, first_weight, second_weight, far_weight)

    arrived = [after(blocks[0], mine), near, inside, long_own, second_sum, first_sum]
    arrived += [master, moment1, moment2]
    next_shard = pl.pallas_call(
        weight_kernel,
        out_shape=block,
        in_specs=[VMEM] * len(arrived),
        out_specs=VMEM,
        compiler_params=params(16),
        cost_estimate=cost(20 * outer * inner * width, 5 * MIB),
        name="next_weight",
    )(*arrived)

    gathered = [next_shard, cross(next_shard, 0), cross(next_shard, 1)]

    total = mine + after(swap(other, 1), next_shard).astype(F32)
    shares = total.astype(BF16)
    v_across_sent = plus(shares[2], outward(shares[3]))
    v_across = inward(v_across_sent)
    v_middle = outward(after(shares[2], v_across_sent))
    v_near = plus(shares[1], jnp.where(within[0], v_across, jnp.zeros_like(v_across)))
    v_inside = plus(shares[3], v_middle)
    values = total[0] + outward(v_near).astype(F32)
    values = values + jnp.where(within[0], inward(v_inside).astype(F32), 0.0)
    v_long = jnp.where(row_mask > 0.0, values, 0.0).astype(BF16)

    new_state = pl.pallas_call(
        state_kernel,
        out_shape=[jax.ShapeDtypeStruct(master.shape, F32)] * 3,
        in_specs=[VMEM] * len(arrived),
        out_specs=[VMEM] * 3,
        compiler_params=params(16),
        cost_estimate=cost(20 * outer * inner * width, 10 * MIB),
        name="new_state",
    )(after(arrived[0], shares), *arrived[1:])

    far = cross(gathered[1], 1)
    early = list(gathered)
    early = early + [swap(x, 1) for x in early]
    kinds = [(i, 0, i % 3, i // 3) for i in range(6)]
    whole_shape = jax.ShapeDtypeStruct((n * outer, inner, width), BF16)
    placed = place(kinds, early, outer, whole_shape, "place_near")
    far = after(far, v_long, new_state[0], early[3])
    next_weight = place([(0, 0, 3, 0), (1, 0, 3, 1)], [far, swap(far, 1)], outer, placed, "place_far")
    return (v_long, *new_state, next_weight)


def solution(mesh):
    placed = (
        P("dp", None, "tensor"),
        P("dp", None),
        P("tensor", "dp", None),
        P("tensor", None),
        P("dp"),
        P("tensor"),
        P("dp", "tensor", None),
        P("dp", "tensor", None),
        P("dp", "tensor", None),
    )
    return jax.shard_map(
        body,
        mesh=mesh,
        in_specs=placed,
        out_specs=(
            P(("dp", "tensor"), None),
            P("dp", "tensor", None),
            P("dp", "tensor", None),
            P("dp", "tensor", None),
            P(None, "tensor", None),
        ),
        check_vma=False,
    )
```

```python
import functools

import jax
import jax.numpy as jnp
from jax import lax
from jax.experimental import pallas as pl
from jax.experimental.pallas import tpu as pltpu
from jax.sharding import PartitionSpec as P

BF16 = jnp.bfloat16
F32 = jnp.float32
MIB = 1 << 20
VMEM = pl.BlockSpec(memory_space=pltpu.VMEM)
SMEM = pl.BlockSpec(memory_space=pltpu.SMEM)
ANY = pl.BlockSpec(memory_space=pl.ANY)
HBM = pl.BlockSpec(memory_space=pltpu.HBM)


def contract_rows(left, right):
    return lax.dot_general(
        left, right, (((0,), (0,)), ((), ())), preferred_element_type=jnp.float32
    )


def adam(master, moment1, moment2, grad):
    new_moment1 = 0.9 * moment1 + 0.1 * grad
    new_moment2 = 0.999 * moment2 + 0.001 * grad * grad
    first_corr = 1.0 - 0.9**10
    second_corr = 1.0 - 0.999**10
    update = new_moment1 / first_corr / (jnp.sqrt(new_moment2 / second_corr) + 1e-08)
    new_master = master - 0.01 * (update + 0.1 * master)
    return new_master, new_moment1, new_moment2


def plain_body(x_long, dv_long, x_short, dv_short, long_len, short_len, master, moment1, moment2):
    weight_shard = master.astype(BF16)
    long_rows, _, inner_part = x_long.shape
    kv_width = master.shape[2]
    short_rows, outer_part, inner_whole = x_short.shape
    piece = lax.all_gather(weight_shard, "dp", axis=0, tiled=True)
    flat_inputs = x_long.reshape(long_rows, piece.shape[0] * inner_part)
    flat_piece = piece.reshape(piece.shape[0] * inner_part, kv_width)
    partial_values = jnp.dot(flat_inputs, flat_piece, preferred_element_type=F32)
    values = lax.psum_scatter(partial_values, "tensor", scatter_dimension=0, tiled=True)
    own_rows = values.shape[0]
    row_start = lax.axis_index("tensor") * own_rows
    own_live = row_start + jnp.arange(own_rows, dtype=jnp.int32) < long_len[0]
    v_long = jnp.where(own_live[:, None], values, 0.0).astype(BF16)
    long_live = jnp.arange(long_rows, dtype=jnp.int32) < long_len[0]
    short_live = jnp.arange(short_rows, dtype=jnp.int32) < short_len[0]
    live_dv_long = jnp.where(long_live[:, None], dv_long, jnp.zeros_like(dv_long))
    live_dv_short = jnp.where(short_live[:, None], dv_short, jnp.zeros_like(dv_short))
    count = lax.axis_size("dp") * master.shape[0]
    grad_long = lax.psum_scatter(
        contract_rows(flat_inputs, live_dv_long).reshape(count, inner_part, kv_width),
        "dp",
        scatter_dimension=0,
        tiled=True,
    )
    flat_inputs = x_short.reshape(short_rows, outer_part * inner_whole)
    product = contract_rows(flat_inputs, live_dv_short).reshape(outer_part, inner_whole, kv_width)
    grad_short = lax.psum_scatter(product, "tensor", scatter_dimension=1, tiled=True)
    new_master, new_moment1, new_moment2 = adam(master, moment1, moment2, grad_long + grad_short)
    next_weight = lax.all_gather(new_master.astype(BF16), "dp", axis=0, tiled=True)
    return (v_long, new_master, new_moment1, new_moment2, next_weight)


def first_kernel(slen_hbm, llen_hbm, xs_hbm, dvs_hbm, xl_hbm, dvl_hbm, master_hbm, *refs):
    blocks, theirs, live_dv, weight, inside, live_rows = refs[:4], *refs[4:9]
    slen_ref, llen_ref, xs_ref, dvs_ref, xl_ref, dvl_ref, master_ref, wide, turned, sems = refs[9:]
    rows, outer, inner = xs_ref.shape
    chips, owned, _, long_rows = theirs.shape
    chunks = 4
    chunk = rows // chunks
    part = inner // 4
    z = lax.axis_index("tensor")
    other = 1 - lax.rem(lax.axis_index("dp"), 2)
    pairs = []
    for c in range(chunks):
        span = pl.ds(c * chunk, chunk)
        pairs.append((xs_hbm.at[span], xs_ref.at[span]))
        pairs.append((dvs_hbm.at[span], dvs_ref.at[span]))
    for c in range(chips):
        pairs.append((xl_hbm.at[pl.ds((2 * c + other) * owned, owned)], xl_ref.at[c]))
    pairs.append((dvl_hbm, dvl_ref))
    pairs.append((master_hbm, master_ref))
    pairs.append((llen_hbm, llen_ref))
    pairs.append((slen_hbm, slen_ref))
    copies = [pltpu.make_async_copy(*pair, sems.at[i]) for i, pair in enumerate(pairs)]
    for copy in copies[-2:] + copies[:-2]:
        copy.start()
    copies[-1].wait()
    for c in range(chunks):
        copies[2 * c].wait()
        copies[2 * c + 1].wait()
        span = slice(c * chunk, (c + 1) * chunk)
        wide[...] = xs_ref[span].reshape(chunk * outer, inner).astype(F32)
        for a in range(outer):
            xa = wide[pl.ds(a, chunk, outer), :].astype(BF16).T
            for j in range(4):
                turned[j, a * part : (a + 1) * part, span] = xa[j * part : (j + 1) * part]
        dv = dvs_ref[span]
        row = lax.broadcasted_iota(jnp.int32, dv.shape, 0) + c * chunk
        dvs_ref[span] = jnp.where(row < slen_ref[0], dv, jnp.zeros_like(dv))
    for k in (3, 2, 1, 0):
        x = turned[lax.bitwise_xor(z, jnp.int32(k))]
        prod = jnp.dot(x, dvs_ref[...], preferred_element_type=F32)
        blocks[k][...] = prod.reshape(outer, part, prod.shape[1]).astype(BF16)
    copies[-2].wait()
    long_len = llen_ref[0]
    for c in range(chips):
        copies[2 * chunks + c].wait()
        x = xl_ref[c]
        row = lax.broadcasted_iota(jnp.int32, x.shape, 2)
        theirs[c] = jnp.where(row < long_len, x, jnp.zeros_like(x))
    copies[-4].wait()
    dv = dvl_ref[...]
    row = lax.broadcasted_iota(jnp.int32, dv.shape, 0)
    live_dv[...] = jnp.where(row < long_len, dv, jnp.zeros_like(dv))
    copies[-3].wait()
    weight[...] = master_ref[...].astype(BF16)
    within = jnp.where(interior(), 1.0, 0.0)
    inside[...] = jnp.full(inside.shape, within, F32)
    row = lax.broadcasted_iota(jnp.int32, live_rows.shape, 0) + z * live_rows.shape[0]
    live_rows[...] = jnp.where(row < long_len, 1.0, 0.0)


def plane_steps():
    core = lax.rem(lax.axis_index("dp"), 2)
    return 0, 1 + core, 2 - core, 3


def long_kernel(x_ref, dv_ref, xs_ref, dvs_ref, *outs):
    chips, outer, inner, rows = xs_ref.shape
    me = lax.axis_index("dp")
    chip, core = me // 2, lax.rem(me, 2)
    for out, rel in reversed(list(zip(outs, plane_steps()))):
        j = lax.bitwise_xor(chip, jnp.int32(rel))
        mine = x_ref[pl.ds((2 * j + core) * outer, outer)].reshape(outer * inner, rows)
        other = xs_ref[j].reshape(outer * inner, rows)
        prod = jnp.dot(mine, dv_ref[...], preferred_element_type=F32)
        prod = prod + jnp.dot(other, dvs_ref[...], preferred_element_type=F32)
        out[...] = prod.reshape(outer, inner, prod.shape[-1]).astype(BF16)


def values_kernel(x_ref, xs_ref, *refs):
    weights, mine_ref, other_ref, acc = refs[:4], refs[-3], refs[-2], refs[-1]
    _, outer, inner, rows = xs_ref.shape
    parts, part, width = mine_ref.shape
    me = lax.axis_index("dp")
    z = lax.axis_index("tensor")
    chip, core = me // 2, lax.rem(me, 2)
    for which, out in ((0, mine_ref), (1, other_ref)):
        total = None
        for weight, rel in zip(weights, plane_steps()):
            j = lax.bitwise_xor(chip, jnp.int32(rel))
            x = xs_ref[j] if which else x_ref[pl.ds((2 * j + core) * outer, outer)]
            w = weight[...].reshape(outer * inner, width)
            term = contract_rows(x.reshape(outer * inner, rows), w)
            total = term if total is None else total + term
        acc[...] = total
        for k in range(parts):
            j = lax.bitwise_xor(z, jnp.int32(k))
            out[k] = acc[pl.ds(pl.multiple_of(j * part, part), part), :].astype(out.dtype)


def partial_kernel(own, inside, *refs):
    *terms, out = refs
    grad = own[...].astype(F32) + jnp.where(interior(), inside[...].astype(F32), 0.0)
    for t in terms:
        grad = grad + t[...].astype(F32)
    out[...] = grad


def update(refs):
    partial, near, master, moment1, moment2 = refs
    grad = partial[...] + near[...].astype(F32)
    return adam(master[...], moment1[...], moment2[...], grad)


def weight_kernel(*refs):
    refs[-1][...] = update(refs[:-1])[0].astype(BF16)


def state_kernel(*refs):
    for out, value in zip(refs[-3:], update(refs[:-3])):
        out[...] = value


def place_kernel(kinds, n, outer, *refs):
    pieces, out, sems = refs[:n], refs[-2], refs[-1]
    me = lax.axis_index("dp")
    steps = plane_steps()
    copies = []
    for s, (i, start, step, core) in enumerate(kinds):
        if core and step in (1, 2):
            step = 3 - step
        owner = lax.bitwise_xor(me, 2 * jnp.int32(steps[step]) + core)
        source = pieces[i].at[pl.ds(start, outer)]
        target = out.at[pl.ds(owner * outer, outer)]
        copies.append(pltpu.make_async_copy(source, target, sems.at[s]))
    for copy in copies:
        copy.start()
    for copy in copies:
        copy.wait()


def place(kinds, pieces, outer, whole, name):
    new = isinstance(whole, jax.ShapeDtypeStruct)
    return pl.pallas_call(
        functools.partial(place_kernel, kinds, len(pieces), outer),
        out_shape=jax.ShapeDtypeStruct(whole.shape, whole.dtype),
        in_specs=[VMEM] * len(pieces) + [ANY] * (not new),
        out_specs=ANY,
        scratch_shapes=[pltpu.SemaphoreType.DMA((len(kinds),))],
        input_output_aliases={} if new else {len(pieces): 0},
        compiler_params=params(16),
        cost_estimate=cost(0, 2 * sum(p.size for p in pieces)),
        name=name,
    )(*pieces, *([] if new else [whole]))


def params(mib):
    return pltpu.CompilerParams(vmem_limit_bytes=mib * MIB)


def cost(flops, moved):
    return pl.CostEstimate(flops=flops, bytes_accessed=moved, transcendentals=0)


def swap(x, bit):
    n = lax.axis_size("dp")
    return lax.ppermute(x, "dp", [(i, i ^ bit) for i in range(n)])


def cross(x, turn):
    n = lax.axis_size("dp")
    return lax.ppermute(x, "dp", [(i, i ^ (2 << ((i & 1) ^ turn))) for i in range(n)])


def interior():
    z = lax.axis_index("tensor")
    return (z > 0) & (z < lax.axis_size("tensor") - 1)


def outward(x):
    return lax.ppermute(x, "tensor", [(i, i ^ 1) for i in range(lax.axis_size("tensor"))])


def inward(x):
    n, m = lax.axis_size("tensor"), lax.axis_size("dp")
    pairs = []
    for d in range(m):
        for i in range(n):
            to = (d, i ^ 3) if 0 < i < n - 1 else (d ^ 1, i)
            pairs.append((d * n + i, to[0] * n + to[1]))
    return lax.ppermute(x, ("dp", "tensor"), pairs)


def after(x, *earlier):
    return lax.optimization_barrier((x, *earlier))[0]


def plus(a, b):
    return (a.astype(F32) + b.astype(F32)).astype(BF16)


def body(x_long, dv_long, x_short, dv_short, long_len, short_len, master, moment1, moment2):
    n = lax.axis_size("dp")
    parts = lax.axis_size("tensor")
    outer, inner, width = master.shape
    rows = x_long.shape[0]
    short_rows, _, inner_whole = x_short.shape
    chips = n // 2
    own_rows = rows // parts
    aligned = (
        n & (n - 1) == 0
        and chips == 4
        and parts == 4
        and short_rows % 512 == 0
        and inner % 16 == 0
        and own_rows % 16 == 0
        and rows % 128 == 0
        and short_rows % 128 == 0
        and inner_whole % 128 == 0
        and width % 128 == 0
    )
    if not aligned:
        return plain_body(
            x_long, dv_long, x_short, dv_short, long_len, short_len, master, moment1, moment2
        )
    x_t = jnp.transpose(x_long, (1, 2, 0))
    dv_other = swap(dv_long, 1)
    block = jax.ShapeDtypeStruct((outer, inner, width), BF16)
    *blocks, theirs, live_dv, weight, end_mask, row_mask = pl.pallas_call(
        first_kernel,
        out_shape=[
            *[block] * 4,
            jax.ShapeDtypeStruct((chips, outer, inner, rows), BF16),
            jax.ShapeDtypeStruct(dv_long.shape, BF16),
            block,
            jax.ShapeDtypeStruct((1, 1, width), F32),
            jax.ShapeDtypeStruct((own_rows, width), F32),
        ],
        in_specs=[HBM] * 7,
        out_specs=[VMEM] * 9,
        scratch_shapes=[
            pltpu.SMEM((1,), jnp.int32),
            pltpu.SMEM((1,), jnp.int32),
            pltpu.VMEM(x_short.shape, BF16),
            pltpu.VMEM(dv_short.shape, BF16),
            pltpu.VMEM((chips, outer, inner, rows), BF16),
            pltpu.VMEM(dv_long.shape, BF16),
            pltpu.VMEM(master.shape, F32),
            pltpu.VMEM((short_rows // 4 * outer, inner_whole), F32),
            pltpu.VMEM((4, outer * inner, short_rows), BF16),
            pltpu.SemaphoreType.DMA((12 + chips,)),
        ],
        compiler_params=params(50),
        cost_estimate=cost(2 * short_rows * outer * inner_whole * width, 8 * MIB),
        name="first",
    )(short_len, long_len, x_short, dv_short, x_t, dv_long, master)
    within = end_mask > 0.0
    x_other = swap(theirs, 1)
    from_end = outward(blocks[3])
    second_weight, first_weight = cross(weight, 1), cross(weight, 0)
    long_own, long_first, long_second, long_far = pl.pallas_call(
        long_kernel,
        out_shape=[block] * 4,
        in_specs=[VMEM] * 4,
        out_specs=[VMEM] * 4,
        compiler_params=params(16),
        cost_estimate=cost(4 * rows * chips * outer * inner * width, 4 * MIB),
        name="long_grad",
    )(x_t, live_dv, x_other, dv_other)

    far_sum = cross(long_far, 1)
    second_sum = cross(long_second, 1)
    middle = outward(after(blocks[2], long_own))
    across_sent = plus(after(blocks[2], long_own), from_end)
    across = inward(across_sent)
    first_sent = plus(long_first, far_sum)
    first_sum = cross(first_sent, 0)
    handed = after(second_weight, first_weight, first_sent)
    far_weight = cross(handed, 0)
    inside_sent = plus(after(blocks[3], handed), middle)
    inside = inward(inside_sent)
    across = after(across, inside_sent)
    near_sent = plus(blocks[1], jnp.where(within, across, jnp.zeros_like(across)))
    near = outward(near_sent)

    mine, other = pl.pallas_call(
        values_kernel,
        out_shape=[jax.ShapeDtypeStruct((parts, own_rows, width), t) for t in (F32, BF16)],
        in_specs=[VMEM] * 6,
        out_specs=[VMEM] * 2,
        scratch_shapes=[pltpu.VMEM((rows, width), F32)],
        compiler_params=params(16),
        cost_estimate=cost(4 * rows * chips * outer * inner * width, 6 * MIB),
        name="values",
    )(x_t, x_other, weight, first_weight, second_weight, far_weight)

    partial = pl.pallas_call(
        partial_kernel,
        out_shape=jax.ShapeDtypeStruct(master.shape, F32),
        in_specs=[VMEM] * 5,
        out_specs=VMEM,
        compiler_params=params(16),
        cost_estimate=cost(5 * outer * inner * width, 4 * MIB),
        name="partial",
    )(after(blocks[0], mine), inside, long_own, second_sum, first_sum)
    arrived = [partial, near, master, moment1, moment2]
    next_shard = pl.pallas_call(
        weight_kernel,
        out_shape=block,
        in_specs=[VMEM] * len(arrived),
        out_specs=VMEM,
        compiler_params=params(16),
        cost_estimate=cost(20 * outer * inner * width, 5 * MIB),
        name="next_weight",
    )(*arrived)

    gathered = [next_shard, cross(next_shard, 0), cross(next_shard, 1)]

    total = mine + after(swap(other, 1), next_shard).astype(F32)
    shares = total.astype(BF16)
    v_across_sent = plus(shares[2], outward(shares[3]))
    v_across = inward(v_across_sent)
    v_middle = outward(after(shares[2], v_across_sent))
    v_near = plus(shares[1], jnp.where(within[0], v_across, jnp.zeros_like(v_across)))
    v_inside = plus(shares[3], v_middle)
    values = total[0] + outward(v_near).astype(F32)
    values = values + jnp.where(within[0], inward(v_inside).astype(F32), 0.0)
    v_long = jnp.where(row_mask > 0.0, values, 0.0).astype(BF16)

    new_state = pl.pallas_call(
        state_kernel,
        out_shape=[jax.ShapeDtypeStruct(master.shape, F32)] * 3,
        in_specs=[VMEM] * len(arrived),
        out_specs=[VMEM] * 3,
        compiler_params=params(16),
        cost_estimate=cost(20 * outer * inner * width, 10 * MIB),
        name="new_state",
    )(after(arrived[0], shares), *arrived[1:])

    far = cross(gathered[1], 1)
    early = list(gathered)
    early = early + [swap(x, 1) for x in early]
    kinds = [(i, 0, i % 3, i // 3) for i in range(6)]
    whole_shape = jax.ShapeDtypeStruct((n * outer, inner, width), BF16)
    placed = place(kinds, early, outer, whole_shape, "place_near")
    far = after(far, v_long, new_state[0], early[3])
    next_weight = place([(0, 0, 3, 0), (1, 0, 3, 1)], [far, swap(far, 1)], outer, placed, "place_far")
    return (v_long, *new_state, next_weight)


def solution(mesh):
    placed = (
        P("dp", None, "tensor"),
        P("dp", None),
        P("tensor", "dp", None),
        P("tensor", None),
        P("dp"),
        P("tensor"),
        P("dp", "tensor", None),
        P("dp", "tensor", None),
        P("dp", "tensor", None),
    )
    return jax.shard_map(
        body,
        mesh=mesh,
        in_specs=placed,
        out_specs=(
            P(("dp", "tensor"), None),
            P("dp", "tensor", None),
            P("dp", "tensor", None),
            P("dp", "tensor", None),
            P(None, "tensor", None),
        ),
        check_vma=False,
    )
```
